32 devices in a mesh: dp: 8 (over z, x), rows: 4 (over y, core).
Axes of the slice: x: 2, y: 2, z: 4, core: 2. Of those that a mesh axis runs over, the one named last changes fastest.
Arguments:
- images: bfloat16 [32, 8, 8, 1024], P(('dp', 'rows')), may hold values from -6 to 6
- styles: bfloat16 [32, 512], P('dp'), may hold values from -6 to 6
- labels: int32 [32], P('dp'), may hold values from 0 to 999
- noise_map: bfloat16 [32, 16, 16], P(('dp', 'rows')), may hold values from -6 to 6
- counts: int32 [32], P('dp'), may hold values from 0 to 1, as said below
- cot_features: bfloat16 [32, 16, 16, 1024], P(('dp', 'rows')), may hold values from -6 to 6
- cot_image: float32 [32, 3, 16, 16], P(('dp', 'rows')), may hold values from -6 to 6
- kernel_bank: bfloat16 [3, 3, 1024, 8, 1024], P(None, None, None, None, 'rows'), may hold values from -0.0625 to 0.0625
- select_proj: bfloat16 [512, 8], replicated, may hold values from -0.25 to 0.25
- style_proj: bfloat16 [512, 1024], replicated, may hold values from -0.125 to 0.125
- conv_bias: bfloat16 [1024], replicated, may hold values from -3 to 3
- noise_gain: bfloat16 [1024], replicated, may hold values from 0.19921875 to 0.796875
- norm_attn: bfloat16 [1024], replicated, may hold values from 0.099609375 to 1.8984375
- query_proj: bfloat16 [1024, 1024], P(None, 'rows'), may hold values from -0.1875 to 0.1875
- key_proj: bfloat16 [1024, 1024], P(None, 'rows'), may hold values from -0.1875 to 0.1875
- value_proj: bfloat16 [1024, 1024], P(None, 'rows'), may hold values from -0.1875 to 0.1875
- out_proj: bfloat16 [1024, 1024], P('rows'), may hold values from -0.75 to 0.75
- norm_cross: bfloat16 [1024], replicated, may hold values from 0.099609375 to 1.8984375
- cross_query: bfloat16 [1024, 1024], P(None, 'rows'), may hold values from -0.1875 to 0.1875
- cross_key: bfloat16 [1024, 1024], P(None, 'rows'), may hold values from -0.125 to 0.125
- cross_value: bfloat16 [1024, 1024], P(None, 'rows'), may hold values from -0.125 to 0.125
- cross_out: bfloat16 [1024, 1024], P('rows'), may hold values from -0.375 to 0.375
- class_table: bfloat16 [1000, 1024], replicated, may hold values from -6 to 6
- class_pos: bfloat16 [16, 1024], replicated, may hold values from -6 to 6
- norm_mlp: bfloat16 [1024], replicated, may hold values from 0.099609375 to 1.8984375
- up_proj: bfloat16 [1024, 4096], P(None, 'rows'), may hold values from -0.1875 to 0.1875
- down_proj: bfloat16 [4096, 1024], P('rows'), may hold values from -0.125 to 0.125
- rgb_style: bfloat16 [512, 1024], replicated, may hold values from -0.125 to 0.125
- color_projection: bfloat16 [1024, 3], replicated, may hold values from -0.1875 to 0.1875
- color_bias: bfloat16 [3], replicated, may hold values from -2 to 2
Outputs:
- features: float32 [32, 16, 16, 1024], P(('dp', 'rows'))
- color_image: float32 [32, 3, 16, 16], P(('dp', 'rows'))
- images_grad: float32 [32, 8, 8, 1024], P(('dp', 'rows'))
- styles_grad: float32 [32, 512], P('dp')
- kernel_bank_grad: float32 [3, 3, 1024, 8, 1024], P(None, None, 'dp', None, 'rows')
- select_proj_grad: float32 [512, 8], replicated
- style_proj_grad: float32 [512, 1024], replicated
- conv_bias_grad: float32 [1024], replicated
- noise_gain_grad: float32 [1024], replicated
- norm_attn_grad: float32 [1024], replicated
- query_proj_grad: float32 [1024, 1024], P('dp', 'rows')
- key_proj_grad: float32 [1024, 1024], P('dp', 'rows')
- value_proj_grad: float32 [1024, 1024], P('dp', 'rows')
- out_proj_grad: float32 [1024, 1024], P('rows', 'dp')
- norm_cross_grad: float32 [1024], replicated
- cross_query_grad: float32 [1024, 1024], P('dp', 'rows')
- cross_key_grad: float32 [1024, 1024], P('dp', 'rows')
- cross_value_grad: float32 [1024, 1024], P('dp', 'rows')
- cross_out_grad: float32 [1024, 1024], P('rows', 'dp')
- class_table_grad: float32 [1000, 1024], replicated
- class_pos_grad: float32 [16, 1024], replicated
- norm_mlp_grad: float32 [1024], replicated
- up_proj_grad: float32 [1024, 4096], P('dp', 'rows')
- down_proj_grad: float32 [4096, 1024], P('rows', 'dp')
- rgb_style_grad: float32 [512, 1024], replicated
- rgb_proj_grad: float32 [1024, 3], replicated
- rgb_bias_grad: float32 [3], replicated
The draws below stay inside these ranges and needn't reach their ends.
Inputs may be any that keep to these rules, and one draw needn't show every extreme that they name: Entry d belongs to device d of the dp and rows axes taken together (dp slowest) and counts the live samples in that device's first slots of 1; some entry is 1.
All inputs are finite; a program needn't handle non-finite values.
Results may differ from the reference program's by a relative error of at most 0.035.
Values may be sent and summed in bfloat16 or wider, within the bound.
No kernel may reach another device: no remote copies, remote signals or barrier semaphores. Data moves between devices by JAX's collectives and lax.ppermute only.
A program may use at most 512 MiB of HBM per device.

```python
import math
import jax
import jax.numpy as jnp
from jax import lax

C = 1024
ZD = 512
K = 8
HD = 64
F = 4096
CLASSES = 1000
CT = 16
RES = 16
SLOTS = 1
LOWRES = 8
SAMPLES = 32
N_DP = 8
N_ROWS = 4


def draw_counts(key, part):
    key = jax.random.fold_in(key, 7)
    spread_key, full_key = jax.random.split(key)
    entries = N_DP * N_ROWS
    drawn = jax.random.randint(spread_key, (entries,), 0, SLOTS + 1)
    full_index = jax.random.randint(full_key, (), 0, entries)
    return jnp.where(jnp.arange(entries) == full_index, SLOTS, drawn).astype(jnp.int32)


def with_ends(values, rng, smallest, high):
    place = [jax.random.randint(jax.random.fold_in(rng, axis), (), 0, length) for axis, length in enumerate(values.shape)]
    longest = values.shape.index(max(values.shape))
    beside = place[:longest] + [(place[longest] + 1) % values.shape[longest]] + place[longest + 1:]
    return values.at[tuple(place)].set(smallest).at[tuple(beside)].set(high)


def spiked(result, own_key, source, target, blocks, factor):
    def block_of(position):
        return (jnp.arange(result.shape[position]) // (result.shape[position] // blocks)).reshape((-1,) + (1,) * (result.ndim - 1 - position))

    near = jax.random.permutation(own_key, blocks)[block_of(target)]
    far = (block_of(target) + blocks // 2) % blocks
    return jnp.where((block_of(source) == near) | (block_of(source) == far), factor * result, result)


def block_scale(key, dims, shards, low, largest):
    def one(position, shards_of):
        draws = jax.random.uniform(jax.random.fold_in(jax.random.fold_in(key, 6), position), (shards_of,), jnp.float32, low / len(shards), largest / len(shards))
        return jnp.repeat(jnp.exp(draws), dims[position] // shards_of).reshape((-1,) + (1,) * (len(dims) - position - 1))

    gain = one(*shards[0])
    for cut in shards[1:]:
        gain = gain * one(*cut)
    return gain


def noise(stream_key, extent, spread, limit, cuts=(), kind=jnp.bfloat16):
    level = block_scale(stream_key, extent, cuts, -0.22, 0.18) if cuts else 1.0
    values = jax.random.normal(stream_key, extent, jnp.float32) * spread * level
    return jnp.minimum(jnp.maximum(values, -limit), limit).astype(kind)


def bell_draw_with(key, extent, deviation, reach, cuts, heavy, held_as=jnp.bfloat16):
    values = deviation * jax.random.normal(key, extent, jnp.float32)
    if cuts:
        values = values * block_scale(key, extent, cuts, -0.22, 0.18)
    return jnp.clip(spiked(values, jax.random.fold_in(key, 3), *heavy), -reach, reach).astype(held_as)


def setup_inputs(seed: int = 0) -> dict:
    streams_of = jax.random.split(jax.random.key(seed), 31)
    return {
        "images": noise(streams_of[0], (SAMPLES, LOWRES, LOWRES, C), 1.0, 6.0, ((0, 32),)),
        "styles": noise(streams_of[1], (SAMPLES, ZD), 1.0, 6.0, ((0, 8),)),
        "labels": with_ends(jax.random.randint(streams_of[2], (SAMPLES,), 0, CLASSES), jax.random.fold_in(streams_of[2], 1), 0, CLASSES - 1).astype(jnp.int32),
        "noise_map": noise(streams_of[3], (SAMPLES, RES, RES), 1.0, 6.0, ((0, 32),)),
        "counts": draw_counts(jax.random.fold_in(streams_of[30], 71), 0),
        "cot_features": bell_draw_with(streams_of[5], (SAMPLES, RES, RES, C), 1.0, 6.0, ((0, 32),), (0, 3, 32, 2.75)),
        "cot_image": noise(streams_of[6], (SAMPLES, 3, RES, RES), 1.0, 6.0, ((0, 32),), jnp.float32),
        "kernel_bank": noise(streams_of[7], (3, 3, C, K, C), (9 * C) ** -0.5, 0.0625, ((4, 4),)),
        "select_proj": noise(streams_of[8], (ZD, K), ZD ** -0.5, 0.25),
        "style_proj": noise(streams_of[9], (ZD, C), (4 * ZD) ** -0.5, 0.125),
        "conv_bias": noise(streams_of[10], (C,), 0.5, 3.0),
        "noise_gain": jnp.clip(jax.random.uniform(streams_of[11], (C,), jnp.float32, 0.19921875, 0.796875), 0.19921875, 0.796875).astype(jnp.bfloat16),
        "norm_attn": jnp.clip(1.0 + 0.18 * jax.random.normal(streams_of[12], (C,), jnp.float32), 0.099609375, 1.8984375).astype(jnp.bfloat16),
        "query_proj": noise(streams_of[13], (C, C), C ** -0.5, 0.1875, ((1, 4),)),
        "key_proj": noise(streams_of[14], (C, C), C ** -0.5, 0.1875, ((1, 4),)),
        "value_proj": noise(streams_of[15], (C, C), C ** -0.5, 0.1875, ((1, 4),)),
        "out_proj": noise(streams_of[16], (C, C), (C // 16) ** -0.5, 0.75, ((0, 4),)),
        "norm_cross": jnp.clip(1.0 + 0.18 * jax.random.normal(streams_of[17], (C,), jnp.float32), 0.099609375, 1.8984375).astype(jnp.bfloat16),
        "cross_query": noise(streams_of[18], (C, C), C ** -0.5, 0.1875, ((1, 4),)),
        "cross_key": noise(streams_of[19], (C, C), (2 * C) ** -0.5, 0.125, ((1, 4),)),
        "cross_value": noise(streams_of[20], (C, C), (2 * C) ** -0.5, 0.125, ((1, 4),)),
        "cross_out": noise(streams_of[21], (C, C), (C // 4) ** -0.5, 0.375, ((0, 4),)),
        "class_table": noise(streams_of[22], (CLASSES, C), 1.0, 6.0),
        "class_pos": noise(streams_of[23], (CT, C), 1.0, 6.0),
        "norm_mlp": jnp.clip(1.0 + 0.18 * jax.random.normal(streams_of[24], (C,), jnp.float32), 0.099609375, 1.8984375).astype(jnp.bfloat16),
        "up_proj": noise(streams_of[25], (C, F), C ** -0.5, 0.1875, ((1, 4),)),
        "down_proj": noise(streams_of[26], (F, C), (F // 2) ** -0.5, 0.125, ((0, 4),)),
        "rgb_style": noise(streams_of[27], (ZD, C), (4 * ZD) ** -0.5, 0.125),
        "color_projection": noise(streams_of[28], (C, 3), C ** -0.5, 0.1875),
        "color_bias": noise(streams_of[29], (3,), 0.3, 2.0),
    }


@jax.custom_vjp
def low(v):
    return lax.optimization_barrier(v.astype(jnp.bfloat16)).astype(jnp.float32)

@jax.custom_vjp
def low_back(v):
    return v

def low_keep(v):
    return (low(v), None)

def low_pass(kept, grad):
    return (grad,)

def back_keep(v):
    return (v, None)

def back_low(kept, grad):
    return (low(grad),)
low.defvjp(low_keep, low_pass)
low_back.defvjp(back_keep, back_low)
HIGH_ACCURACY = lax.Precision.HIGHEST

def product(former, latter):
    return jnp.dot(former, latter, precision=HIGH_ACCURACY)

def rms_norm(field, norm_gain):
    inverse = lax.rsqrt(lax.optimization_barrier(jnp.mean(field * field, axis=-1, keepdims=True)) + 1e-06)
    return field * inverse * norm_gain

def split_heads(field):
    return field.reshape(field.shape[0], field.shape[1], field.shape[2] // HD, HD)

def block_group(params, pieces):
    kernel_bank, select_proj, style_proj, conv_bias, noise_gain, norm_attn, query_proj, key_proj, value_proj, out_proj, norm_cross, cross_query, cross_key, cross_value, cross_out, class_table, class_pos, norm_mlp, up_proj, down_proj, rgb_style, color_projection, color_bias = params
    images, styles, noise_map, labels = pieces
    samples_here = images.shape[0]
    places = RES * RES
    widened = jnp.repeat(jnp.repeat(images, 2, axis=1), 2, axis=2)
    mixing = jax.nn.softmax(product(styles, select_proj), axis=-1)
    scale_in = product(styles, style_proj) + 1.0
    color_scale = product(styles, rgb_style) + 1.0
    bank_taps = kernel_bank.reshape(9, C, K, C)
    mixed = jnp.einsum('gk,tiko->gtio', mixing, bank_taps, precision=HIGH_ACCURACY)
    energy = jnp.einsum('gi,gtio->go', scale_in * scale_in, mixed * mixed, precision=HIGH_ACCURACY)
    demod_scale = lax.rsqrt(energy + 1e-08)
    mixed_low = low(mixed)
    modulated = low(widened * scale_in[:, None, None, :])
    padded = jnp.pad(modulated, ((0, 0), (1, 1), (1, 1), (0, 0)))
    conv_sum = jnp.zeros((samples_here, places, C), jnp.float32)
    for tap_index in range(9):
        view = padded[:, tap_index // 3:tap_index // 3 + RES, tap_index % 3:tap_index % 3 + RES, :].reshape(samples_here, places, C)
        conv_sum = conv_sum + jnp.einsum('gpi,gio->gpo', view, mixed_low[:, tap_index], precision=HIGH_ACCURACY)
    conv_sum = low_back(conv_sum)
    noise_flat = noise_map.reshape(samples_here, places, 1)
    residual_flow = jax.nn.silu(conv_sum * demod_scale[:, None, :] + noise_gain * noise_flat + conv_bias)
    normed = low(rms_norm(residual_flow, norm_attn))
    queries = split_heads(low(low_back(product(normed, query_proj))))
    key_heads = split_heads(low(low_back(product(normed, key_proj))))
    value_heads = split_heads(low(low_back(product(normed, value_proj))))
    raw_scores = low_back(jnp.einsum('gphd,gshd->ghps', queries, key_heads, precision=HIGH_ACCURACY))
    key_square = jnp.transpose(lax.optimization_barrier(jnp.sum(key_heads * key_heads, axis=-1)), (0, 2, 1))
    scores = (2.0 * raw_scores - key_square[:, :, None, :]) / math.sqrt(HD)
    weight = low(jax.nn.softmax(scores, axis=-1))
    attended = low(low_back(jnp.einsum('ghps,gshd->gphd', weight, value_heads, precision=HIGH_ACCURACY)))
    residual_flow = residual_flow + low_back(product(attended.reshape(samples_here, places, C), out_proj))
    context = low(class_table[labels][:, None, :] + class_pos[None, :, :])
    normed = low(rms_norm(residual_flow, norm_cross))
    cross_queries = split_heads(low(low_back(product(normed, cross_query))))
    cross_keys = split_heads(low(low_back(product(context, cross_key))))
    cross_values = split_heads(low(low_back(product(context, cross_value))))
    raw_scores = low_back(jnp.einsum('gphd,gjhd->ghpj', cross_queries, cross_keys, precision=HIGH_ACCURACY))
    weight = low(jax.nn.softmax(raw_scores / math.sqrt(HD), axis=-1))
    attended = low(low_back(jnp.einsum('ghpj,gjhd->gphd', weight, cross_values, precision=HIGH_ACCURACY)))
    residual_flow = residual_flow + low_back(product(attended.reshape(samples_here, places, C), cross_out))
    normed = low(rms_norm(residual_flow, norm_mlp))
    inner_act = low_back(product(normed, up_proj))
    residual_flow = residual_flow + low_back(product(low(jax.nn.silu(inner_act)), down_proj))
    color_image = jnp.einsum('jvk,jk,ko->jov', residual_flow, color_scale, color_projection, precision=HIGH_ACCURACY) + color_bias[None, :, None]
    return (residual_flow.reshape(samples_here, RES, RES, C), color_image.reshape(samples_here, 3, RES, RES))

def forward(params, images, styles, noise_map, labels):
    groups = SAMPLES // SLOTS

    def run_group(pieces):
        return block_group(params, pieces)
    features, color_image = lax.map(jax.checkpoint(run_group), (images.reshape(groups, SLOTS, LOWRES, LOWRES, C), styles.reshape(groups, SLOTS, ZD), noise_map.reshape(groups, SLOTS, RES, RES), labels.reshape(groups, SLOTS)))
    return (features.reshape(SAMPLES, RES, RES, C), color_image.reshape(SAMPLES, 3, RES, RES))

def reference(images, styles, labels, noise_map, counts, cot_features, cot_image, kernel_bank, select_proj, style_proj, conv_bias, noise_gain, norm_attn, query_proj, key_proj, value_proj, out_proj, norm_cross, cross_query, cross_key, cross_value, cross_out, class_table, class_pos, norm_mlp, up_proj, down_proj, rgb_style, color_projection, color_bias):
    params = tuple((weight.astype(jnp.float32) for weight in (kernel_bank, select_proj, style_proj, conv_bias, noise_gain, norm_attn, query_proj, key_proj, value_proj, out_proj, norm_cross, cross_query, cross_key, cross_value, cross_out, class_table, class_pos, norm_mlp, up_proj, down_proj, rgb_style, color_projection, color_bias)))
    sample_index = jnp.arange(SAMPLES, dtype=jnp.int32)
    live_mask = (sample_index % SLOTS < counts[sample_index // SLOTS]).astype(jnp.float32)
    sample_total = jnp.sum(counts.astype(jnp.float32))
    noise_float = noise_map.astype(jnp.float32)

    def wrapped(params, images, styles):
        return forward(params, images, styles, noise_float, labels)
    (features, color_image), pullback = jax.vjp(wrapped, params, images.astype(jnp.float32), styles.astype(jnp.float32))
    gradients, images_grad, styles_grad = pullback((cot_features.astype(jnp.float32) * live_mask[:, None, None, None], cot_image * live_mask[:, None, None, None]))
    gradients = tuple((entry / sample_total for entry in gradients))
    return (features, color_image, images_grad / sample_total, styles_grad / sample_total, gradients[0], gradients[1], gradients[2], gradients[3], gradients[4], gradients[5], gradients[6], gradients[7], gradients[8], gradients[9], gradients[10], gradients[11], gradients[12], gradients[13], gradients[14], gradients[15], gradients[16], gradients[17], gradients[18], gradients[19], gradients[20], gradients[21], gradients[22])
```

```python
import functools
import math

import jax
import jax.numpy as jnp
from jax import lax
from jax.experimental import pallas as pl
from jax.experimental.pallas import tpu as pltpu
from jax.sharding import PartitionSpec as P

HD = 64
SUB = 32
BF = jnp.bfloat16
F = jnp.float32
VMEM_LIMIT = 56 * 2**20
EPS = 1e-6


def dot_nn(a, b):
    return lax.dot_general(a, b, (((1,), (0,)), ((), ())), preferred_element_type=F)


def dot_nt(a, b):
    return lax.dot_general(a, b, (((1,), (1,)), ((), ())), preferred_element_type=F)


def dot_tn(a, b):
    return lax.dot_general(a, b, (((0,), (0,)), ((), ())), preferred_element_type=F)


def params():
    return pltpu.CompilerParams(vmem_limit_bytes=VMEM_LIMIT)


def swap(x, axis, delta):
    n = lax.axis_size(axis)
    return lax.ppermute(x, axis, [(i, i ^ delta) for i in range(n)])


def spread(x):
    n = lax.axis_size("rows")
    blocks = [None] * n
    blocks[0] = x
    for j in range(2, n, 2):
        blocks[j] = swap(x, "rows", j)
    for j in range(0, n, 2):
        blocks[j + 1] = swap(blocks[j], "rows", 1)
    return blocks


def collect(blocks):
    n = len(blocks)
    total = None
    for j in list(range(2, n, 2)) + [0]:
        near = blocks[j].astype(F) + swap(blocks[j + 1].astype(BF), "rows", 1).astype(F)
        part = near if j == 0 else swap(near.astype(BF), "rows", j).astype(F)
        total = part if total is None else total + part
    return total


def double(x, axis, place):
    delta = 1
    while delta < lax.axis_size(axis):
        other = swap(x, axis, delta)
        high = (place & delta) != 0
        x = jnp.where(high, jnp.concatenate([other, x]), jnp.concatenate([x, other]))
        delta *= 2
    return x


def merge(sums, gathered, axis, place):
    rows = sums.shape[0]
    delta = 1
    while delta < lax.axis_size(axis):
        other = swap(jnp.concatenate([sums, gathered]), axis, delta)
        sums = sums + other[:rows]
        high = (place & delta) != 0
        theirs = other[rows:]
        gathered = jnp.where(
            high, jnp.concatenate([theirs, gathered]), jnp.concatenate([gathered, theirs])
        )
        delta *= 2
    return sums, gathered


def add_over(sums, axis):
    delta = 1
    while delta < lax.axis_size(axis):
        sums = sums + swap(sums, axis, delta)
        delta *= 2
    return sums


def ring_perm(n, step, flip):
    lines = n // 2
    return [(i, ((i // 2 + step) % lines) * 2 + ((i % 2) ^ flip)) for i in range(n)]


def ring_gather(x):
    n = lax.axis_size("dp")
    out = []
    held = x
    for step in range(n // 2):
        if step:
            held = lax.ppermute(held, "dp", ring_perm(n, 1, 0))
        out.append(held)
        out.append(lax.ppermute(held, "dp", ring_perm(n, 0, 1)))
    return out


def ring_source(n, place, slot):
    lines = n // 2
    return ((place // 2 - slot // 2) % lines) * 2 + ((place % 2) ^ (slot % 2))


def ring_target(n, place, slot):
    lines = n // 2
    return ((place // 2 + slot // 2) % lines) * 2 + ((place % 2) ^ (slot % 2))


def move_up(v, axis):
    shape = list(v.shape)
    shape[axis] = 1
    kept = lax.slice_in_dim(v, 0, v.shape[axis] - 1, axis=axis)
    return jnp.concatenate([jnp.zeros(shape, v.dtype), kept], axis=axis)


def move_down(v, axis):
    shape = list(v.shape)
    shape[axis] = 1
    kept = lax.slice_in_dim(v, 1, v.shape[axis], axis=axis)
    return jnp.concatenate([kept, jnp.zeros(shape, v.dtype)], axis=axis)


def band_mask(kernels):
    width = SUB * kernels
    row = lax.broadcasted_iota(jnp.int32, (SUB, width), 0)
    lane = lax.broadcasted_iota(jnp.int32, (SUB, width), 1)
    return (lane // kernels) == row


def conv_forward(xs, mix_row, scaled_mix, widen, bank, groups, side):
    rows, channels = xs.shape
    kernels, width = bank.shape[3], bank.shape[4]
    block = widen.shape[0]
    steps = channels // block
    parts = block // SUB
    span = SUB * kernels
    low = rows // groups

    def body(x_ref, m_ref, s_ref, w_ref, b_ref, out_ref, raw_ref, dem_ref, acc, en):
        step = pl.program_id(0)

        @pl.when(step == 0)
        def _():
            acc[...] = jnp.zeros_like(acc)
            en[...] = jnp.zeros_like(en)

        wide = dot_nn(x_ref[...], w_ref[...]).reshape(groups, low, block * kernels)
        a = (wide * m_ref[...]).astype(BF).reshape(rows, block * kernels)
        mask = band_mask(kernels)[None]
        left = []
        for u in range(parts):
            d = jnp.where(mask, s_ref[:, :, u * span : (u + 1) * span], 0.0).astype(BF)
            left.append(
                jnp.concatenate([a[:, u * span : (u + 1) * span], d.reshape(groups * SUB, span)])
            )
        energy = en[...]
        for t in range(9):
            b = b_ref[t // 3, t % 3].reshape(block * kernels, width)
            total = acc[t]
            for u in range(parts):
                p = dot_nn(left[u], b[u * span : (u + 1) * span])
                total = total + p[:rows]
                m = p[rows:]
                energy = energy + jnp.sum((m * m).reshape(groups, SUB // 8, 8, width), axis=1)
            acc[t] = total
        en[...] = energy

        @pl.when(step == steps - 1)
        def _():
            demod = lax.rsqrt(jnp.sum(en[...], axis=1, keepdims=True) + 1e-8)
            dem_ref[...] = demod
            for s in range(groups):
                v = [acc[t, s * low : (s + 1) * low].reshape(side, side, width) for t in range(9)]
                for py in range(2):
                    h = []
                    for tx in range(3):
                        if py == 0:
                            h.append(move_up(v[tx], 0) + v[3 + tx] + v[6 + tx])
                        else:
                            h.append(v[tx] + v[3 + tx] + move_down(v[6 + tx], 0))
                    for px in range(2):
                        if px == 0:
                            o = move_up(h[0], 1) + h[1] + h[2]
                        else:
                            o = h[0] + h[1] + move_down(h[2], 1)
                        o = o.reshape(low, width)
                        q = (py * 2 + px) * low
                        raw_ref[s, q : q + low] = o.astype(raw_ref.dtype)
                        out_ref[s, q : q + low] = (o * demod[s]).astype(BF)

    return pl.pallas_call(
        body,
        grid=(steps,),
        in_specs=[
            pl.BlockSpec((rows, block), lambda i: (0, i)),
            pl.BlockSpec((groups, 1, block * kernels), lambda i: (0, 0, 0)),
            pl.BlockSpec((groups, 1, block * kernels), lambda i: (0, 0, i)),
            pl.BlockSpec((block, block * kernels), lambda i: (0, 0)),
            pl.BlockSpec((3, 3, block, kernels, width), lambda i: (0, 0, i, 0, 0)),
        ],
        out_specs=[
            pl.BlockSpec((groups, 4 * low, width), lambda i: (0, 0, 0)),
            pl.BlockSpec((groups, 4 * low, width), lambda i: (0, 0, 0)),
            pl.BlockSpec((groups, 1, width), lambda i: (0, 0, 0)),
        ],
        out_shape=[
            jax.ShapeDtypeStruct((groups, 4 * low, width), BF),
            jax.ShapeDtypeStruct((groups, 4 * low, width), BF),
            jax.ShapeDtypeStruct((groups, 1, width), F),
        ],
        scratch_shapes=[pltpu.VMEM((9, rows, width), F), pltpu.VMEM((groups, 8, width), F)],
        compiler_params=params(),
        cost_estimate=pl.CostEstimate(
            flops=27 * rows * channels * kernels * width,
            bytes_accessed=18 * channels * kernels * width,
            transcendentals=0,
        ),
        name="conv_forward",
    )(xs, mix_row, scaled_mix, widen, bank)


def conv_back(gs, xs, mix_row, widen, bank, groups):
    _, rows, width = gs.shape
    channels, kernels = xs.shape[1], bank.shape[3]
    block = widen.shape[0]
    steps = channels // block
    low = rows // groups

    def body(g_ref, x_ref, m_ref, w_ref, b_ref, low_ref, mix_ref, acc):
        step = pl.program_id(0)

        @pl.when(step == 0)
        def _():
            acc[...] = jnp.zeros_like(acc)

        total = None
        for t in range(9):
            p = dot_nt(g_ref[t], b_ref[t // 3, t % 3].reshape(block * kernels, width))
            total = p if total is None else total + p
        wide = dot_nn(x_ref[...], w_ref[...])
        acc[...] += jnp.sum((wide * total).reshape(groups, low // 8, 8, block * kernels), axis=1)
        mixed = total.reshape(groups, low, block * kernels) * m_ref[...]
        low_ref[...] = dot_nt(mixed.astype(BF).reshape(rows, block * kernels), w_ref[...]).astype(BF)

        @pl.when(step == steps - 1)
        def _():
            mix_ref[...] = jnp.sum(acc[...], axis=1, keepdims=True)

    return pl.pallas_call(
        body,
        grid=(steps,),
        in_specs=[
            pl.BlockSpec((9, rows, width), lambda i: (0, 0, 0)),
            pl.BlockSpec((rows, block), lambda i: (0, i)),
            pl.BlockSpec((groups, 1, block * kernels), lambda i: (0, 0, 0)),
            pl.BlockSpec((block, block * kernels), lambda i: (0, 0)),
            pl.BlockSpec((3, 3, block, kernels, width), lambda i: (0, 0, i, 0, 0)),
        ],
        out_specs=[
            pl.BlockSpec((rows, block), lambda i: (0, i)),
            pl.BlockSpec((groups, 1, block * kernels), lambda i: (0, 0, 0)),
        ],
        out_shape=[
            jax.ShapeDtypeStruct((rows, channels), BF),
            jax.ShapeDtypeStruct((groups, 1, block * kernels), F),
        ],
        scratch_shapes=[pltpu.VMEM((groups, 8, block * kernels), F)],
        compiler_params=params(),
        cost_estimate=pl.CostEstimate(
            flops=18 * rows * channels * kernels * width,
            bytes_accessed=18 * channels * kernels * width,
            transcendentals=0,
        ),
        name="conv_back",
    )(gs, xs, mix_row, widen, bank)


def bank_energy(scaled_mix, ge, bank, first, bands):
    samples = scaled_mix.shape[0]
    kernels, width = bank.shape[3], bank.shape[4]
    span = SUB * kernels
    chunk = min(samples, 32)
    chunks = samples // chunk
    kind = BF if chunks == 1 else F

    def body(first_ref, s_ref, g_ref, b_ref, e_ref, diag_ref):
        part = pl.program_id(1)
        mask = band_mask(kernels)[None]
        d = jnp.where(mask, s_ref[...], 0.0).astype(BF).reshape(chunk * SUB, span)
        d_turned = d.T
        acc = None
        for t in range(9):
            b = b_ref[t // 3, t % 3].reshape(span, width)
            m = dot_nn(d, b)
            w = (m.reshape(chunk, SUB, width) * g_ref[...]).reshape(chunk * SUB, width).astype(BF)
            e = dot_nn(d_turned, w).reshape(SUB, kernels, width)
            if chunks == 1:
                e_ref[t // 3, t % 3] = e.astype(kind)
            else:
                e_ref[t // 3, t % 3] = e + jnp.where(part == 0, 0.0, e_ref[t // 3, t % 3])
            p = dot_nt(w, b)
            acc = p if acc is None else acc + p
        kept = jnp.where(mask, acc.reshape(chunk, SUB, span), 0.0)
        diag_ref[...] = jnp.sum(kept, axis=1, keepdims=True)

    return pl.pallas_call(
        body,
        grid_spec=pltpu.PrefetchScalarGridSpec(
            num_scalar_prefetch=1,
            grid=(bands, chunks),
            in_specs=[
                pl.BlockSpec((chunk, 1, span), lambda i, c, s: (c, 0, i)),
                pl.BlockSpec((chunk, 1, width), lambda i, c, s: (c, 0, 0)),
                pl.BlockSpec((3, 3, SUB, kernels, width), lambda i, c, s: (0, 0, s[0] + i, 0, 0)),
            ],
            out_specs=[
                pl.BlockSpec((3, 3, SUB, kernels, width), lambda i, c, s: (0, 0, i, 0, 0)),
                pl.BlockSpec((chunk, 1, span), lambda i, c, s: (c, 0, i)),
            ],
        ),
        out_shape=[
            jax.ShapeDtypeStruct((3, 3, bands * SUB, kernels, width), kind),
            jax.ShapeDtypeStruct((samples, 1, bands * span), F),
        ],
        compiler_params=params(),
        cost_estimate=pl.CostEstimate(
            flops=54 * bands * samples * SUB * span * width,
            bytes_accessed=36 * bands * span * width,
            transcendentals=0,
        ),
        name="bank_energy",
    )(first, scaled_mix, ge, bank)


def bank_main(at, gs, energy):
    _, points, width = gs.shape
    band, kernels = energy.shape[2], energy.shape[3]

    def body(a_ref, g_ref, e_ref, o_ref):
        p = dot_nn(a_ref[...], g_ref[0]).reshape(band, kernels, width)
        o_ref[0, 0] = p + e_ref[0, 0].astype(F)

    return pl.pallas_call(
        body,
        grid=(9,),
        in_specs=[
            pl.BlockSpec((band * kernels, points), lambda t: (0, 0)),
            pl.BlockSpec((1, points, width), lambda t: (t, 0, 0)),
            pl.BlockSpec((1, 1, band, kernels, width), lambda t: (t // 3, t % 3, 0, 0, 0)),
        ],
        out_specs=pl.BlockSpec((1, 1, band, kernels, width), lambda t: (t // 3, t % 3, 0, 0, 0)),
        out_shape=jax.ShapeDtypeStruct((3, 3, band, kernels, width), F),
        compiler_params=params(),
        cost_estimate=pl.CostEstimate(
            flops=18 * band * kernels * points * width,
            bytes_accessed=18 * points * width + 54 * band * kernels * width,
            transcendentals=0,
        ),
        name="bank_main",
    )(at, gs, energy)


def tap_sums(grads, side):
    samples, _, width = grads.shape
    g = grads.astype(F).reshape(samples, 2, 2, side, side, width)
    lines = [g[:, 1] + move_down(g[:, 0], 2), g[:, 0] + g[:, 1], g[:, 0] + move_up(g[:, 1], 2)]
    out = []
    for v in lines:
        out.append(v[:, 1] + move_down(v[:, 0], 2))
        out.append(v[:, 0] + v[:, 1])
        out.append(v[:, 0] + move_up(v[:, 1], 2))
    return jnp.stack(out).astype(BF).reshape(9, samples * side * side, width)


def rms(field, gain):
    inverse = lax.rsqrt(jnp.mean(field * field, axis=-1, keepdims=True) + EPS)
    return field * inverse * gain, inverse


def rms_back(field, gain, grad_out):
    inverse = lax.rsqrt(jnp.mean(field * field, axis=-1, keepdims=True) + EPS)
    scaled = grad_out * gain
    grad_gain = jnp.sum(grad_out * field * inverse, axis=0, keepdims=True)
    mean = jnp.mean(scaled * field, axis=-1, keepdims=True)
    return inverse * scaled - field * inverse**3 * mean, grad_gain


def sigmoid(v):
    return 1.0 / (1.0 + jnp.exp(-v))


def silu_slope(v):
    q = sigmoid(v)
    return q * (1.0 + v * (1.0 - q))


def self_prob(q, k):
    kf = k.astype(F)
    square = jnp.sum(kf * kf, axis=1, keepdims=True)
    scores = (2.0 * dot_nt(k, q) - square) * (1.0 / math.sqrt(HD))
    e = jnp.exp(scores - jnp.max(scores, axis=0, keepdims=True))
    return e * (1.0 / jnp.sum(e, axis=0, keepdims=True))


def cross_prob(q, k):
    scores = dot_nt(k, q) * (1.0 / math.sqrt(HD))
    e = jnp.exp(scores - jnp.max(scores, axis=0, keepdims=True))
    return e * (1.0 / jnp.sum(e, axis=0, keepdims=True))


def middle_forward(conv, noise, noise_gain, bias, g_attn, g_cross, g_mlp, wqkv, wo, cq, co, ckv):
    points, channels = conv.shape
    n = len(wqkv)
    share = cq[0].shape[1]
    tokens = ckv[0].shape[0]

    def body(conv_ref, noise_ref, ng_ref, cb_ref, ga_ref, gc_ref, gm_ref, *rest):
        wqkv_r, wo_r, cq_r, co_r, ckv_r = (rest[i * n : (i + 1) * n] for i in range(5))
        two_ref, three_ref, mlp_ref, qkv_ref, att_ref, xq_ref, xatt_ref = rest[5 * n :]
        out = conv_ref[...].astype(F) + ng_ref[...] * noise_ref[...] + cb_ref[...]
        one = out * sigmoid(out)
        normed = rms(one, ga_ref[...])[0].astype(BF)
        two = one
        for j in range(n):
            qkv = dot_nn(normed, wqkv_r[j][...]).astype(BF)
            qkv_ref[j] = qkv
            heads = []
            for h in range(share // HD):
                q, k, v = (qkv[:, i * share + h * HD : i * share + (h + 1) * HD] for i in range(3))
                heads.append(dot_tn(self_prob(q, k).astype(BF), v).astype(BF))
            att_ref[j] = jnp.concatenate(heads, axis=1)
            two = two + dot_nn(att_ref[j], wo_r[j][...])
        two_ref[...] = two
        normed = rms(two, gc_ref[...])[0].astype(BF)
        three = two_ref[...]
        for j in range(n):
            xq = dot_nn(normed, cq_r[j][...]).astype(BF)
            xq_ref[j] = xq
            kv = ckv_r[j][...]
            heads = []
            for h in range(share // HD):
                q = xq[:, h * HD : (h + 1) * HD]
                k = kv[:, h * HD : (h + 1) * HD]
                v = kv[:, share + h * HD : share + (h + 1) * HD]
                heads.append(dot_tn(cross_prob(q, k).astype(BF), v).astype(BF))
            xatt_ref[j] = jnp.concatenate(heads, axis=1)
            three = three + dot_nn(xatt_ref[j], co_r[j][...])
        three_ref[...] = three
        mlp_ref[...] = rms(three, gm_ref[...])[0].astype(BF)

    return pl.pallas_call(
        body,
        out_shape=[
            jax.ShapeDtypeStruct((points, channels), F),
            jax.ShapeDtypeStruct((points, channels), F),
            jax.ShapeDtypeStruct((points, channels), BF),
            jax.ShapeDtypeStruct((n, points, 3 * share), BF),
            jax.ShapeDtypeStruct((n, points, share), BF),
            jax.ShapeDtypeStruct((n, points, share), BF),
            jax.ShapeDtypeStruct((n, points, share), BF),
        ],
        compiler_params=params(),
        cost_estimate=pl.CostEstimate(
            flops=14 * points * channels * channels,
            bytes_accessed=24 * channels * channels,
            transcendentals=points * points * channels // HD,
        ),
        name="middle_forward",
    )(conv, noise, noise_gain, bias, g_attn, g_cross, g_mlp, *wqkv, *wo, *cq, *co, *ckv)


def cross_backward(grad_norm, grad_four, three, two, g_mlp, g_cross, xq, xatt, cq, co, ckv):
    points, channels = three.shape
    n, _, share = xq.shape
    tokens = ckv[0].shape[0]

    def body(gn_ref, g4_ref, three_ref, two_ref, gm_ref, gc_ref, xq_ref, xatt_ref, *rest):
        cq_r, co_r, ckv_r = (rest[i * n : (i + 1) * n] for i in range(3))
        two_out, gmlp_out, gcross_out, dcq_ref, dco_ref, dkv_ref, held = rest[3 * n :]
        back, gain = rms_back(three_ref[...], gm_ref[...], gn_ref[...])
        gmlp_out[...] = gain
        grad_three = g4_ref[...] + back
        gb = grad_three.astype(BF)
        normed = rms(two_ref[...], gc_ref[...])[0].astype(BF)
        grad_norm2 = jnp.zeros((points, channels), F)
        for j in range(n):
            ga = dot_nt(gb, co_r[j][...]).astype(BF)
            dco_ref[j] = dot_tn(gb, xatt_ref[j]).astype(BF)
            kv = ckv_r[j][...]
            gq, gk, gv = [], [], []
            for h in range(share // HD):
                q = xq_ref[j, :, h * HD : (h + 1) * HD]
                k = kv[:, h * HD : (h + 1) * HD]
                v = kv[:, share + h * HD : share + (h + 1) * HD]
                g = ga[:, h * HD : (h + 1) * HD]
                p = cross_prob(q, k)
                gp = dot_nt(v, g)
                gs = p * (gp - jnp.sum(p * gp, axis=0, keepdims=True))
                raw = (gs * (1.0 / math.sqrt(HD))).astype(BF)
                gq.append(dot_tn(raw, k).astype(BF))
                gk.append(dot_nn(raw, q).astype(BF))
                gv.append(dot_nn(p.astype(BF), g).astype(BF))
            held[j] = jnp.concatenate(gq, axis=1)
            dkv_ref[j] = jnp.concatenate(gk + gv, axis=1)
            dcq_ref[j] = dot_tn(normed, held[j]).astype(BF)
            grad_norm2 = grad_norm2 + dot_nt(held[j], cq_r[j][...])
        back, gain = rms_back(two_ref[...], gc_ref[...], grad_norm2)
        gcross_out[...] = gain
        two_out[...] = grad_three + back

    return pl.pallas_call(
        body,
        out_shape=[
            jax.ShapeDtypeStruct((points, channels), F),
            jax.ShapeDtypeStruct((1, channels), F),
            jax.ShapeDtypeStruct((1, channels), F),
            jax.ShapeDtypeStruct((n, channels, share), BF),
            jax.ShapeDtypeStruct((n, channels, share), BF),
            jax.ShapeDtypeStruct((n, tokens, 2 * share), BF),
        ],
        scratch_shapes=[pltpu.VMEM((n, points, share), BF)],
        compiler_params=params(),
        cost_estimate=pl.CostEstimate(
            flops=8 * points * channels * channels,
            bytes_accessed=12 * channels * channels,
            transcendentals=points * channels,
        ),
        name="cross_backward",
    )(grad_norm, grad_four, three, two, g_mlp, g_cross, xq, xatt, *cq, *co, *ckv)


def attn_backward(grad_two, conv, noise, noise_gain, bias, g_attn, qkv, att, wqkv, wo):
    points, channels = grad_two.shape
    n, _, share = att.shape

    def body(g2_ref, conv_ref, noise_ref, ng_ref, cb_ref, ga_ref, qkv_ref, att_ref, *rest):
        wqkv_r, wo_r = rest[:n], rest[n : 2 * n]
        gc_ref, sums_ref, dqkv_ref, dwo_ref, held = rest[2 * n :]
        grad_two = g2_ref[...]
        gb = grad_two.astype(BF)
        out = conv_ref[...].astype(F) + ng_ref[...] * noise_ref[...] + cb_ref[...]
        one = out * sigmoid(out)
        normed = rms(one, ga_ref[...])[0].astype(BF)
        grad_norm = jnp.zeros((points, channels), F)
        for j in range(n):
            ga = dot_nt(gb, wo_r[j][...]).astype(BF)
            dwo_ref[j] = dot_tn(gb, att_ref[j]).astype(BF)
            gq, gk, gv = [], [], []
            for h in range(share // HD):
                q, k, v = (
                    qkv_ref[j, :, i * share + h * HD : i * share + (h + 1) * HD] for i in range(3)
                )
                g = ga[:, h * HD : (h + 1) * HD]
                p = self_prob(q, k)
                gp = dot_nt(v, g)
                gs = p * (gp - jnp.sum(p * gp, axis=0, keepdims=True))
                square = jnp.sum(gs, axis=1, keepdims=True) * (-1.0 / math.sqrt(HD))
                raw = (gs * (2.0 / math.sqrt(HD))).astype(BF)
                gq.append(dot_tn(raw, k).astype(BF))
                gk.append((dot_nn(raw, q) + 2.0 * k.astype(F) * square).astype(BF))
                gv.append(dot_nn(p.astype(BF), g).astype(BF))
            held[j] = jnp.concatenate(gq + gk + gv, axis=1)
            dqkv_ref[j] = dot_tn(normed, held[j]).astype(BF)
            grad_norm = grad_norm + dot_nt(held[j], wqkv_r[j][...])
        back, gain = rms_back(one, ga_ref[...], grad_norm)
        grad_conv = (grad_two + back) * silu_slope(out)
        gc_ref[...] = grad_conv.astype(BF)
        sums_ref[0:1] = gain
        sums_ref[1:2] = jnp.sum(grad_conv, axis=0, keepdims=True)
        sums_ref[2:3] = jnp.sum(grad_conv * noise_ref[...], axis=0, keepdims=True)

    return pl.pallas_call(
        body,
        out_shape=[
            jax.ShapeDtypeStruct((points, channels), BF),
            jax.ShapeDtypeStruct((3, channels), F),
            jax.ShapeDtypeStruct((n, channels, 3 * share), BF),
            jax.ShapeDtypeStruct((n, channels, share), BF),
        ],
        scratch_shapes=[pltpu.VMEM((n, points, 3 * share), BF)],
        compiler_params=params(),
        cost_estimate=pl.CostEstimate(
            flops=24 * points * channels * channels,
            bytes_accessed=24 * channels * channels,
            transcendentals=points * points * channels // HD,
        ),
        name="attn_backward",
    )(grad_two, conv, noise, noise_gain, bias, g_attn, qkv, att, *wqkv, *wo)


def local(
    images,
    styles,
    labels,
    noise_map,
    counts,
    cot_features,
    cot_image,
    kernel_bank,
    select_proj,
    style_proj,
    conv_bias,
    noise_gain,
    norm_attn,
    query_proj,
    key_proj,
    value_proj,
    out_proj,
    norm_cross,
    cross_query,
    cross_key,
    cross_value,
    cross_out,
    class_table,
    class_pos,
    norm_mlp,
    up_proj,
    down_proj,
    rgb_style,
    color_projection,
    color_bias,
):
    n, n_dp = lax.axis_size("rows"), lax.axis_size("dp")
    r, d = lax.axis_index("rows"), lax.axis_index("dp")
    side, channels = images.shape[1], images.shape[3]
    low = side * side
    points = 4 * low
    kernels, width = kernel_bank.shape[3], kernel_bank.shape[4]
    tokens = class_pos.shape[0]
    share = query_proj.shape[1]
    band = channels // n_dp
    samples = n * n_dp

    def by_phase(field):
        rest = field.shape[2:]
        split = field.reshape((side, 2, side, 2) + rest)
        order = (1, 3, 0, 2) + tuple(range(4, 4 + len(rest)))
        return split.transpose(order).reshape((points,) + rest)

    group_order = jnp.arange(n, dtype=jnp.int32) ^ r
    slots = jnp.arange(n_dp, dtype=jnp.int32)
    ring_order = ring_source(n_dp, d, slots)
    ring_back = ((d // 2 - slots // 2) % (n_dp // 2)) * 2 + ((d % 2) ^ (slots % 2))

    def row(v):
        return v.astype(F).reshape(1, -1)

    def style_values(codes):
        mixing = jax.nn.softmax(
            jnp.dot(codes, select_proj, preferred_element_type=F), axis=-1
        )
        scale = jnp.dot(codes, style_proj, preferred_element_type=F) + 1.0
        return mixing, scale

    def scaled_rows(mixing, scale):
        return (scale[:, :, None] * mixing[:, None, :]).reshape(scale.shape[0], 1, -1)

    codes = jnp.take(styles, group_order, axis=0)
    mixing, scale_in = style_values(codes)
    own_scale = scale_in[0]
    own_images = images[0].reshape(low, channels)
    modulated = (own_images.astype(F) * own_scale).astype(BF)
    xs = jnp.concatenate(spread(modulated))
    block = min(channels, 128)
    widen = (
        jnp.arange(block * kernels, dtype=jnp.int32)[None, :] // kernels
        == jnp.arange(block, dtype=jnp.int32)[:, None]
    ).astype(BF)
    mix_row = jnp.tile(mixing, (1, block))[:, None, :]
    conv_part, conv_raw, demod = conv_forward(
        xs, mix_row, scaled_rows(mixing, scale_in), widen, kernel_bank, n, side
    )

    wqkv = spread(jnp.concatenate([query_proj, key_proj, value_proj], axis=1))
    wo = spread(out_proj)
    cq = spread(cross_query)
    co = spread(cross_out)

    class_rows = jnp.take(class_table, jnp.take(labels, group_order), axis=0)
    context = (class_rows.astype(F)[:, None, :] + class_pos.astype(F)[None]).astype(BF)
    flat_context = context.reshape(n * tokens, channels)
    ckv = jnp.dot(
        flat_context,
        jnp.concatenate([cross_key, cross_value], axis=1),
        preferred_element_type=F,
    ).astype(BF)
    ckv = ckv.reshape(n, tokens, 2 * share)
    ckv = [ckv[0]] + [swap(ckv[j], "rows", j) for j in range(1, n)]

    live = counts.astype(F)
    total = add_over(jnp.broadcast_to(jnp.sum(live), (8, 128)), "dp")[0, 0]
    own_live = lax.dynamic_index_in_dim(live, r, 0, keepdims=False) / total
    color_scale = (
        jnp.dot(codes[:1], rgb_style, preferred_element_type=F) + 1.0
    )
    grad_image = by_phase(cot_image[0].transpose(1, 2, 0)) * own_live
    colors = color_projection.astype(F)
    tinted = jnp.dot(grad_image, colors.T, precision=lax.Precision.HIGHEST)
    grad_four = by_phase(cot_features[0]).astype(F) * own_live + tinted * color_scale
    grad_four_group = spread(grad_four.astype(BF))

    parts = [conv_part[0]] + [swap(conv_part[j], "rows", j) for j in range(1, n)]
    parts = jnp.stack(parts)
    conv = jnp.concatenate(
        [lax.dynamic_index_in_dim(parts, r ^ j, 0, keepdims=False) for j in range(n)], axis=1
    )
    noise = by_phase(noise_map[0]).astype(F).reshape(points, 1)
    rows_of = (row(noise_gain), row(conv_bias), row(norm_attn))
    two, three, normed_mlp, qkv, att, xq, xatt = middle_forward(
        conv, noise, *rows_of, row(norm_cross), row(norm_mlp), wqkv, wo, cq, co, ckv
    )

    mlp_in = spread(normed_mlp)
    forward, backward, acts, inners = [], [], [], []
    for j in range(n):
        inner = jnp.dot(mlp_in[j], up_proj, preferred_element_type=F)
        gate = sigmoid(inner)
        act = (inner * gate).astype(BF)
        grad_act = lax.dot_general(
            grad_four_group[j], down_proj, (((1,), (1,)), ((), ())), preferred_element_type=F
        )
        grad_inner = (grad_act * (gate * (1.0 + inner * (1.0 - gate)))).astype(BF)
        backward.append(dot_nt(grad_inner, up_proj).astype(BF))
        forward.append(jnp.dot(act, down_proj, preferred_element_type=F).astype(BF))
        acts.append(act)
        inners.append(grad_inner)
    grad_norm = collect(backward)
    four = three + collect(forward)
    d_up = sum(dot_tn(mlp_in[j], inners[j]) for j in range(n))
    d_down = sum(dot_tn(grad_four_group[j], acts[j]) for j in range(n))

    features = four.reshape(2, 2, side, side, channels).transpose(2, 0, 3, 1, 4)
    features = features.reshape(1, 2 * side, 2 * side, channels)
    tint = color_scale.T * colors
    color_image = jnp.dot(four, tint, precision=lax.Precision.HIGHEST) + color_bias.astype(F)
    color_image = color_image.reshape(2, 2, side, side, 3).transpose(4, 2, 0, 3, 1)
    color_image = color_image.reshape(1, 3, 2 * side, 2 * side)
    four_image = lax.dot_general(
        four, grad_image, (((0,), (0,)), ((), ())), precision=lax.Precision.HIGHEST
    )
    grad_colors = four_image * color_scale.T
    grad_scale_rgb = jnp.sum(four_image * colors, axis=1)
    grad_color_bias = jnp.sum(grad_image, axis=0)

    grad_two, d_norm_mlp, d_norm_cross, dcq, dco, dkv = cross_backward(
        grad_norm, grad_four, three, two, row(norm_mlp), row(norm_cross), xq, xatt, cq, co, ckv
    )
    grad_conv, late_sums, dqkv, dwo = attn_backward(
        grad_two, conv, noise, *rows_of, qkv, att, wqkv, wo
    )

    dkv = [dkv[0]] + [swap(dkv[j], "rows", j) for j in range(1, n)]
    dkv = jnp.concatenate(dkv)
    d_ck_cv = dot_tn(flat_context, dkv).astype(BF)
    grad_context = dot_nt(dkv[:, :share], cross_key) + dot_nt(dkv[:, share:], cross_value)
    grad_context = grad_context.reshape(n, tokens, channels)
    token_sum = jnp.take(jnp.sum(grad_context, axis=1), group_order, axis=0)

    rgb_rows = jnp.where((jnp.arange(n) == r)[:, None], grad_scale_rgb[None], 0.0)
    bias_row = jnp.pad(grad_color_bias, (0, channels - 3))[None]
    early = jnp.concatenate(
        [jnp.sum(grad_context, axis=0), d_norm_mlp, d_norm_cross, grad_colors.T, bias_row]
    )
    held = add_over(jnp.concatenate([early, token_sum, rgb_rows]), "rows")
    count = early.shape[0]
    early, per_sample = merge(held[:count], held[count:], "dp", d)
    per_sample = per_sample.reshape(n_dp, 2, n, channels)
    token_all = per_sample[:, 0].reshape(samples, channels)
    rgb_all = per_sample[:, 1].reshape(samples, channels)
    styles_all = double(styles, "dp", d)
    labels_all = double(labels, "dp", d)

    shares = [
        lax.dynamic_slice_in_dim(grad_conv, (r ^ j) * width, width, axis=1) for j in range(n)
    ]
    shares = jnp.stack([shares[0]] + [swap(shares[j], "rows", j) for j in range(1, n)])
    grad_part = shares.astype(F)
    grad_demod = jnp.sum(grad_part * conv_raw.astype(F), axis=1, keepdims=True)
    grad_energy = -0.5 * grad_demod * demod**3
    grad_taps = (grad_part * demod).astype(BF)

    ge_all = jnp.concatenate(ring_gather(grad_energy[:, 0])).reshape(samples, 1, width)
    taps_all = jnp.stack(ring_gather(grad_taps)).reshape(samples, points, width)

    xs_points = xs.reshape(n * low, n_dp, band)
    band_blocks = []
    for slot in range(n_dp):
        target = ring_target(n_dp, d, slot)
        piece = lax.dynamic_slice_in_dim(xs, target * band, band, axis=1)
        if slot:
            piece = lax.ppermute(piece, "dp", ring_perm(n_dp, slot // 2, slot % 2))
        band_blocks.append(piece)
    x_turned = jnp.concatenate(band_blocks).T
    codes_all = jnp.take(styles_all.reshape(n_dp, n, -1), ring_order, axis=0)
    codes_all = jnp.take(codes_all, group_order, axis=1).reshape(samples, -1)
    mixing_all, scale_all = style_values(codes_all)
    scale_band = lax.dynamic_slice_in_dim(scale_all, d * band, band, axis=1)
    first = (d * (band // SUB)).astype(jnp.int32).reshape(1)
    energy, diag = bank_energy(
        scaled_rows(mixing_all, scale_band), 2.0 * ge_all, kernel_bank, first, band // SUB
    )
    diag = diag.reshape(samples, band, kernels)
    scale_energy = jnp.sum(diag * mixing_all[:, None, :], axis=2)
    mixing_energy = jnp.sum(diag * scale_band[:, :, None], axis=1)
    at = x_turned.astype(F)[:, None, :] * jnp.repeat(mixing_all.T, low, axis=1)[None]
    at = at.astype(BF).reshape(band * kernels, samples * low)
    grad_bank = bank_main(at, tap_sums(taps_all, side), energy)

    gs = tap_sums(grad_taps, side)
    low_part, mix_part = conv_back(gs, xs, mix_row, widen, kernel_bank, n)
    low_part = low_part.reshape(n, low, channels)
    grad_low = collect([low_part[j] for j in range(n)])
    grad_images = (grad_low * own_scale).reshape(1, side, side, channels)
    scale_low = jnp.sum(grad_low * own_images.astype(F), axis=0)
    mixing_conv = jnp.sum(mix_part.reshape(n, block, kernels), axis=1)

    def ordered(field):
        rest = field.shape[1:]
        field = jnp.take(field.reshape((n_dp, n) + rest), ring_back, axis=0)
        return jnp.take(field, group_order, axis=1).reshape((samples,) + rest)

    scale_rows = jnp.where((jnp.arange(n) == r)[:, None], scale_low[None], 0.0)
    energy_rows = ordered(scale_energy).reshape(n, channels)
    mixing_rows = jnp.take(mixing_conv, group_order, axis=0).reshape(1, -1)
    mixing_rows = jnp.pad(mixing_rows, ((0, 0), (0, channels - mixing_rows.shape[1])))
    mixing_sum = ordered(mixing_energy).reshape(1, -1)
    mixing_sum = jnp.pad(mixing_sum, ((0, 0), (0, -mixing_sum.shape[1] % channels)))
    mixing_sum = mixing_sum.reshape(-1, channels)
    sums = jnp.concatenate([late_sums, mixing_sum])
    count = sums.shape[0]
    held = add_over(jnp.concatenate([sums, scale_rows, energy_rows, mixing_rows]), "rows")
    sums, per_sample = merge(held[:count], held[count:], "dp", d)
    late_sums, mixing_sum = sums[:3], sums[3:]
    per_sample = per_sample.reshape(n_dp, 2 * n + 1, channels)
    scale_grad = per_sample[:, :n].reshape(samples, channels)
    bands_grad = per_sample[:, n : 2 * n].reshape(n_dp, samples, band).transpose(1, 0, 2)
    scale_grad = scale_grad + bands_grad.reshape(samples, channels)
    mixing_grad = per_sample[:, 2 * n, : n * kernels].reshape(samples, kernels)
    mixing_grad = mixing_grad + mixing_sum.reshape(-1)[: samples * kernels].reshape(samples, kernels)
    mixing_flat = style_values(styles_all)[0]
    grad_logit = mixing_flat * (
        mixing_grad - jnp.sum(mixing_flat * mixing_grad, axis=-1, keepdims=True)
    )

    def style_weight(grad):
        return dot_tn(styles_all, grad.astype(BF))

    def own_group(field):
        return lax.dynamic_slice_in_dim(field, d * n, n, axis=0)

    styles_grad = (
        dot_nt(own_group(grad_logit).astype(BF), select_proj)
        + dot_nt(own_group(scale_grad).astype(BF), style_proj)
        + dot_nt(own_group(rgb_all).astype(BF), rgb_style)
    )
    class_ids = jnp.arange(class_table.shape[0], dtype=jnp.int32)
    one_hot = (labels_all[:, None] == class_ids[None, :]).astype(F)
    d_table = lax.dot_general(
        one_hot, token_all, (((0,), (0,)), ((), ())), precision=lax.Precision.HIGHEST
    )

    def scatter(grads):
        return lax.psum_scatter(grads, "dp", scatter_dimension=0, tiled=True).astype(F)

    g_mlp = scatter(jnp.concatenate([d_up.astype(BF), d_down.astype(BF)], axis=1))
    wide = up_proj.shape[1]
    g_cross = [collect([dcq[j] for j in range(n)]), collect([dco[j] for j in range(n)])]
    g_cross = scatter(jnp.concatenate([g.astype(BF) for g in g_cross] + [d_ck_cv], axis=1))
    g_attn = [collect([dqkv[j] for j in range(n)]), collect([dwo[j] for j in range(n)])]
    g_attn = scatter(jnp.concatenate([g.astype(BF) for g in g_attn], axis=1))

    def column(grads, i):
        return grads[:, i * share : (i + 1) * share]

    return (
        features,
        color_image,
        grad_images,
        styles_grad,
        grad_bank,
        style_weight(grad_logit),
        style_weight(scale_grad),
        late_sums[1],
        late_sums[2],
        late_sums[0],
        column(g_attn, 0),
        column(g_attn, 1),
        column(g_attn, 2),
        column(g_attn, 3).T,
        early[tokens + 1],
        column(g_cross, 0),
        column(g_cross, 2),
        column(g_cross, 3),
        column(g_cross, 1).T,
        d_table,
        early[:tokens],
        early[tokens],
        g_mlp[:, :wide],
        g_mlp[:, wide:].T,
        style_weight(rgb_all),
        early[tokens + 2 : tokens + 5].T,
        early[tokens + 5, :3],
    )


def solution(mesh):
    whole = P()
    columns = P(None, "rows")
    lines = P("rows", None)
    both = P(("dp", "rows"), None, None, None)
    placed = (
        both,
        P("dp", None),
        P("dp"),
        P(("dp", "rows"), None, None),
        P("dp"),
        both,
        both,
        P(None, None, None, None, "rows"),
        whole,
        whole,
        whole,
        whole,
        whole,
        columns,
        columns,
        columns,
        lines,
        whole,
        columns,
        columns,
        columns,
        lines,
        whole,
        whole,
        whole,
        columns,
        lines,
        whole,
        whole,
        whole,
    )
    given = (
        both,
        both,
        both,
        P("dp", None),
        P(None, None, "dp", None, "rows"),
        whole,
        whole,
        whole,
        whole,
        whole,
        P("dp", "rows"),
        P("dp", "rows"),
        P("dp", "rows"),
        P("rows", "dp"),
        whole,
        P("dp", "rows"),
        P("dp", "rows"),
        P("dp", "rows"),
        P("rows", "dp"),
        whole,
        whole,
        whole,
        P("dp", "rows"),
        P("rows", "dp"),
        whole,
        whole,
        whole,
    )
    return jax.shard_map(local, mesh=mesh, in_specs=placed, out_specs=given, check_vma=False)
```

```python
import functools
import math

import jax
import jax.numpy as jnp
from jax import lax
from jax.experimental import pallas as pl
from jax.experimental.pallas import tpu as pltpu
from jax.sharding import PartitionSpec as P

HD = 64
SUB = 32
BF = jnp.bfloat16
F = jnp.float32
VMEM_LIMIT = 56 * 2**20
EPS = 1e-6


def dot_nn(a, b):
    return lax.dot_general(a, b, (((1,), (0,)), ((), ())), preferred_element_type=F)


def dot_nt(a, b):
    return lax.dot_general(a, b, (((1,), (1,)), ((), ())), preferred_element_type=F)


def dot_tn(a, b):
    return lax.dot_general(a, b, (((0,), (0,)), ((), ())), preferred_element_type=F)


def params():
    return pltpu.CompilerParams(vmem_limit_bytes=VMEM_LIMIT)


def swap(x, axis, delta):
    n = lax.axis_size(axis)
    return lax.ppermute(x, axis, [(i, i ^ delta) for i in range(n)])


def spread(x):
    n = lax.axis_size("rows")
    blocks = [None] * n
    blocks[0] = x
    for j in range(2, n, 2):
        blocks[j] = swap(x, "rows", j)
    for j in range(0, n, 2):
        blocks[j + 1] = swap(blocks[j], "rows", 1)
    return blocks


def near_sums(blocks):
    out = []
    for j in range(0, len(blocks), 2):
        near = blocks[j].astype(F) + swap(blocks[j + 1], "rows", 1).astype(F)
        out.append(near.astype(BF))
    return out


def far_sum(near):
    total = near[0].astype(F)
    for j in range(1, len(near)):
        total = total + swap(near[j], "rows", 2 * j).astype(F)
    return total


def collect(blocks):
    return far_sum(near_sums(blocks))


def double(x, axis, place):
    delta = 1
    while delta < lax.axis_size(axis):
        other = swap(x, axis, delta)
        high = (place & delta) != 0
        x = jnp.where(high, jnp.concatenate([other, x]), jnp.concatenate([x, other]))
        delta *= 2
    return x


def merge_step(sums, gathered, axis, place, delta):
    rows = sums.shape[0]
    other = swap(jnp.concatenate([sums, gathered]), axis, delta)
    high = (place & delta) != 0
    theirs = other[rows:]
    gathered = jnp.where(
        high, jnp.concatenate([theirs, gathered]), jnp.concatenate([gathered, theirs])
    )
    return sums + other[:rows], gathered


def add_over(sums, axis):
    delta = 1
    while delta < lax.axis_size(axis):
        sums = sums + swap(sums, axis, delta)
        delta *= 2
    return sums


def tree(parts):
    while len(parts) > 1:
        parts = [a + b for a, b in zip(parts[::2], parts[1::2])]
    return parts[0]


def everyone(x, axis):
    return [x] + [swap(x, axis, j) for j in range(1, lax.axis_size(axis))]


def in_order(blocks, place):
    stacked = jnp.stack(blocks)
    return jnp.take(stacked, jnp.arange(len(blocks), dtype=jnp.int32) ^ place, axis=0)


def ring_perm(n, step, flip):
    lines = n // 2
    return [(i, ((i // 2 + step) % lines) * 2 + ((i % 2) ^ flip)) for i in range(n)]


def ring_gather(x):
    n = lax.axis_size("dp")
    out = []
    held = x
    for step in range(n // 2):
        if step:
            held = lax.ppermute(held, "dp", ring_perm(n, 1, 0))
        out.append(held)
        out.append(lax.ppermute(held, "dp", ring_perm(n, 0, 1)))
    return out


def ring_source(n, place, slot):
    lines = n // 2
    return ((place // 2 - slot // 2) % lines) * 2 + ((place % 2) ^ (slot % 2))


def ring_target(n, place, slot):
    lines = n // 2
    return ((place // 2 + slot // 2) % lines) * 2 + ((place % 2) ^ (slot % 2))


def scatter_side(grads):
    n = lax.axis_size("dp")
    side = lax.axis_index("dp") % 2
    bands = grads.reshape(n // 2, 2, grads.shape[0] // n, grads.shape[1])
    mine = lax.dynamic_index_in_dim(bands, side, 1, keepdims=False)
    theirs = lax.dynamic_index_in_dim(bands, 1 - side, 1, keepdims=False)
    return mine, lax.ppermute(theirs, "dp", ring_perm(n, 0, 1))


def scatter_lines(mine, theirs):
    n = lax.axis_size("dp")
    lines = n // 2
    line = lax.axis_index("dp") // 2
    half = (mine.astype(F) + theirs.astype(F)).astype(BF)
    pieces = [lax.dynamic_index_in_dim(half, line, 0, keepdims=False)]
    for step in range(1, lines):
        piece = lax.dynamic_index_in_dim(half, (line + step) % lines, 0, keepdims=False)
        pieces.append(lax.ppermute(piece, "dp", ring_perm(n, step, 0)))
    return pieces


def tie(*values):
    return lax.optimization_barrier(values)


def move_up(v, axis):
    shape = list(v.shape)
    shape[axis] = 1
    kept = lax.slice_in_dim(v, 0, v.shape[axis] - 1, axis=axis)
    return jnp.concatenate([jnp.zeros(shape, v.dtype), kept], axis=axis)


def move_down(v, axis):
    shape = list(v.shape)
    shape[axis] = 1
    kept = lax.slice_in_dim(v, 1, v.shape[axis], axis=axis)
    return jnp.concatenate([kept, jnp.zeros(shape, v.dtype)], axis=axis)


def band_mask(kernels):
    width = SUB * kernels
    row = lax.broadcasted_iota(jnp.int32, (SUB, width), 0)
    lane = lax.broadcasted_iota(jnp.int32, (SUB, width), 1)
    return (lane // kernels) == row


def split_dot(a, b):
    high = a.astype(BF)
    rest = (a - high.astype(F)).astype(BF)
    return dot_nn(high, b) + dot_nn(rest, b)


def widen_mask(block, kernels):
    row = lax.broadcasted_iota(jnp.int32, (block, block * kernels), 0)
    lane = lax.broadcasted_iota(jnp.int32, (block, block * kernels), 1)
    return jnp.where(lane // kernels == row, 1.0, 0.0).astype(BF)


def tile_mask(block, kernels):
    row = lax.broadcasted_iota(jnp.int32, (kernels, block * kernels), 0)
    lane = lax.broadcasted_iota(jnp.int32, (kernels, block * kernels), 1)
    return jnp.where(lane % kernels == row, 1.0, 0.0).astype(BF)


def conv_forward(codes, select, style, images, bank, side):
    groups = len(images)
    low, channels = images[0].shape
    rows = groups * low
    kernels, width = bank.shape[3], bank.shape[4]
    pad, depth = codes.shape
    block = min(channels, 128)
    steps = channels // block
    parts = block // SUB
    span = SUB * kernels

    def body(c_ref, sel_ref, sty_ref, *rest):
        x_refs = rest[:groups]
        b_ref, out_ref, raw_ref, dem_ref, xs_ref, mix_ref, sc_ref = rest[groups : groups + 7]
        acc, en, scale, mix_row, widen = rest[groups + 7 :]
        step = pl.program_id(0)

        @pl.when(step == 0)
        def _():
            acc[...] = jnp.zeros_like(acc)
            en[...] = jnp.zeros_like(en)
            logits = dot_nn(c_ref[...], sel_ref[...])
            e = jnp.exp(logits - jnp.max(logits, axis=1, keepdims=True))
            mixing = e / jnp.sum(e, axis=1, keepdims=True)
            mix_ref[...] = mixing
            mix_row[...] = split_dot(mixing, tile_mask(block, kernels))
            scale[...] = dot_nn(c_ref[...], sty_ref[...]) + 1.0
            sc_ref[...] = scale[...]
            widen[...] = widen_mask(block, kernels)

        here = scale[:, pl.ds(pl.multiple_of(step * block, block), block)]
        wide_scale = split_dot(here, widen[...]) * mix_row[...]
        mask = band_mask(kernels)
        xs = []
        for s in range(groups):
            xs.append((x_refs[s][...].astype(F) * here[s : s + 1]).astype(BF))
            xs_ref[s * low : (s + 1) * low] = xs[s]
        a = []
        for s in range(groups):
            a.append((dot_nn(xs[s], widen[...]) * mix_row[s : s + 1]).astype(BF))
        left = []
        for u in range(parts):
            cut = slice(u * span, (u + 1) * span)
            pieces = [v[:, cut] for v in a]
            for s in range(groups):
                pieces.append(jnp.where(mask, wide_scale[s : s + 1, cut], 0.0).astype(BF))
            left.append(jnp.concatenate(pieces))
        energy = en[...]
        for t in range(9):
            b = b_ref[t // 3, t % 3].reshape(block * kernels, width)
            total = acc[t]
            for u in range(parts):
                p = dot_nn(left[u], b[u * span : (u + 1) * span])
                total = total + p[:rows]
                m = p[rows:]
                energy = energy + jnp.sum((m * m).reshape(groups, SUB // 8, 8, width), axis=1)
            acc[t] = total
        en[...] = energy

        @pl.when(step == steps - 1)
        def _():
            demod = lax.rsqrt(jnp.sum(en[...], axis=1, keepdims=True) + 1e-8)
            dem_ref[...] = demod
            for s in range(groups):
                v = [acc[t, s * low : (s + 1) * low].reshape(side, side, width) for t in range(9)]
                for py in range(2):
                    h = []
                    for tx in range(3):
                        if py == 0:
                            h.append(move_up(v[tx], 0) + v[3 + tx] + v[6 + tx])
                        else:
                            h.append(v[tx] + v[3 + tx] + move_down(v[6 + tx], 0))
                    for px in range(2):
                        if px == 0:
                            o = move_up(h[0], 1) + h[1] + h[2]
                        else:
                            o = h[0] + h[1] + move_down(h[2], 1)
                        o = o.reshape(low, width)
                        q = (py * 2 + px) * low
                        raw_ref[s, q : q + low] = o.astype(raw_ref.dtype)
                        out_ref[s, q : q + low] = (o * demod[s]).astype(BF)

    return pl.pallas_call(
        body,
        grid=(steps,),
        in_specs=[
            pl.BlockSpec((pad, depth), lambda i: (0, 0)),
            pl.BlockSpec((depth, kernels), lambda i: (0, 0)),
            pl.BlockSpec((depth, channels), lambda i: (0, 0)),
        ]
        + [pl.BlockSpec((low, block), lambda i: (0, i))] * groups
        + [pl.BlockSpec((3, 3, block, kernels, width), lambda i: (0, 0, i, 0, 0))],
        out_specs=[
            pl.BlockSpec((groups, 4 * low, width), lambda i: (0, 0, 0)),
            pl.BlockSpec((groups, 4 * low, width), lambda i: (0, 0, 0)),
            pl.BlockSpec((groups, 1, width), lambda i: (0, 0, 0)),
            pl.BlockSpec((rows, block), lambda i: (0, i)),
            pl.BlockSpec((pad, kernels), lambda i: (0, 0)),
            pl.BlockSpec((pad, channels), lambda i: (0, 0)),
        ],
        out_shape=[
            jax.ShapeDtypeStruct((groups, 4 * low, width), BF),
            jax.ShapeDtypeStruct((groups, 4 * low, width), BF),
            jax.ShapeDtypeStruct((groups, 1, width), F),
            jax.ShapeDtypeStruct((rows, channels), BF),
            jax.ShapeDtypeStruct((pad, kernels), F),
            jax.ShapeDtypeStruct((pad, channels), F),
        ],
        scratch_shapes=[
            pltpu.VMEM((9, rows, width), F),
            pltpu.VMEM((groups, 8, width), F),
            pltpu.VMEM((pad, channels), F),
            pltpu.VMEM((pad, block * kernels), F),
            pltpu.VMEM((block, block * kernels), BF),
        ],
        compiler_params=params(),
        cost_estimate=pl.CostEstimate(
            flops=27 * rows * channels * kernels * width,
            bytes_accessed=18 * channels * kernels * width,
            transcendentals=0,
        ),
        name="conv_forward",
    )(codes, select, style, *images, bank)


def conv_back(gs, xs, mixing, bank, groups):
    _, rows, width = gs.shape
    channels, kernels = xs.shape[1], bank.shape[3]
    pad = mixing.shape[0]
    block = min(channels, 128)
    steps = channels // block
    low = rows // groups

    def body(g_ref, x_ref, m_ref, b_ref, low_ref, mix_ref, acc, mix_row, widen):
        step = pl.program_id(0)

        @pl.when(step == 0)
        def _():
            acc[...] = jnp.zeros_like(acc)
            mix_row[...] = split_dot(m_ref[...], tile_mask(block, kernels))
            widen[...] = widen_mask(block, kernels)

        total = None
        for t in range(9):
            p = dot_nt(g_ref[t], b_ref[t // 3, t % 3].reshape(block * kernels, width))
            total = p if total is None else total + p
        wide = dot_nn(x_ref[...], widen[...])
        acc[...] += jnp.sum((wide * total).reshape(groups, low // 8, 8, block * kernels), axis=1)
        for s in range(groups):
            cut = slice(s * low, (s + 1) * low)
            mixed = (total[cut] * mix_row[s : s + 1]).astype(BF)
            low_ref[s] = dot_nt(mixed, widen[...]).astype(BF)

        @pl.when(step == steps - 1)
        def _():
            sums = jnp.sum(acc[...], axis=1)
            mix_ref[...] = lax.dot_general(
                sums,
                tile_mask(block, kernels).astype(F),
                (((1,), (1,)), ((), ())),
                precision=lax.Precision.HIGHEST,
                preferred_element_type=F,
            )

    return pl.pallas_call(
        body,
        grid=(steps,),
        in_specs=[
            pl.BlockSpec((9, rows, width), lambda i: (0, 0, 0)),
            pl.BlockSpec((rows, block), lambda i: (0, i)),
            pl.BlockSpec((pad, kernels), lambda i: (0, 0)),
            pl.BlockSpec((3, 3, block, kernels, width), lambda i: (0, 0, i, 0, 0)),
        ],
        out_specs=[
            pl.BlockSpec((groups, low, block), lambda i: (0, 0, i)),
            pl.BlockSpec((groups, kernels), lambda i: (0, 0)),
        ],
        out_shape=[
            jax.ShapeDtypeStruct((groups, low, channels), BF),
            jax.ShapeDtypeStruct((groups, kernels), F),
        ],
        scratch_shapes=[
            pltpu.VMEM((groups, 8, block * kernels), F),
            pltpu.VMEM((pad, block * kernels), F),
            pltpu.VMEM((block, block * kernels), BF),
        ],
        compiler_params=params(),
        cost_estimate=pl.CostEstimate(
            flops=18 * rows * channels * kernels * width,
            bytes_accessed=18 * channels * kernels * width,
            transcendentals=0,
        ),
        name="conv_back",
    )(gs, xs, mixing, bank)


def bank_energy(place, mixing, scale, ge, bank, group):
    samples, kernels = mixing.shape
    band = scale.shape[1]
    width = bank.shape[4]
    span = SUB * kernels
    bands = band // SUB
    chunk = min(samples, 32)
    chunks = samples // chunk
    kind = BF if chunks == 1 else F

    def body(place_ref, m_ref, s_ref, g_ref, b_ref, e_ref, se_ref, me_ref, rows, wides, diag):
        u, part = pl.program_id(0), pl.program_id(1)
        cut = pl.ds(pl.multiple_of(part * chunk, chunk), chunk)

        @pl.when((u == 0) & (part == 0))
        def _():
            rows[...] = split_dot(m_ref[...], tile_mask(band, kernels))
            wides[...] = split_dot(s_ref[...], widen_mask(band, kernels))

        lanes = pl.ds(pl.multiple_of(u * span, span), span)
        scaled = rows[cut, lanes] * wides[cut, lanes]
        mask = band_mask(kernels)[None]
        d = jnp.where(mask, scaled[:, None, :], 0.0).astype(BF).reshape(chunk * SUB, span)
        d_turned = d.T
        ge = 2.0 * g_ref[...]
        acc = None
        for t in range(9):
            b = b_ref[t // 3, t % 3].reshape(span, width)
            m = dot_nn(d, b)
            w = (m.reshape(chunk, SUB, width) * ge).reshape(chunk * SUB, width).astype(BF)
            e = dot_nn(d_turned, w).reshape(SUB, kernels, width)
            if chunks == 1:
                e_ref[t // 3, t % 3] = e.astype(kind)
            else:
                e_ref[t // 3, t % 3] = e + jnp.where(part == 0, 0.0, e_ref[t // 3, t % 3])
            p = dot_nt(w, b)
            acc = p if acc is None else acc + p
        kept = jnp.where(mask, acc.reshape(chunk, SUB, span), 0.0)
        diag[cut, lanes] = jnp.sum(kept, axis=1)

        @pl.when((u == bands - 1) & (part == chunks - 1))
        def _():
            exact = dict(precision=lax.Precision.HIGHEST, preferred_element_type=F)
            over = (((1,), (1,)), ((), ()))
            se = lax.dot_general(diag[...] * rows[...], widen_mask(band, kernels).astype(F), over, **exact)
            me = lax.dot_general(diag[...] * wides[...], tile_mask(band, kernels).astype(F), over, **exact)
            for s in range(samples):
                to = pl.ds(s // group * group + lax.bitwise_xor(place_ref[0], s % group), 1)
                se_ref[to] = se[s : s + 1]
                me_ref[to] = me[s : s + 1]

    return pl.pallas_call(
        body,
        grid_spec=pltpu.PrefetchScalarGridSpec(
            num_scalar_prefetch=1,
            grid=(bands, chunks),
            in_specs=[
                pl.BlockSpec((samples, kernels), lambda i, c, s: (0, 0)),
                pl.BlockSpec((samples, band), lambda i, c, s: (0, 0)),
                pl.BlockSpec((chunk, 1, width), lambda i, c, s: (c, 0, 0)),
                pl.BlockSpec(
                    (3, 3, SUB, kernels, width), lambda i, c, s: (0, 0, s[1] * bands + i, 0, 0)
                ),
            ],
            out_specs=[
                pl.BlockSpec((3, 3, SUB, kernels, width), lambda i, c, s: (0, 0, i, 0, 0)),
                pl.BlockSpec((samples, band), lambda i, c, s: (0, 0)),
                pl.BlockSpec((samples, kernels), lambda i, c, s: (0, 0)),
            ],
            scratch_shapes=[
                pltpu.VMEM((samples, band * kernels), F),
                pltpu.VMEM((samples, band * kernels), F),
                pltpu.VMEM((samples, band * kernels), F),
            ],
        ),
        out_shape=[
            jax.ShapeDtypeStruct((3, 3, band, kernels, width), kind),
            jax.ShapeDtypeStruct((samples, band), F),
            jax.ShapeDtypeStruct((samples, kernels), F),
        ],
        compiler_params=params(),
        cost_estimate=pl.CostEstimate(
            flops=54 * bands * samples * SUB * span * width,
            bytes_accessed=36 * bands * span * width,
            transcendentals=0,
        ),
        name="bank_energy",
    )(place, mixing, scale, ge, bank)


def line_sums(g, tap, axis):
    if tap == 0:
        return g[1] + move_down(g[0], axis)
    if tap == 1:
        return g[0] + g[1]
    return g[0] + move_up(g[1], axis)


def bank_main(tap_row, before, sources, scale, at, taps, energy, side):
    blocks = len(taps)
    groups, points, width = taps[0].shape
    low = side * side
    held = blocks * groups * low
    band, kernels = energy.shape[2], energy.shape[3]

    def body(src_ref, scale_ref, a_ref, *rest):
        g_refs = rest[:blocks]
        e_ref = rest[blocks]
        o_ref, lines, sums = rest[-3:]
        tx = pl.program_id(0)

        @pl.when(tx == 0)
        def _():
            for b in range(blocks):
                for s in range(groups):
                    g = g_refs[b][s].astype(F).reshape(2, 2, side, side, width)
                    at_row = pl.multiple_of((src_ref[b] * groups + s) * low, low)
                    for px in range(2):
                        v = line_sums((g[0, px], g[1, px]), tap_row, 0)
                        lines[px, pl.ds(at_row, low)] = v.reshape(low, width)

        for tap in range(3):

            @pl.when(tx == tap)
            def _():
                for b in range(blocks * groups):
                    cut = slice(b * low, (b + 1) * low)
                    pair = [lines[px, cut].reshape(side, side, width) for px in range(2)]
                    sums[cut] = line_sums(pair, tap, 1).reshape(low, width).astype(BF)

        p = dot_nn(a_ref[...], sums[...]).reshape(band, kernels, width)
        o_ref[0, 0] = (p + e_ref[0, 0].astype(F)) * scale_ref[0]

    whole = [] if before is None else [before]
    tap_block = pl.BlockSpec((1, 1, band, kernels, width), lambda t: (tap_row, t, 0, 0, 0))
    return pl.pallas_call(
        body,
        grid=(3,),
        in_specs=[smem(), smem(), pl.BlockSpec((band * kernels, held), lambda t: (0, 0))]
        + [pl.BlockSpec((groups, points, width), lambda t: (0, 0, 0))] * blocks
        + [tap_block]
        + [pl.BlockSpec(memory_space=pl.ANY)] * len(whole),
        out_specs=tap_block,
        out_shape=jax.ShapeDtypeStruct((3, 3, band, kernels, width), F),
        input_output_aliases={4 + blocks: 0} if whole else {},
        scratch_shapes=[pltpu.VMEM((2, held, width), F), pltpu.VMEM((held, width), BF)],
        compiler_params=params(),
        cost_estimate=pl.CostEstimate(
            flops=6 * band * kernels * held * width,
            bytes_accessed=6 * held * width + 18 * band * kernels * width,
            transcendentals=0,
        ),
        name="bank_main",
    )(sources, scale, at, *taps, energy, *whole)


def tap_sums(grads, demod, raw, side):
    groups = len(grads)
    _, points, width = raw.shape
    low = side * side

    def body(d_ref, r_ref, *rest):
        g_refs = rest[:groups]
        taps_ref, sums_ref, en_ref = rest[groups:]
        for s in range(groups):
            part = g_refs[s][:points].astype(F)
            demod = d_ref[s]
            grad_demod = jnp.sum(part * r_ref[s].astype(F), axis=0, keepdims=True)
            en_ref[s] = -0.5 * grad_demod * demod * demod * demod
            taps_ref[s] = (part * demod).astype(BF)
            g = taps_ref[s].astype(F).reshape(2, 2, side, side, width)
            for ty in range(3):
                lines = [line_sums((g[0, px], g[1, px]), ty, 0) for px in range(2)]
                for tx in range(3):
                    v = line_sums(lines, tx, 1).reshape(low, width).astype(BF)
                    sums_ref[3 * ty + tx, s * low : (s + 1) * low] = v

    return pl.pallas_call(
        body,
        out_shape=[
            jax.ShapeDtypeStruct((groups, points, width), BF),
            jax.ShapeDtypeStruct((9, groups * low, width), BF),
            jax.ShapeDtypeStruct((groups, 1, width), F),
        ],
        compiler_params=params(),
        name="tap_sums",
    )(demod, raw, *grads)


def rms(field, gain):
    inverse = lax.rsqrt(jnp.mean(field * field, axis=-1, keepdims=True) + EPS)
    return field * inverse * gain, inverse


def rms_back(field, gain, grad_out):
    inverse = lax.rsqrt(jnp.mean(field * field, axis=-1, keepdims=True) + EPS)
    scaled = grad_out * gain
    grad_gain = jnp.sum(grad_out * field * inverse, axis=0, keepdims=True)
    mean = jnp.mean(scaled * field, axis=-1, keepdims=True)
    return inverse * scaled - field * inverse**3 * mean, grad_gain


def sigmoid(v):
    return 1.0 / (1.0 + jnp.exp(-v))


def silu_slope(v):
    q = sigmoid(v)
    return q * (1.0 + v * (1.0 - q))


def self_prob(q, k):
    kf = k.astype(F)
    square = jnp.sum(kf * kf, axis=1, keepdims=True)
    scores = (2.0 * dot_nt(k, q) - square) * (1.0 / math.sqrt(HD))
    e = jnp.exp(scores - jnp.max(scores, axis=0, keepdims=True))
    return e * (1.0 / jnp.sum(e, axis=0, keepdims=True))


def cross_prob(q, k):
    scores = dot_nt(k, q) * (1.0 / math.sqrt(HD))
    e = jnp.exp(scores - jnp.max(scores, axis=0, keepdims=True))
    return e * (1.0 / jnp.sum(e, axis=0, keepdims=True))


def side_slot(own_ref, send_ref, j, start, width):
    at = start + j // 2 * width
    return (send_ref if j % 2 else own_ref), slice(at, at + width)


def smem():
    return pl.BlockSpec(memory_space=pltpu.SMEM)


def vmem(count):
    return [pl.BlockSpec(memory_space=pltpu.VMEM)] * count


def attn_forward(place, conv_parts, noise, gains, wqkv, wo):
    n = len(wo)
    points, width = conv_parts[0].shape
    share, channels = wo[0].shape

    def body(place_ref, noise_ref, gains_ref, *rest):
        part_r, wqkv_r, wo_r = (rest[i * n : (i + 1) * n] for i in range(3))
        conv_ref, two_ref, qkv_ref, own_ref, send_ref = rest[3 * n :]
        here = place_ref[0]
        for j in range(n):
            start = pl.multiple_of(lax.bitwise_xor(here, j) * width, width)
            conv_ref[:, pl.ds(start, width)] = part_r[j][...]
        out = conv_ref[...].astype(F) + gains_ref[0:1] * noise_ref[...] + gains_ref[1:2]
        one = out * sigmoid(out)
        normed = rms(one, gains_ref[2:3])[0].astype(BF)
        own_ref[:, :channels] = normed
        send_ref[:, :channels] = normed
        two_ref[...] = one
        for j in range(n):
            qkv_ref[j] = dot_nn(normed, wqkv_r[j][...]).astype(BF)
            heads = []
            for h in range(share // HD):
                q, k, v = (
                    qkv_ref[j, :, i * share + h * HD : i * share + (h + 1) * HD] for i in range(3)
                )
                heads.append(dot_tn(self_prob(q, k).astype(BF), v).astype(BF))
            side_ref, cut = side_slot(own_ref, send_ref, j, channels, share)
            side_ref[:, cut] = jnp.concatenate(heads, axis=1)
            two_ref[...] += dot_nn(side_ref[:, cut], wo_r[j][...])

    return pl.pallas_call(
        body,
        in_specs=[smem()] + vmem(2 + 3 * n),
        out_shape=[
            jax.ShapeDtypeStruct((points, channels), BF),
            jax.ShapeDtypeStruct((points, channels), F),
            jax.ShapeDtypeStruct((n, points, 3 * share), BF),
        ]
        + [jax.ShapeDtypeStruct((points, channels + n // 2 * share), BF)] * 2,
        compiler_params=params(),
        cost_estimate=pl.CostEstimate(
            flops=10 * points * channels * channels,
            bytes_accessed=16 * channels * channels,
            transcendentals=points * points * channels // HD,
        ),
        name="attn_forward",
    )(place, noise, gains, *conv_parts, *wqkv, *wo)


def cross_forward(two, gains, cq, co, ckv):
    points, channels = two.shape
    n = len(cq)
    share = cq[0].shape[1]

    def body(two_ref, gains_ref, *rest):
        cq_r, co_r, ckv_r = (rest[i * n : (i + 1) * n] for i in range(3))
        three_ref, mlp_ref, xq_ref, own_ref, send_ref = rest[3 * n :]
        normed = rms(two_ref[...], gains_ref[3:4])[0].astype(BF)
        own_ref[:, :channels] = normed
        send_ref[:, :channels] = normed
        three_ref[...] = two_ref[...]
        for j in range(n):
            xq_ref[j] = dot_nn(normed, cq_r[j][...]).astype(BF)
            heads = []
            for h in range(share // HD):
                q = xq_ref[j, :, h * HD : (h + 1) * HD]
                k = ckv_r[j][:, h * HD : (h + 1) * HD]
                v = ckv_r[j][:, share + h * HD : share + (h + 1) * HD]
                heads.append(dot_tn(cross_prob(q, k).astype(BF), v).astype(BF))
            side_ref, cut = side_slot(own_ref, send_ref, j, channels, share)
            side_ref[:, cut] = jnp.concatenate(heads, axis=1)
            three_ref[...] += dot_nn(side_ref[:, cut], co_r[j][...])
        mlp_ref[...] = rms(three_ref[...], gains_ref[4:5])[0].astype(BF)

    return pl.pallas_call(
        body,
        out_shape=[
            jax.ShapeDtypeStruct((points, channels), F),
            jax.ShapeDtypeStruct((points, channels), BF),
            jax.ShapeDtypeStruct((n, points, share), BF),
        ]
        + [jax.ShapeDtypeStruct((points, channels + n // 2 * share), BF)] * 2,
        compiler_params=params(),
        cost_estimate=pl.CostEstimate(
            flops=5 * points * channels * channels,
            bytes_accessed=8 * channels * channels,
            transcendentals=points * channels,
        ),
        name="cross_forward",
    )(two, gains, *cq, *co, *ckv)


def mlp_core(inputs, grad_out, up, down):
    count = len(inputs)
    points, channels = inputs[0].shape
    hidden = up.shape[1]
    tile = min(hidden, 256)
    steps = hidden // tile
    rows = count * points

    def body(*refs):
        x_r, g_r = refs[:count], refs[count : 2 * count]
        up_ref, down_ref, act_ref, gi_ref = refs[2 * count : 2 * count + 4]
        back_r = refs[2 * count + 4 : 3 * count + 4]
        x_all, g_all, acc = refs[3 * count + 4 :]
        step = pl.program_id(0)

        @pl.when(step == 0)
        def _():
            for j in range(count):
                x_all[j * points : (j + 1) * points] = x_r[j][...]
                g_all[j * points : (j + 1) * points] = g_r[j][...]
            acc[...] = jnp.zeros_like(acc)

        inner = dot_nn(x_all[...], up_ref[...])
        gate = sigmoid(inner)
        act_ref[...] = (inner * gate).astype(BF)
        grad_act = dot_nt(g_all[...], down_ref[...])
        gi_ref[...] = (grad_act * (gate * (1.0 + inner * (1.0 - gate)))).astype(BF)
        acc[...] += dot_nt(gi_ref[...], up_ref[...])

        @pl.when(step == steps - 1)
        def _():
            for j in range(count):
                back_r[j][...] = acc[j * points : (j + 1) * points].astype(BF)

    block = pl.BlockSpec((points, channels), lambda i: (0, 0))
    return pl.pallas_call(
        body,
        grid=(steps,),
        in_specs=[block] * (2 * count)
        + [
            pl.BlockSpec((channels, tile), lambda i: (0, i)),
            pl.BlockSpec((tile, channels), lambda i: (i, 0)),
        ],
        out_specs=[pl.BlockSpec((rows, tile), lambda i: (0, i))] * 2 + [block] * count,
        out_shape=[jax.ShapeDtypeStruct((rows, hidden), BF)] * 2
        + [jax.ShapeDtypeStruct((points, channels), BF)] * count,
        scratch_shapes=[
            pltpu.VMEM((rows, channels), BF),
            pltpu.VMEM((rows, channels), BF),
            pltpu.VMEM((rows, channels), F),
        ],
        compiler_params=params(),
        cost_estimate=pl.CostEstimate(
            flops=6 * rows * channels * hidden,
            bytes_accessed=4 * channels * hidden,
            transcendentals=rows * hidden,
        ),
        name="mlp_core",
    )(*inputs, *grad_out, up, down)


def mlp_rest(inputs, grad_out, grad_inner, acts, down):
    n = len(inputs)
    points, channels = inputs[0].shape
    hidden = acts[0].shape[1]
    tile = min(hidden, 256)
    groups = len(acts)
    each = n // groups

    def body(down_ref, *rest):
        x_r, go_r = rest[:n], rest[n : 2 * n]
        gi_r, act_r = rest[2 * n : 2 * n + groups], rest[2 * n + groups : 2 * n + 2 * groups]
        outs, dw_ref = rest[2 * n + 2 * groups : 3 * n + 2 * groups], rest[3 * n + 2 * groups]
        turned = rest[3 * n + 2 * groups + 1]
        for j in range(n):
            cut = slice(j % each * points, (j % each + 1) * points)
            outs[j][...] = dot_nn(act_r[j // each][cut], down_ref[...]).astype(BF)
        for side, refs, other in ((0, x_r, gi_r), (1, go_r, act_r)):
            for j in range(n):
                turned[:, j * points : (j + 1) * points] = refs[j][...].T
            for c in range(hidden // tile):
                cut = slice(c * tile, (c + 1) * tile)
                total = None
                for g in range(groups):
                    span = each * points
                    p = dot_nn(turned[:, g * span : (g + 1) * span], other[g][:, cut])
                    total = p if total is None else total + p
                at = side * hidden + c * tile
                dw_ref[:, at : at + tile] = total.astype(BF)

    return pl.pallas_call(
        body,
        out_shape=[jax.ShapeDtypeStruct((points, channels), BF)] * n
        + [jax.ShapeDtypeStruct((channels, 2 * hidden), BF)],
        scratch_shapes=[pltpu.VMEM((channels, n * points), BF)],
        compiler_params=params(),
        cost_estimate=pl.CostEstimate(
            flops=6 * n * points * channels * hidden,
            bytes_accessed=16 * channels * hidden,
            transcendentals=0,
        ),
        name="mlp_rest",
    )(down, *inputs, *grad_out, *grad_inner, *acts)


def cross_backward(grad_norm, grad_four, three, two, gains, xq, cq, co, ckv):
    points, channels = three.shape
    n, _, share = xq.shape
    tokens = ckv[0].shape[0]

    def body(gn_ref, g4_ref, three_ref, two_ref, in_ref, xq_ref, *rest):
        cq_r, co_r, ckv_r = (rest[i * n : (i + 1) * n] for i in range(3))
        two_out, gains_ref, own_ref, send_ref = rest[3 * n : 3 * n + 4]
        dkv_r = rest[3 * n + 4 : 4 * n + 4]
        back, gain = rms_back(three_ref[...], in_ref[4:5], gn_ref[...])
        gains_ref[0:1] = gain
        grad_three = g4_ref[...] + back
        gb = grad_three.astype(BF)
        own_ref[:, :channels] = gb
        send_ref[:, :channels] = gb
        grad_norm2 = jnp.zeros((points, channels), F)
        for j in range(n):
            ga = dot_nt(gb, co_r[j][...]).astype(BF)
            kv = ckv_r[j][...]
            gq, gk, gv = [], [], []
            for h in range(share // HD):
                q = xq_ref[j, :, h * HD : (h + 1) * HD]
                k = kv[:, h * HD : (h + 1) * HD]
                v = kv[:, share + h * HD : share + (h + 1) * HD]
                g = ga[:, h * HD : (h + 1) * HD]
                p = cross_prob(q, k)
                gp = dot_nt(v, g)
                gs = p * (gp - jnp.sum(p * gp, axis=0, keepdims=True))
                raw = (gs * (1.0 / math.sqrt(HD))).astype(BF)
                gq.append(dot_tn(raw, k).astype(BF))
                gk.append(dot_nn(raw, q).astype(BF))
                gv.append(dot_nn(p.astype(BF), g).astype(BF))
            side_ref, cut = side_slot(own_ref, send_ref, j, 2 * channels, share)
            side_ref[:, cut] = jnp.concatenate(gq, axis=1)
            dkv_r[j][...] = jnp.concatenate(gk + gv, axis=1)
            grad_norm2 = grad_norm2 + dot_nt(side_ref[:, cut], cq_r[j][...])
        back, gain = rms_back(two_ref[...], in_ref[3:4], grad_norm2)
        gains_ref[1:2] = gain
        two_out[...] = grad_three + back
        gb = two_out[...].astype(BF)
        own_ref[:, channels : 2 * channels] = gb
        send_ref[:, channels : 2 * channels] = gb

    return pl.pallas_call(
        body,
        out_shape=[
            jax.ShapeDtypeStruct((points, channels), F),
            jax.ShapeDtypeStruct((2, channels), F),
        ]
        + [jax.ShapeDtypeStruct((points, 2 * channels + n // 2 * share), BF)] * 2
        + [jax.ShapeDtypeStruct((tokens, 2 * share), BF)] * n,
        compiler_params=params(),
        cost_estimate=pl.CostEstimate(
            flops=8 * points * channels * channels,
            bytes_accessed=12 * channels * channels,
            transcendentals=points * channels,
        ),
        name="cross_backward",
    )(grad_norm, grad_four, three, two, gains, xq, *cq, *co, *ckv)


def attn_backward(place, grad_two, conv, noise, gains, qkv, token_grads, wqkv, wo, width):
    points, channels = grad_two.shape
    n = len(wo)
    share = wo[0].shape[0]
    tokens = token_grads[0].shape[0]

    def body(place_ref, g2_ref, conv_ref, noise_ref, gains_ref, qkv_ref, *rest):
        wqkv_r, wo_r, token_r = (rest[i * n : (i + 1) * n] for i in range(3))
        sums_ref = rest[3 * n]
        share_r = rest[3 * n + 1 : 4 * n + 1]
        own_ref, send_ref, gc_ref = rest[4 * n + 1 :]
        here = place_ref[0]
        grad_two = g2_ref[...]
        gb = grad_two.astype(BF)
        out = conv_ref[...].astype(F) + gains_ref[0:1] * noise_ref[...] + gains_ref[1:2]
        one = out * sigmoid(out)
        grad_norm = jnp.zeros((points, channels), F)
        for j in range(n):
            ga = dot_nt(gb, wo_r[j][...]).astype(BF)
            gq, gk, gv = [], [], []
            for h in range(share // HD):
                q, k, v = (
                    qkv_ref[j, :, i * share + h * HD : i * share + (h + 1) * HD] for i in range(3)
                )
                g = ga[:, h * HD : (h + 1) * HD]
                p = self_prob(q, k)
                gp = dot_nt(v, g)
                gs = p * (gp - jnp.sum(p * gp, axis=0, keepdims=True))
                square = jnp.sum(gs, axis=1, keepdims=True) * (-1.0 / math.sqrt(HD))
                raw = (gs * (2.0 / math.sqrt(HD))).astype(BF)
                gq.append(dot_tn(raw, k).astype(BF))
                gk.append((dot_nn(raw, q) + 2.0 * k.astype(F) * square).astype(BF))
                gv.append(dot_nn(p.astype(BF), g).astype(BF))
            side_ref, cut = side_slot(own_ref, send_ref, j, 0, 3 * share)
            side_ref[:, cut] = jnp.concatenate(gq + gk + gv, axis=1)
            grad_norm = grad_norm + dot_nt(side_ref[:, cut], wqkv_r[j][...])
        back, gain = rms_back(one, gains_ref[2:3], grad_norm)
        grad_conv = (grad_two + back) * silu_slope(out)
        gc_ref[...] = grad_conv.astype(BF)
        for j in range(n):
            start = pl.multiple_of(lax.bitwise_xor(here, j) * width, width)
            share_r[j][:points] = gc_ref[:, pl.ds(start, width)]
            for i in range(2):
                rows = slice(points + i * tokens, points + (i + 1) * tokens)
                share_r[j][rows] = token_r[j][:, i * width : (i + 1) * width]
        sums_ref[0:1] = gain
        sums_ref[1:2] = jnp.sum(grad_conv, axis=0, keepdims=True)
        sums_ref[2:3] = jnp.sum(grad_conv * noise_ref[...], axis=0, keepdims=True)

    return pl.pallas_call(
        body,
        out_shape=[
            jax.ShapeDtypeStruct((3, channels), F),
        ]
        + [jax.ShapeDtypeStruct((points + 2 * tokens, width), BF)] * n
        + [jax.ShapeDtypeStruct((points, n // 2 * 3 * share), BF)] * 2,
        in_specs=[smem()] + vmem(5 + 3 * n),
        scratch_shapes=[pltpu.VMEM((points, channels), BF)],
        compiler_params=params(),
        cost_estimate=pl.CostEstimate(
            flops=24 * points * channels * channels,
            bytes_accessed=24 * channels * channels,
            transcendentals=points * points * channels // HD,
        ),
        name="attn_backward",
    )(place, grad_two, conv, noise, gains, qkv, *wqkv, *wo, *token_grads)


def turn(turned, blocks, start, channels):
    points = blocks[0].shape[0]
    for i, block in enumerate(blocks):
        turned[:, i * points : (i + 1) * points] = block[:, start : start + channels].T


def pair_product(turned, blocks, cut):
    points = blocks[0].shape[0]
    total = None
    for i, block in enumerate(blocks):
        p = dot_nn(turned[:, i * points : (i + 1) * points], block[:, cut])
        total = p if total is None else total + p
    return total.astype(BF)


def cross_weights(attn_pair, cross_pair, grad_pair, count, share):
    points = attn_pair[0].shape[0]
    channels = attn_pair[0].shape[1] - count * share

    def body(*refs):
        attn, cross, grad = refs[:2], refs[2:4], refs[4:6]
        both, out = refs[6 : 6 + count], refs[6 + count : 6 + 2 * count]
        turned = refs[-1]
        turn(turned, cross, 0, channels)
        for i in range(count):
            cut = slice(2 * channels + i * share, 2 * channels + (i + 1) * share)
            both[i][:, :share] = pair_product(turned, grad, cut)
        turn(turned, grad, 0, channels)
        for i in range(count):
            cut = slice(channels + i * share, channels + (i + 1) * share)
            both[i][:, share:] = pair_product(turned, cross, cut)
        turn(turned, grad, channels, channels)
        for i in range(count):
            cut = slice(channels + i * share, channels + (i + 1) * share)
            out[i][...] = pair_product(turned, attn, cut)

    return pl.pallas_call(
        body,
        out_shape=[jax.ShapeDtypeStruct((channels, 2 * share), BF)] * count
        + [jax.ShapeDtypeStruct((channels, share), BF)] * count,
        scratch_shapes=[pltpu.VMEM((channels, 2 * points), BF)],
        compiler_params=params(),
        cost_estimate=pl.CostEstimate(
            flops=12 * count * points * channels * share,
            bytes_accessed=20 * points * channels,
            transcendentals=0,
        ),
        name="cross_weights",
    )(*attn_pair, *cross_pair, *grad_pair)


def attn_weights(attn_pair, grad_pair, count, share):
    points = attn_pair[0].shape[0]
    channels = attn_pair[0].shape[1] - count * share

    def body(*refs):
        attn, grad = refs[:2], refs[2:4]
        out, turned = refs[4 : 4 + 3 * count], refs[-1]
        turn(turned, attn, 0, channels)
        for i in range(count):
            for k in range(3):
                cut = slice((3 * i + k) * share, (3 * i + k + 1) * share)
                out[k * count + i][...] = pair_product(turned, grad, cut)

    return pl.pallas_call(
        body,
        out_shape=[jax.ShapeDtypeStruct((channels, share), BF)] * (3 * count),
        scratch_shapes=[pltpu.VMEM((channels, 2 * points), BF)],
        compiler_params=params(),
        cost_estimate=pl.CostEstimate(
            flops=12 * count * points * channels * share,
            bytes_accessed=16 * points * channels,
            transcendentals=0,
        ),
        name="attn_weights",
    )(*attn_pair, *grad_pair)


def band_prepare(place, received, codes, select, style, points_low):
    n_dp, _, band = received.shape
    samples, depth = codes.shape
    kernels = select.shape[1]
    low = n_dp * points_low // samples
    columns = samples * low
    step = 8

    def body(place_ref, x_ref, c_ref, sel_ref, sty_ref, at_ref, mix_ref, scale_ref, turned):
        logits = dot_nn(c_ref[...], sel_ref[...])
        e = jnp.exp(logits - jnp.max(logits, axis=1, keepdims=True))
        mixing = e / jnp.sum(e, axis=1, keepdims=True)
        mix_ref[...] = mixing
        scale_ref[...] = dot_nn(c_ref[...], sty_ref[...]) + 1.0
        for b in range(n_dp):
            turned[:, b * points_low : (b + 1) * points_low] = x_ref[b, :points_low].astype(F).T
        row = lax.broadcasted_iota(jnp.int32, (samples, columns), 0)
        lane = lax.broadcasted_iota(jnp.int32, (samples, columns), 1)
        repeat = jnp.where(lane // low == row, 1.0, 0.0).astype(BF)
        high = mixing.astype(BF)
        rest = (mixing - high.astype(F)).astype(BF)
        wide = dot_tn(high, repeat) + dot_tn(rest, repeat)
        for i in range(band // step):
            x = turned[i * step : (i + 1) * step]
            a = (x[:, None, :] * wide[None]).reshape(step * kernels, columns)
            at_ref[i * step * kernels : (i + 1) * step * kernels] = a.astype(BF)

    return pl.pallas_call(
        body,
        in_specs=[smem()] + vmem(4),
        out_shape=[
            jax.ShapeDtypeStruct((band * kernels, columns), BF),
            jax.ShapeDtypeStruct((samples, kernels), F),
            jax.ShapeDtypeStruct((samples, band), F),
        ],
        scratch_shapes=[pltpu.VMEM((band, columns), F)],
        compiler_params=params(),
        name="band_prepare",
    )(place, received, codes, select, style)


def side_outputs(place, three, branch, image_grad, color_scale, colors, bias, context, shares, ck, cv, gains, late, count_sums, count_all, side):
    points, channels = three.shape
    n, parts = len(shares), len(branch)
    share = ck.shape[1]
    tokens = context.shape[0] // n
    low = side * side
    exact = dict(precision=lax.Precision.HIGHEST, preferred_element_type=F)

    def body(place_ref, three_ref, gi_ref, cs_ref, col_ref, bias_ref, ctx_ref, ck_ref, cv_ref, gains_ref, late_ref, *rest):
        branch_r, share_r = rest[:parts], rest[parts : parts + n]
        feat_ref, color_ref, dkv_ref, pack_ref, four_ref, keys, values = rest[parts + n :]
        here = place_ref[0]
        four = three_ref[...]
        for b in branch_r:
            four = four + b[...].astype(F)
        four_ref[...] = four
        row = lax.broadcasted_iota(jnp.int32, (points, points), 0)
        lane = lax.broadcasted_iota(jnp.int32, (points, points), 1)
        phase, spot = lane // low, lane % low
        line = 2 * (spot // side) + phase // 2
        target = 2 * side * line + 2 * (spot % side) + phase % 2
        order = jnp.where(row == target, 1.0, 0.0)
        moved = lax.dot_general(order, four, (((1,), (0,)), ((), ())), **exact)
        feat_ref[...] = moved.reshape(1, 2 * side, 2 * side, channels)
        scale, col = cs_ref[...], col_ref[...]
        tint = col * scale
        color_ref[...] = bias_ref[...] + lax.dot_general(
            tint, four_ref[...], (((1,), (1,)), ((), ())), **exact
        )
        gi = gi_ref[...]
        image = lax.dot_general(gi, four_ref[...], (((0,), (0,)), ((), ())), **exact)
        for j in range(n):
            cut = slice(j * tokens, (j + 1) * tokens)
            keys[cut] = share_r[j][points : points + tokens]
            values[cut] = share_r[j][points + tokens : points + 2 * tokens]
        turned = ctx_ref[...]
        dkv_ref[:, :share] = dot_tn(turned, keys[...]).astype(BF)
        dkv_ref[:, share:] = dot_tn(turned, values[...]).astype(BF)
        grad = dot_nt(keys[...], ck_ref[...]) + dot_nt(values[...], cv_ref[...])
        pack_ref[...] = jnp.zeros_like(pack_ref)
        total = None
        for j in range(n):
            part = grad[j * tokens : (j + 1) * tokens]
            total = part if total is None else total + part
            row = count_sums + 2 * n + lax.bitwise_xor(here, j)
            pack_ref[pl.ds(row, 1)] = jnp.sum(part, axis=0, keepdims=True)
        pack_ref[:tokens] = total
        pack_ref[tokens : tokens + 2] = gains_ref[...]
        pack_ref[tokens + 2 : tokens + 5] = image * scale
        lane = lax.broadcasted_iota(jnp.int32, (1, channels), 1)
        row = jnp.zeros((1, channels), F)
        for c in range(3):
            row = jnp.where(lane == c, jnp.sum(gi[:, c : c + 1]), row)
        pack_ref[tokens + 5 : tokens + 6] = row
        pack_ref[tokens + 6 : tokens + 9] = late_ref[...]
        pack_ref[pl.ds(count_sums + 3 * n + here, 1)] = jnp.sum(image * col, axis=0, keepdims=True)

    return pl.pallas_call(
        body,
        in_specs=[smem()] + vmem(10 + parts + n),
        out_shape=[
            jax.ShapeDtypeStruct((1, 2 * side, 2 * side, channels), F),
            jax.ShapeDtypeStruct((3, points), F),
            jax.ShapeDtypeStruct((channels, 2 * share), BF),
            jax.ShapeDtypeStruct((count_all, channels), F),
        ],
        scratch_shapes=[
            pltpu.VMEM((points, channels), F),
            pltpu.VMEM((n * tokens, share), BF),
            pltpu.VMEM((n * tokens, share), BF),
        ],
        compiler_params=params(),
        name="side_outputs",
    )(place, three, image_grad, color_scale, colors, bias, context, ck, cv, gains, late, *branch, *shares)


def late_sums_kernel(place, scale, pack, low_parts, images, own_scale, energy, mixing_sum, mixing, count_sums, at_sum):
    low, channels = images.shape
    parts = len(low_parts)
    n, kernels = mixing.shape
    rows = mixing_sum.shape[0]

    def body(place_ref, scale_ref, pack_ref, im_ref, own_ref, en_ref, ms_ref, mix_ref, *rest):
        low_r, (out_ref, grad_ref) = rest[:parts], rest[parts:]
        here = place_ref[0]
        total = low_r[0][...].astype(F)
        for v in low_r[1:]:
            total = total + v[...].astype(F)
        grad_ref[...] = total * (own_ref[...] * scale_ref[0])
        out_ref[...] = pack_ref[...]
        line = jnp.sum(total * im_ref[...].astype(F), axis=0, keepdims=True)
        out_ref[pl.ds(count_sums + here, 1)] = line
        out_ref[count_sums + n : count_sums + 2 * n] = en_ref[...]
        out_ref[at_sum : at_sum + rows] = ms_ref[...]
        wide = split_dot(mix_ref[...], tile_mask(channels // kernels, kernels))
        lane = lax.broadcasted_iota(jnp.int32, (n, channels), 1) // kernels
        row = lax.bitwise_xor(lax.broadcasted_iota(jnp.int32, (n, channels), 0), here)
        line = jnp.sum(jnp.where(lane == row, wide, 0.0), axis=0, keepdims=True)
        out_ref[count_sums + 4 * n : count_sums + 4 * n + 1] = line

    return pl.pallas_call(
        body,
        in_specs=[smem(), smem()] + vmem(6 + parts),
        out_shape=[
            jax.ShapeDtypeStruct(pack.shape, F),
            jax.ShapeDtypeStruct((low, channels), F),
        ],
        compiler_params=params(),
        name="late_sums",
    )(place, scale, pack, images, own_scale, energy, mixing_sum, mixing, *low_parts)


def style_final(scale, mixing_grad, scale_grad, rgb_grad, tokens, codes, labels, select, style, rgb, classes):
    samples, channels = scale_grad.shape
    depth, kernels = select.shape

    def body(s_ref, mg_ref, sg_ref, rg_ref, t_ref, c_ref, l_ref, sel_ref, sty_ref, rgb_ref, *outs):
        dsel_ref, dsty_ref, drgb_ref, dcodes_ref, table_ref = outs
        by = s_ref[0]
        codes = c_ref[...]
        logits = dot_nn(codes, sel_ref[...])
        e = jnp.exp(logits - jnp.max(logits, axis=1, keepdims=True))
        mixing = e / jnp.sum(e, axis=1, keepdims=True)
        mg = mg_ref[...] * by
        logit = (mixing * (mg - jnp.sum(mixing * mg, axis=1, keepdims=True))).astype(BF)
        sg = (sg_ref[...] * by).astype(BF)
        rg = (rg_ref[...] * by).astype(BF)
        dsel_ref[...] = dot_tn(codes, logit)
        dsty_ref[...] = dot_tn(codes, sg)
        drgb_ref[...] = dot_tn(codes, rg)
        dcodes_ref[...] = (
            dot_nt(logit, sel_ref[...]) + dot_nt(sg, sty_ref[...]) + dot_nt(rg, rgb_ref[...])
        )
        ids = lax.broadcasted_iota(jnp.int32, (samples, classes), 1)
        one_hot = jnp.where(ids == l_ref[...], 1.0, 0.0).astype(BF)
        t = t_ref[...] * by
        high = t.astype(BF)
        rest = (t - high.astype(F)).astype(BF)
        table_ref[...] = dot_tn(one_hot, high) + dot_tn(one_hot, rest)

    return pl.pallas_call(
        body,
        in_specs=[smem()] + vmem(9),
        out_shape=[
            jax.ShapeDtypeStruct((depth, kernels), F),
            jax.ShapeDtypeStruct((depth, channels), F),
            jax.ShapeDtypeStruct((depth, channels), F),
            jax.ShapeDtypeStruct((samples, depth), F),
            jax.ShapeDtypeStruct((classes, channels), F),
        ],
        compiler_params=params(),
        name="style_final",
    )(scale, mixing_grad, scale_grad, rgb_grad, tokens, codes, labels, select, style, rgb)


def local(
    images,
    styles,
    labels,
    noise_map,
    counts,
    cot_features,
    cot_image,
    kernel_bank,
    select_proj,
    style_proj,
    conv_bias,
    noise_gain,
    norm_attn,
    query_proj,
    key_proj,
    value_proj,
    out_proj,
    norm_cross,
    cross_query,
    cross_key,
    cross_value,
    cross_out,
    class_table,
    class_pos,
    norm_mlp,
    up_proj,
    down_proj,
    rgb_style,
    color_projection,
    color_bias,
):
    n, n_dp = lax.axis_size("rows"), lax.axis_size("dp")
    r, d = lax.axis_index("rows"), lax.axis_index("dp")
    side, channels = images.shape[1], images.shape[3]
    low = side * side
    points = 4 * low
    kernels, width = kernel_bank.shape[3], kernel_bank.shape[4]
    tokens = class_pos.shape[0]
    share = query_proj.shape[1]
    band = channels // n_dp
    samples = n * n_dp

    def by_phase(field):
        rest = field.shape[2:]
        split = field.reshape((side, 2, side, 2) + rest)
        order = (1, 3, 0, 2) + tuple(range(4, 4 + len(rest)))
        return split.transpose(order).reshape((points,) + rest)

    group_order = jnp.arange(n, dtype=jnp.int32) ^ r
    slots = jnp.arange(n_dp, dtype=jnp.int32)

    def tie_lists(*lists):
        flat = tie(*[v for part in lists for v in part])
        out = []
        for part in lists:
            out.append(list(flat[: len(part)]))
            flat = flat[len(part) :]
        return out

    def far_swaps(m):
        return [swap(m, "rows", j) for j in range(2, n, 2)]

    def near_swaps(blocks):
        return [swap(b, "rows", 1) for b in blocks]

    def whole(m, far_m, near_m):
        out = [None] * n
        out[::2] = [m] + far_m
        out[1::2] = near_m
        return out

    half = n // 2
    own_images = images[0].reshape(low, channels)
    codes = jnp.take(styles, jnp.arange(max(n, 8), dtype=jnp.int32) % n ^ r, axis=0)
    image_blocks = spread(own_images)
    qkv_proj = jnp.concatenate([query_proj, key_proj, value_proj], axis=1)
    image_blocks, (codes, qkv_proj) = tie_lists(image_blocks, [codes, qkv_proj])
    qkv_far = far_swaps(qkv_proj)
    near = [near_swaps([m])[0] for m in (qkv_proj, out_proj, cross_query, cross_out)]
    conv_part, conv_raw, demod, xs, mixing, scale_in = conv_forward(
        codes, select_proj, style_proj, image_blocks, kernel_bank, side
    )

    later = [styles, labels, counts, cot_features, cot_image, noise_map, conv_bias, noise_gain]
    later += [norm_attn, norm_cross, norm_mlp, class_table, class_pos, cross_key, cross_value]
    later += [rgb_style, color_projection, color_bias, out_proj, cross_query, cross_out, xs]
    (conv_part,), later, qkv_far, near = tie_lists([conv_part], later, qkv_far, near)
    styles, labels, counts, cot_features, cot_image, noise_map, conv_bias, noise_gain = later[:8]
    norm_attn, norm_cross, norm_mlp, class_table, class_pos, cross_key, cross_value = later[8:15]
    rgb_style, color_projection, color_bias, out_proj, cross_query, cross_out, xs = later[15:]

    parts = [conv_part[0]] + [swap(conv_part[j], "rows", j) for j in range(1, n)]
    qkv_near = near[:1] + near_swaps(qkv_far)
    wo_far = far_swaps(out_proj)
    own_live = lax.dynamic_index_in_dim(counts.astype(F), r, 0, keepdims=False)
    color_scale = jnp.dot(codes[:1], rgb_style, preferred_element_type=F) + 1.0
    grad_image = by_phase(cot_image[0].transpose(1, 2, 0)) * own_live
    colors = color_projection.astype(F)
    tinted = jnp.dot(grad_image, colors.T, precision=lax.Precision.HIGHEST)
    grad_four = by_phase(cot_features[0]).astype(F) * own_live + tinted * color_scale
    noise = by_phase(noise_map[0]).astype(F).reshape(points, 1)
    place = r.astype(jnp.int32).reshape(1)
    gains = jnp.stack([noise_gain, conv_bias, norm_attn, norm_cross, norm_mlp]).astype(F)
    parts, qkv_near, wo_far, rest = tie_lists(
        parts, qkv_near, wo_far, [grad_four, noise, gains, xs, styles, labels, class_table]
    )
    grad_four, noise, gains, xs, styles, labels, class_table = rest

    bands = xs.reshape(n * low, n_dp, band).transpose(1, 0, 2)
    label_rows = jnp.stack([labels // 256, labels % 256, counts]).astype(BF)
    codes_flat = jnp.concatenate([styles.reshape(-1), label_rows.reshape(-1)])
    codes_flat = jnp.pad(codes_flat, (0, -codes_flat.shape[0] % (16 * band))).reshape(-1, band)
    sent = jnp.concatenate(
        [bands, jnp.broadcast_to(codes_flat[None], (n_dp,) + codes_flat.shape)], axis=1
    )
    wo_near = near[1:2] + near_swaps(wo_far)
    wqkv = whole(qkv_proj, qkv_far, qkv_near)
    wo = whole(out_proj, wo_far, wo_near)
    conv, two, qkv, attn_own, attn_sent = attn_forward(place, parts, noise, gains, wqkv, wo)
    cq_far, co_far = far_swaps(cross_query), far_swaps(cross_out)
    (two, sent, labels, class_table), cq_far, co_far = tie_lists(
        [two, sent, labels, class_table], cq_far, co_far
    )

    class_rows = jnp.take(class_table, jnp.take(labels, group_order), axis=0)
    context = (class_rows.astype(F)[:, None, :] + class_pos.astype(F)[None]).astype(BF)
    flat_context = context.reshape(n * tokens, channels)
    ckv = jnp.dot(
        flat_context,
        jnp.concatenate([cross_key, cross_value], axis=1),
        preferred_element_type=F,
    ).astype(BF)
    ckv = ckv.reshape(n, tokens, 2 * share)
    ckv = [ckv[0]] + [swap(ckv[j], "rows", j) for j in range(1, n)]
    cq = whole(cross_query, cq_far, near[2:3] + near_swaps(cq_far))
    co = whole(cross_out, co_far, near[3:4] + near_swaps(co_far))
    received = lax.all_to_all(sent, "dp", 0, 0, tiled=True)
    grad_four_low = grad_four.astype(BF)
    three, normed_mlp, xq, cross_own, cross_sent = cross_forward(two, gains, cq, co, ckv)
    grad_far = far_swaps(grad_four_low)
    grad_near = near_swaps([grad_four_low])
    attn_near = near_swaps([attn_sent])
    (three, normed_mlp, received), grad_far, grad_near, attn_near = tie_lists(
        [three, normed_mlp, received], grad_far, grad_near, attn_near
    )

    normed_near = near_swaps([normed_mlp])
    grad_near += near_swaps(grad_far)
    (normed_mlp,), normed_near, grad_near = tie_lists([normed_mlp], normed_near, grad_near)
    grad_pairs = list(zip([grad_four_low] + grad_far, grad_near))
    normed_far = far_swaps(normed_mlp)
    mlp_in = [normed_mlp] + normed_near
    act, inner, *backward = mlp_core(mlp_in, grad_pairs[0], up_proj, down_proj)
    points_low = n * low
    depth = styles.shape[1]
    codes_back = received[:, points_low:].reshape(n_dp, -1)
    styles_all = codes_back[:, : n * depth].reshape(samples, depth)
    label_back = codes_back[:, n * depth : n * depth + 3 * n]
    label_back = label_back.reshape(n_dp, 3, n).astype(jnp.int32)
    inverse = (1.0 / jnp.sum(label_back[:, 2]).astype(F)).reshape(1)
    labels_all = (label_back[:, 0] * 256 + label_back[:, 1]).reshape(samples, 1)
    codes_all = jnp.take(styles_all.reshape(n_dp, n, depth), group_order, axis=1)
    band_proj = lax.dynamic_slice_in_dim(style_proj, d * band, band, axis=1)
    bands_ready = band_prepare(
        place, received, codes_all.reshape(samples, depth), select_proj, band_proj, points_low
    )
    cross_near = near_swaps([cross_sent])
    (act, inner), backward, normed_far, bands_ready, cross_near, ready = tie_lists(
        [act, inner],
        backward,
        normed_far,
        bands_ready,
        cross_near,
        [styles_all, labels_all, inverse],
    )
    at, mixing_all, scale_band = bands_ready
    styles_all, labels_all, inverse = ready
    acts, inners = [act], [inner]
    for i, block in enumerate(normed_far):
        pair = [block] + near_swaps([block])
        act, inner, *back = mlp_core(pair, grad_pairs[i + 1], up_proj, down_proj)
        acts.append(act)
        inners.append(inner)
        mlp_in += pair
        backward += back
    backward, acts, inners = tie_lists(near_sums(backward), acts, inners)
    grad_norm = far_sum(backward)
    grad_group = [g for p in grad_pairs for g in p]
    *forward, d_mlp = mlp_rest(mlp_in, grad_group, inners, acts, down_proj)
    (grad_norm, d_mlp), forward = tie_lists([grad_norm, d_mlp], forward)
    g_mlp = lax.psum_scatter(d_mlp, "dp", scatter_dimension=0, tiled=True)

    back = cross_backward(grad_norm, grad_four, three, two, gains, xq, cq, co, ckv)
    grad_two, d_gains, grads_own, grads_sent = back[:4]
    dkv = list(back[4:])
    forward_near = near_swaps(forward[1::2])
    (grad_two, grads_sent), forward_near = tie_lists([grad_two, grads_sent], forward_near)

    def pair_sums(blocks, near_blocks):
        return [
            (a.astype(F) + b.astype(F)).astype(BF) for a, b in zip(blocks[::2], near_blocks)
        ]

    def far_parts(sums):
        return sums[:1] + [swap(v, "rows", 2 * j) for j, v in enumerate(sums) if j]

    def add_all(blocks):
        total = blocks[0].astype(F)
        for v in blocks[1:]:
            total = total + v.astype(F)
        return total

    branch = far_parts(pair_sums(forward, forward_near))
    grads_near = near_swaps([grads_sent])
    back = attn_backward(place, grad_two, conv, noise, gains, qkv, dkv, wqkv, wo, width)
    late_sums, shares, (qkv_own, qkv_sent) = back[0], list(back[1 : 1 + n]), back[1 + n :]
    (late_sums, qkv_sent), shares, grads_near, branch = tie_lists(
        [late_sums, qkv_sent], shares, grads_near, branch
    )

    shares = [shares[0]] + [swap(shares[j], "rows", j) for j in range(1, n)]
    sent_near = near_swaps([qkv_sent])
    back = cross_weights(
        [attn_own] + attn_near, [cross_own] + cross_near, [grads_own] + grads_near, half, share
    )
    d_cross, d_out = list(back[:half]), list(back[half:])
    shares, d_cross, d_out, sent_near = tie_lists(shares, d_cross, d_out, sent_near)
    grad_taps, gs, grad_energy = tap_sums(shares, demod, conv_raw, side)

    rest, branch, d_cross, d_out, shares = tie_lists(
        [grad_taps, gs, grad_energy, late_sums, d_gains], branch, d_cross, d_out, shares
    )
    grad_taps, gs, grad_energy, late_sums, d_gains = rest
    lines = n_dp // 2
    ring = [grad_taps]
    flipped = []

    def ring_step(*work):
        flipped.append(lax.ppermute(ring[-1], "dp", ring_perm(n_dp, 0, 1)))
        if len(ring) < lines:
            ring.append(lax.ppermute(ring[-1], "dp", ring_perm(n_dp, 1, 0)))
        (ring[-1], flipped[-1]), *work = tie_lists([ring[-1], flipped[-1]], *work)
        return work

    ge_all = jnp.broadcast_to(grad_energy.reshape(1, n, width), (n_dp, n, width))
    ge_all = lax.all_to_all(ge_all, "dp", 0, 0, tiled=True).reshape(samples, 1, width)
    d_cross = far_parts(d_cross)
    back = attn_weights([attn_own] + attn_near, [qkv_own] + sent_near, half, share)
    d_query, d_key, d_value = (list(back[i * half : (i + 1) * half]) for i in range(3))
    (low_part, mixing_conv, ge_all), d_cross, d_query, d_key, d_value, d_out = ring_step(
        [*conv_back(gs, xs, mixing, kernel_bank, n), ge_all],
        d_cross,
        d_query,
        d_key,
        d_value,
        d_out,
    )

    d_out, d_query, d_key = far_parts(d_out), far_parts(d_query), far_parts(d_key)
    cross_side = scatter_side(add_all(d_cross).astype(BF))
    places = jnp.stack([r, d]).astype(jnp.int32)
    low_near = near_sums([low_part[j] for j in range(n)])
    done = bank_energy(places, mixing_all, scale_band, ge_all, kernel_bank, n)
    done, d_out, d_query, d_key, d_value, cross_side, low_near, (g_mlp,) = ring_step(
        list(done), d_out, d_query, d_key, d_value, cross_side, low_near, [g_mlp]
    )
    energy, scale_energy, mixing_energy = done

    count_sums = -(-(tokens + 9 + -(-samples * kernels // channels)) // 8) * 8
    count_all = -(-(count_sums + 4 * n + 1) // 8) * 8
    features, color_image, d_ck_cv, pack = side_outputs(
        place,
        three,
        branch,
        grad_image,
        color_scale,
        colors.T,
        color_bias.astype(F).reshape(3, 1),
        flat_context,
        shares,
        cross_key,
        cross_value,
        d_gains,
        late_sums,
        count_sums,
        count_all,
        side,
    )
    color_image = color_image.reshape(3, 2, 2, side, side).transpose(0, 3, 1, 4, 2)
    color_image = color_image.reshape(1, 3, 2 * side, 2 * side)
    low_parts = far_parts(low_near)

    def as_rows(v):
        v = v.reshape(1, -1)
        v = jnp.pad(v, ((0, 0), (0, -v.shape[1] % channels)))
        return v.reshape(-1, channels)

    pack, grad_images = late_sums_kernel(
        place,
        inverse,
        pack,
        low_parts,
        own_images,
        scale_in[:1],
        scale_energy.reshape(n, channels),
        as_rows(mixing_energy),
        mixing_conv,
        count_sums,
        tokens + 9,
    )
    (grad_images, pack), d_value, cross_side, d_out, d_query, d_key = ring_step(
        [grad_images, pack], d_value, cross_side, d_out, d_query, d_key
    )

    d_value = far_parts(d_value)
    pack = add_over(pack, "rows")
    while len(flipped) < lines:
        ((pack,),) = ring_step([pack])
    blocks = [None] * n_dp
    for t in range(lines):
        for e, v in enumerate((ring[t], flipped[t])):
            blocks[2 * t + e] = v

    sources = ring_source(n_dp, d, slots).astype(jnp.int32)
    cross_parts = scatter_lines(*cross_side)
    query_side = scatter_side(jnp.concatenate([add_all(d_out), add_all(d_query)], axis=1).astype(BF))
    sums, gathered = pack[:count_sums], pack[count_sums:]
    grad_bank = None
    delta = 1
    for tap_row in range(3):
        grad_bank = bank_main(tap_row, grad_bank, sources, inverse, at, blocks, energy, side)
        if delta < n_dp:
            sums, gathered = merge_step(sums, gathered, "dp", d, delta)
            delta *= 2
        if tap_row == 0:
            (grad_bank, sums, gathered), cross_parts, query_side = tie_lists(
                [grad_bank, sums, gathered], cross_parts, query_side
            )
            query_parts = scatter_lines(*query_side)
            keyval = [add_all(d_key), add_all(d_value), d_ck_cv.astype(F)]
            keyval_side = scatter_side(jnp.concatenate(keyval, axis=1).astype(BF))
        else:
            grad_bank, sums, gathered = tie(grad_bank, sums, gathered)
    while delta < n_dp:
        sums, gathered = merge_step(sums, gathered, "dp", d, delta)
        delta *= 2
    keyval_parts = scatter_lines(*keyval_side)
    gathered = gathered.reshape(n_dp, -1, channels)
    scale_grad, bands_grad, token_all, rgb_all = (
        gathered[:, i * n : (i + 1) * n].reshape(samples, channels) for i in range(4)
    )
    bands_grad = bands_grad.reshape(n_dp, samples, band).transpose(1, 0, 2)
    scale_grad = scale_grad + bands_grad.reshape(samples, channels)
    mixing_grad = gathered[:, 4 * n, : n * kernels].reshape(samples, kernels)
    mixing_sum = sums[tokens + 9 :].reshape(-1)[: samples * kernels]
    mixing_grad = mixing_grad + mixing_sum.reshape(samples, kernels)
    sums = sums[: tokens + 9] * inverse
    grad_images = grad_images.reshape(1, side, side, channels)

    d_select, d_style, d_rgb, d_codes, d_table = style_final(
        inverse,
        mixing_grad,
        scale_grad,
        rgb_all,
        token_all,
        styles_all,
        labels_all,
        select_proj,
        style_proj,
        rgb_style,
        class_table.shape[0],
    )
    styles_grad = lax.dynamic_slice_in_dim(d_codes, d * n, n, axis=0)

    cross_grads, query_grads, keyval_grads = tie(
        *(add_all(v) * inverse for v in (cross_parts, query_parts, keyval_parts))
    )
    g_mlp = g_mlp.astype(F) * inverse
    wide = up_proj.shape[1]

    def column(grads, i):
        return grads[:, i * share : (i + 1) * share]

    return (
        features,
        color_image,
        grad_images,
        styles_grad,
        grad_bank,
        d_select,
        d_style,
        sums[tokens + 7],
        sums[tokens + 8],
        sums[tokens + 6],
        column(query_grads, 1),
        column(keyval_grads, 0),
        column(keyval_grads, 1),
        column(query_grads, 0).T,
        sums[tokens + 1],
        column(cross_grads, 0),
        column(keyval_grads, 2),
        column(keyval_grads, 3),
        column(cross_grads, 1).T,
        d_table,
        sums[:tokens],
        sums[tokens],
        g_mlp[:, :wide],
        g_mlp[:, wide:].T,
        d_rgb,
        sums[tokens + 2 : tokens + 5].T,
        sums[tokens + 5, :3],
    )


def solution(mesh):
    whole = P()
    columns = P(None, "rows")
    lines = P("rows", None)
    both = P(("dp", "rows"), None, None, None)
    placed = (
        both,
        P("dp", None),
        P("dp"),
        P(("dp", "rows"), None, None),
        P("dp"),
        both,
        both,
        P(None, None, None, None, "rows"),
        whole,
        whole,
        whole,
        whole,
        whole,
        columns,
        columns,
        columns,
        lines,
        whole,
        columns,
        columns,
        columns,
        lines,
        whole,
        whole,
        whole,
        columns,
        lines,
        whole,
        whole,
        whole,
    )
    given = (
        both,
        both,
        both,
        P("dp", None),
        P(None, None, "dp", None, "rows"),
        whole,
        whole,
        whole,
        whole,
        whole,
        P("dp", "rows"),
        P("dp", "rows"),
        P("dp", "rows"),
        P("rows", "dp"),
        whole,
        P("dp", "rows"),
        P("dp", "rows"),
        P("dp", "rows"),
        P("rows", "dp"),
        whole,
        whole,
        whole,
        P("dp", "rows"),
        P("rows", "dp"),
        whole,
        whole,
        whole,
    )
    return jax.shard_map(local, mesh=mesh, in_specs=placed, out_specs=given, check_vma=False)
```

```python
import functools
import math

import jax
import jax.numpy as jnp
from jax import lax
from jax.experimental import pallas as pl
from jax.experimental.pallas import tpu as pltpu
from jax.sharding import PartitionSpec as P

HD = 64
SUB = 32
BF = jnp.bfloat16
F = jnp.float32
VMEM_LIMIT = 56 * 2**20
EPS = 1e-6


def dot_nn(a, b):
    return lax.dot_general(a, b, (((1,), (0,)), ((), ())), preferred_element_type=F)


def dot_nt(a, b):
    return lax.dot_general(a, b, (((1,), (1,)), ((), ())), preferred_element_type=F)


def dot_tn(a, b):
    return lax.dot_general(a, b, (((0,), (0,)), ((), ())), preferred_element_type=F)


def params():
    return pltpu.CompilerParams(vmem_limit_bytes=VMEM_LIMIT)


def swap(x, axis, delta):
    n = lax.axis_size(axis)
    return lax.ppermute(x, axis, [(i, i ^ delta) for i in range(n)])


def spread(x):
    n = lax.axis_size("rows")
    blocks = [None] * n
    blocks[0] = x
    for j in range(2, n, 2):
        blocks[j] = swap(x, "rows", j)
    for j in range(0, n, 2):
        blocks[j + 1] = swap(blocks[j], "rows", 1)
    return blocks


def near_sums(blocks):
    out = []
    for j in range(0, len(blocks), 2):
        near = blocks[j].astype(F) + swap(blocks[j + 1], "rows", 1).astype(F)
        out.append(near.astype(BF))
    return out


def far_sum(near):
    total = near[0].astype(F)
    for j in range(1, len(near)):
        total = total + swap(near[j], "rows", 2 * j).astype(F)
    return total


def collect(blocks):
    return far_sum(near_sums(blocks))


def double(x, axis, place):
    delta = 1
    while delta < lax.axis_size(axis):
        other = swap(x, axis, delta)
        high = (place & delta) != 0
        x = jnp.where(high, jnp.concatenate([other, x]), jnp.concatenate([x, other]))
        delta *= 2
    return x


def merge_step(sums, gathered, axis, place, delta):
    rows = sums.shape[0]
    other = swap(jnp.concatenate([sums, gathered]), axis, delta)
    high = (place & delta) != 0
    theirs = other[rows:]
    gathered = jnp.where(
        high, jnp.concatenate([theirs, gathered]), jnp.concatenate([gathered, theirs])
    )
    return sums + other[:rows], gathered


def add_over(sums, axis):
    delta = 1
    while delta < lax.axis_size(axis):
        sums = sums + swap(sums, axis, delta)
        delta *= 2
    return sums


def tree(parts):
    while len(parts) > 1:
        parts = [a + b for a, b in zip(parts[::2], parts[1::2])]
    return parts[0]


def everyone(x, axis):
    return [x] + [swap(x, axis, j) for j in range(1, lax.axis_size(axis))]


def in_order(blocks, place):
    stacked = jnp.stack(blocks)
    return jnp.take(stacked, jnp.arange(len(blocks), dtype=jnp.int32) ^ place, axis=0)


def ring_perm(n, step, flip):
    lines = n // 2
    return [(i, ((i // 2 + step) % lines) * 2 + ((i % 2) ^ flip)) for i in range(n)]


def ring_gather(x):
    n = lax.axis_size("dp")
    out = []
    held = x
    for step in range(n // 2):
        if step:
            held = lax.ppermute(held, "dp", ring_perm(n, 1, 0))
        out.append(held)
        out.append(lax.ppermute(held, "dp", ring_perm(n, 0, 1)))
    return out


def ring_source(n, place, slot):
    lines = n // 2
    return ((place // 2 - slot // 2) % lines) * 2 + ((place % 2) ^ (slot % 2))


def ring_target(n, place, slot):
    lines = n // 2
    return ((place // 2 + slot // 2) % lines) * 2 + ((place % 2) ^ (slot % 2))


def scatter(grads):
    return lax.psum_scatter(grads, "dp", scatter_dimension=0, tiled=True)


def scatter_side(grads):
    n = lax.axis_size("dp")
    side = lax.axis_index("dp") % 2
    bands = grads.reshape(n // 2, 2, grads.shape[0] // n, grads.shape[1])
    mine = lax.dynamic_index_in_dim(bands, side, 1, keepdims=False)
    theirs = lax.dynamic_index_in_dim(bands, 1 - side, 1, keepdims=False)
    return mine, lax.ppermute(theirs, "dp", ring_perm(n, 0, 1))


def scatter_lines(mine, theirs):
    n = lax.axis_size("dp")
    lines = n // 2
    line = lax.axis_index("dp") // 2
    half = (mine.astype(F) + theirs.astype(F)).astype(BF)
    pieces = [lax.dynamic_index_in_dim(half, line, 0, keepdims=False)]
    for step in range(1, lines):
        piece = lax.dynamic_index_in_dim(half, (line + step) % lines, 0, keepdims=False)
        pieces.append(lax.ppermute(piece, "dp", ring_perm(n, step, 0)))
    return pieces


def tie(*values):
    return lax.optimization_barrier(values)


def move_up(v, axis):
    shape = list(v.shape)
    shape[axis] = 1
    kept = lax.slice_in_dim(v, 0, v.shape[axis] - 1, axis=axis)
    return jnp.concatenate([jnp.zeros(shape, v.dtype), kept], axis=axis)


def move_down(v, axis):
    shape = list(v.shape)
    shape[axis] = 1
    kept = lax.slice_in_dim(v, 1, v.shape[axis], axis=axis)
    return jnp.concatenate([kept, jnp.zeros(shape, v.dtype)], axis=axis)


def band_mask(kernels):
    width = SUB * kernels
    row = lax.broadcasted_iota(jnp.int32, (SUB, width), 0)
    lane = lax.broadcasted_iota(jnp.int32, (SUB, width), 1)
    return (lane // kernels) == row


def split_dot(a, b):
    high = a.astype(BF)
    rest = (a - high.astype(F)).astype(BF)
    return dot_nn(high, b) + dot_nn(rest, b)


def widen_mask(block, kernels):
    row = lax.broadcasted_iota(jnp.int32, (block, block * kernels), 0)
    lane = lax.broadcasted_iota(jnp.int32, (block, block * kernels), 1)
    return jnp.where(lane // kernels == row, 1.0, 0.0).astype(BF)


def tile_mask(block, kernels):
    row = lax.broadcasted_iota(jnp.int32, (kernels, block * kernels), 0)
    lane = lax.broadcasted_iota(jnp.int32, (kernels, block * kernels), 1)
    return jnp.where(lane % kernels == row, 1.0, 0.0).astype(BF)


def conv_forward(codes, select, style, payload, images, bank, side):
    groups = len(images)
    low, channels = images[0].shape
    rows = groups * low
    kernels, width = bank.shape[3], bank.shape[4]
    pad, depth = codes.shape
    block = min(channels, 128)
    steps = channels // block
    parts = block // SUB
    span = SUB * kernels

    extra = payload.shape[0]

    def body(c_ref, sel_ref, sty_ref, pay_ref, *rest):
        x_refs = rest[:groups]
        b_ref, out_r = rest[groups], rest[groups + 1 : 2 * groups + 1]
        raw_ref, dem_ref, xs_ref, mix_ref, sc_ref = rest[2 * groups + 1 : 2 * groups + 6]
        acc, en, scale, mix_row, widen = rest[2 * groups + 6 :]
        step = pl.program_id(0)

        @pl.when(step == 0)
        def _():
            acc[...] = jnp.zeros_like(acc)
            en[...] = jnp.zeros_like(en)
            logits = dot_nt(c_ref[...], sel_ref[...])
            e = jnp.exp(logits - jnp.max(logits, axis=1, keepdims=True))
            mixing = e / jnp.sum(e, axis=1, keepdims=True)
            mix_ref[...] = mixing
            mix_row[...] = split_dot(mixing, tile_mask(block, kernels))
            scale[...] = dot_nn(c_ref[...], sty_ref[...]) + 1.0
            sc_ref[...] = scale[...]
            widen[...] = widen_mask(block, kernels)

        here = scale[:, pl.ds(pl.multiple_of(step * block, block), block)]
        wide_scale = split_dot(here, widen[...]) * mix_row[...]
        mask = band_mask(kernels)
        xs = []
        for s in range(groups):
            xs.append((x_refs[s][...].astype(F) * here[s : s + 1]).astype(BF))
            xs_ref[0, s * low : (s + 1) * low] = xs[s]
        xs_ref[0, rows:] = pay_ref[...]
        a = []
        for s in range(groups):
            a.append((dot_nn(xs[s], widen[...]) * mix_row[s : s + 1]).astype(BF))
        left = []
        for u in range(parts):
            cut = slice(u * span, (u + 1) * span)
            pieces = [v[:, cut] for v in a]
            for s in range(groups):
                pieces.append(jnp.where(mask, wide_scale[s : s + 1, cut], 0.0).astype(BF))
            left.append(jnp.concatenate(pieces))
        energy = en[...]
        for t in range(9):
            b = b_ref[t // 3, t % 3].reshape(block * kernels, width)
            total = acc[t]
            for u in range(parts):
                p = dot_nn(left[u], b[u * span : (u + 1) * span])
                total = total + p[:rows]
                m = p[rows:]
                energy = energy + jnp.sum((m * m).reshape(groups, SUB // 8, 8, width), axis=1)
            acc[t] = total
        en[...] = energy

        @pl.when(step == steps - 1)
        def _():
            demod = lax.rsqrt(jnp.sum(en[...], axis=1, keepdims=True) + 1e-8)
            dem_ref[...] = demod
            for s in range(groups):
                v = [acc[t, s * low : (s + 1) * low].reshape(side, side, width) for t in range(9)]
                for py in range(2):
                    h = []
                    for tx in range(3):
                        if py == 0:
                            h.append(move_up(v[tx], 0) + v[3 + tx] + v[6 + tx])
                        else:
                            h.append(v[tx] + v[3 + tx] + move_down(v[6 + tx], 0))
                    for px in range(2):
                        if px == 0:
                            o = move_up(h[0], 1) + h[1] + h[2]
                        else:
                            o = h[0] + h[1] + move_down(h[2], 1)
                        o = o.reshape(low, width)
                        q = (py * 2 + px) * low
                        raw_ref[s, q : q + low] = o.astype(raw_ref.dtype)
                        out_r[s][q : q + low] = (o * demod[s]).astype(BF)

    return pl.pallas_call(
        body,
        grid=(steps,),
        in_specs=[
            pl.BlockSpec((pad, depth), lambda i: (0, 0)),
            pl.BlockSpec((kernels, depth), lambda i: (0, 0)),
            pl.BlockSpec((depth, channels), lambda i: (0, 0)),
            pl.BlockSpec((extra, block), lambda i: (0, 0)),
        ]
        + [pl.BlockSpec((low, block), lambda i: (0, i))] * groups
        + [pl.BlockSpec((3, 3, block, kernels, width), lambda i: (0, 0, i, 0, 0))],
        out_specs=[pl.BlockSpec((4 * low, width), lambda i: (0, 0))] * groups
        + [
            pl.BlockSpec((groups, 4 * low, width), lambda i: (0, 0, 0)),
            pl.BlockSpec((groups, 1, width), lambda i: (0, 0, 0)),
            pl.BlockSpec((1, rows + extra, block), lambda i: (i, 0, 0)),
            pl.BlockSpec((pad, kernels), lambda i: (0, 0)),
            pl.BlockSpec((pad, channels), lambda i: (0, 0)),
        ],
        out_shape=[jax.ShapeDtypeStruct((4 * low, width), BF)] * groups
        + [
            jax.ShapeDtypeStruct((groups, 4 * low, width), BF),
            jax.ShapeDtypeStruct((groups, 1, width), F),
            jax.ShapeDtypeStruct((steps, rows + extra, block), BF),
            jax.ShapeDtypeStruct((pad, kernels), F),
            jax.ShapeDtypeStruct((pad, channels), F),
        ],
        scratch_shapes=[
            pltpu.VMEM((9, rows, width), F),
            pltpu.VMEM((groups, 8, width), F),
            pltpu.VMEM((pad, channels), F),
            pltpu.VMEM((pad, block * kernels), F),
            pltpu.VMEM((block, block * kernels), BF),
        ],
        compiler_params=params(),
        cost_estimate=pl.CostEstimate(
            flops=27 * rows * channels * kernels * width,
            bytes_accessed=18 * channels * kernels * width,
            transcendentals=0,
        ),
        name="conv_forward",
    )(codes, select, style, payload, *images, bank)


def conv_back(gs, xs, mixing, bank, groups, part, parts):
    _, rows, width = gs.shape
    blocks, held, block = xs.shape
    steps = blocks // parts
    first = part * steps
    channels, kernels = steps * block, bank.shape[3]
    pad = mixing.shape[0]
    low = rows // groups

    def body(g_ref, x_ref, m_ref, b_ref, low_ref, mix_ref, acc, mix_row, widen):
        step = pl.program_id(0)

        @pl.when(step == 0)
        def _():
            acc[...] = jnp.zeros_like(acc)
            mix_row[...] = split_dot(m_ref[...], tile_mask(block, kernels))
            widen[...] = widen_mask(block, kernels)

        total = None
        for t in range(9):
            p = dot_nt(g_ref[t], b_ref[t // 3, t % 3].reshape(block * kernels, width))
            total = p if total is None else total + p
        wide = dot_nn(x_ref[0, :rows], widen[...])
        acc[...] += jnp.sum((wide * total).reshape(groups, low // 8, 8, block * kernels), axis=1)
        for s in range(groups):
            cut = slice(s * low, (s + 1) * low)
            mixed = (total[cut] * mix_row[s : s + 1]).astype(BF)
            low_ref[s] = dot_nt(mixed, widen[...]).astype(BF)

        @pl.when(step == steps - 1)
        def _():
            sums = jnp.sum(acc[...], axis=1)
            mix_ref[...] = lax.dot_general(
                sums,
                tile_mask(block, kernels).astype(F),
                (((1,), (1,)), ((), ())),
                precision=lax.Precision.HIGHEST,
                preferred_element_type=F,
            )

    return pl.pallas_call(
        body,
        grid=(steps,),
        in_specs=[
            pl.BlockSpec((9, rows, width), lambda i: (0, 0, 0)),
            pl.BlockSpec((1, held, block), lambda i: (first + i, 0, 0)),
            pl.BlockSpec((pad, kernels), lambda i: (0, 0)),
            pl.BlockSpec((3, 3, block, kernels, width), lambda i: (0, 0, first + i, 0, 0)),
        ],
        out_specs=[
            pl.BlockSpec((groups, low, block), lambda i: (0, 0, i)),
            pl.BlockSpec((groups, kernels), lambda i: (0, 0)),
        ],
        out_shape=[
            jax.ShapeDtypeStruct((groups, low, channels), BF),
            jax.ShapeDtypeStruct((groups, kernels), F),
        ],
        scratch_shapes=[
            pltpu.VMEM((groups, 8, block * kernels), F),
            pltpu.VMEM((pad, block * kernels), F),
            pltpu.VMEM((block, block * kernels), BF),
        ],
        compiler_params=params(),
        cost_estimate=pl.CostEstimate(
            flops=18 * rows * channels * kernels * width,
            bytes_accessed=18 * channels * kernels * width,
            transcendentals=0,
        ),
        name="conv_back",
    )(gs, xs, mixing, bank)


def roll_kernels(v, shift):
    n = v.shape[-2]
    return pltpu.roll(v, shift % n, v.ndim - 2) if shift % n else v


def bank_pairs(place, bank, band):
    kernels, width = bank.shape[3], bank.shape[4]
    count = kernels // 2 + 1
    block = min(band, SUB)

    def body(place_ref, b_ref, q_ref):
        for c in range(block // 8):
            cut = slice(c * 8, (c + 1) * 8)
            total = [None] * count
            for t in range(9):
                b = b_ref[t // 3, t % 3, cut].astype(F)
                for r in range(count):
                    p = b * roll_kernels(b, -r)
                    total[r] = p if t == 0 else total[r] + p
            for r in range(count):
                q_ref[r, c * 8 * kernels : (c + 1) * 8 * kernels] = (
                    total[r].reshape(8 * kernels, width).astype(BF)
                )

    return pl.pallas_call(
        body,
        grid_spec=pltpu.PrefetchScalarGridSpec(
            num_scalar_prefetch=1,
            grid=(band // block,),
            in_specs=[
                pl.BlockSpec(
                    (3, 3, block, kernels, width),
                    lambda i, s: (0, 0, s[1] * (band // block) + i, 0, 0),
                )
            ],
            out_specs=pl.BlockSpec((count, block * kernels, width), lambda i, s: (0, i, 0)),
        ),
        out_shape=jax.ShapeDtypeStruct((count, band * kernels, width), BF),
        compiler_params=params(),
        cost_estimate=pl.CostEstimate(
            flops=20 * count * band * kernels * width,
            bytes_accessed=18 * band * kernels * width,
            transcendentals=0,
        ),
        name="bank_pairs",
    )(place, bank)


def energy_sums(place, mixing, scale, ge, pairs, group):
    samples, kernels = mixing.shape
    band = scale.shape[1]
    count = pairs.shape[0]
    exact = dict(precision=lax.Precision.HIGHEST, preferred_element_type=F)
    along = (((1,), (0,)), ((), ()))

    def fold(a, mask):
        high = a.astype(BF)
        rest = (a - high.astype(F)).astype(BF)
        return dot_nt(high, mask) + dot_nt(rest, mask)

    def body(place_ref, m_ref, s_ref, g_ref, q_ref, se_ref, me_ref):
        m = m_ref[...]
        wides = split_dot(s_ref[...], widen_mask(band, kernels))
        ge = (2.0 * g_ref[...]).astype(BF)
        row = lax.broadcasted_iota(jnp.int32, (kernels, kernels), 0)
        lane = lax.broadcasted_iota(jnp.int32, (kernels, kernels), 1)
        tile = tile_mask(band, kernels)
        square = wides * wides
        se, me = None, None
        for r in range(count):
            g = dot_nt(ge, q_ref[r])
            ahead = jnp.where(row == (lane + r) % kernels, 1.0, 0.0)
            behind = jnp.where(row == (lane + kernels - r) % kernels, 1.0, 0.0)
            next_m = lax.dot_general(m, ahead, along, **exact)
            both = split_dot(m * next_m, tile)
            weight = 1.0 if r == 0 or 2 * r == kernels else 2.0
            part = (weight * both) * g
            se = part if se is None else se + part
            h = fold(g * square, tile)
            part = next_m * h
            if weight == 2.0:
                part = part + lax.dot_general(m * h, behind, along, **exact)
            me = part if me is None else me + part
        se = fold(se * wides, widen_mask(band, kernels))
        for s in range(samples):
            to = pl.ds(s // group * group + lax.bitwise_xor(place_ref[0], s % group), 1)
            se_ref[to] = se[s : s + 1]
            me_ref[to] = me[s : s + 1]

    return pl.pallas_call(
        body,
        in_specs=[smem()] + vmem(4),
        out_shape=[
            jax.ShapeDtypeStruct((samples, band), F),
            jax.ShapeDtypeStruct((samples, kernels), F),
        ],
        compiler_params=params(),
        name="energy_sums",
    )(place, mixing, scale, ge, pairs)


def bank_energy(place, lefts, ge, bank):
    kernels, width = bank.shape[3], bank.shape[4]
    count, rows_all, samples = lefts.shape
    band = rows_all // kernels
    step = min(band, 16)

    def body(place_ref, l_ref, ge_ref, b_ref, o_ref, rights):
        @pl.when(pl.program_id(0) == 0)
        def _():
            ge = ge_ref[...].astype(BF)
            for r in range(count):
                rights[r] = dot_nn(l_ref[r], ge)

        for tx in range(3):
            for i in range(band // step):
                cut = slice(i * step * kernels, (i + 1) * step * kernels)
                b = b_ref[0, tx, i * step : (i + 1) * step].astype(F)
                e = rights[0, cut].reshape(step, kernels, width) * b
                for r in range(1, count):
                    right = rights[r, cut].reshape(step, kernels, width)
                    e = e + right * roll_kernels(b, -r)
                    if 2 * r != kernels:
                        e = e + roll_kernels(right * b, r)
                o_ref[0, tx, i * step : (i + 1) * step] = e.astype(BF)

    return pl.pallas_call(
        body,
        grid_spec=pltpu.PrefetchScalarGridSpec(
            num_scalar_prefetch=1,
            grid=(3,),
            in_specs=[
                pl.BlockSpec((count, band * kernels, samples), lambda t, s: (0, 0, 0)),
                pl.BlockSpec((samples, width), lambda t, s: (0, 0)),
                pl.BlockSpec((1, 3, band, kernels, width), lambda t, s: (t, 0, s[1], 0, 0)),
            ],
            out_specs=pl.BlockSpec((1, 3, band, kernels, width), lambda t, s: (t, 0, 0, 0, 0)),
            scratch_shapes=[pltpu.VMEM((count, band * kernels, width), F)],
        ),
        out_shape=jax.ShapeDtypeStruct((3, 3, band, kernels, width), BF),
        compiler_params=params(),
        cost_estimate=pl.CostEstimate(
            flops=400 * band * kernels * width,
            bytes_accessed=36 * band * kernels * width,
            transcendentals=0,
        ),
        name="bank_energy",
    )(place, lefts, ge, bank)


def line_sums(g, tap, axis):
    if tap == 0:
        return g[1] + move_down(g[0], axis)
    if tap == 1:
        return g[0] + g[1]
    return g[0] + move_up(g[1], axis)


def bank_main(sources, scale, at, taps, energy, side):
    blocks = len(taps)
    groups, points, width = taps[0].shape
    low = side * side
    held = blocks * groups * low
    band, kernels = energy.shape[2], energy.shape[3]

    def body(place_ref, scale_ref, a_ref, *rest):
        here = place_ref[1]
        g_refs = rest[:blocks]
        e_ref, o_ref, lines, sums = rest[blocks:]
        ty = pl.program_id(0)
        for tap in range(3):

            @pl.when(ty == tap)
            def _():
                for b in range(blocks):
                    for s in range(groups):
                        g = g_refs[b][s].astype(F).reshape(2, 2, side, side, width)
                        for px in range(2):
                            v = line_sums((g[0, px], g[1, px]), tap, 0)
                            line = lax.rem(here // 2 + blocks // 2 - b // 2, blocks // 2)
                            source = 2 * line + lax.bitwise_xor(lax.rem(here, 2), b % 2)
                            at_row = (source * groups + s) * low
                            at_row = pl.multiple_of(at_row, low)
                            lines[px, pl.ds(at_row, low)] = v.reshape(low, width)

        for tx in range(3):
            for b in range(blocks * groups):
                cut = slice(b * low, (b + 1) * low)
                pair = [lines[px, cut].reshape(side, side, width) for px in range(2)]
                sums[cut] = line_sums(pair, tx, 1).reshape(low, width).astype(BF)
            p = dot_nn(a_ref[...], sums[...]).reshape(band, kernels, width)
            o_ref[0, tx] = (p + e_ref[0, tx].astype(F)) * scale_ref[0]

    return pl.pallas_call(
        body,
        grid=(3,),
        in_specs=[smem(), smem(), pl.BlockSpec((band * kernels, held), lambda t: (0, 0))]
        + [pl.BlockSpec((groups, points, width), lambda t: (0, 0, 0))] * blocks
        + [pl.BlockSpec((1, 3, band, kernels, width), lambda t: (t, 0, 0, 0, 0))],
        out_specs=pl.BlockSpec((1, 3, band, kernels, width), lambda t: (t, 0, 0, 0, 0)),
        out_shape=jax.ShapeDtypeStruct((3, 3, band, kernels, width), F),
        scratch_shapes=[pltpu.VMEM((2, held, width), F), pltpu.VMEM((held, width), BF)],
        compiler_params=params(),
        cost_estimate=pl.CostEstimate(
            flops=18 * band * kernels * held * width,
            bytes_accessed=18 * held * width + 54 * band * kernels * width,
            transcendentals=0,
        ),
        name="bank_main",
    )(sources, scale, at, *taps, energy)


def tap_sums(grads, demod, raw, context, side, copies):
    groups = len(grads)
    _, points, width = raw.shape
    low = side * side

    channels = context.shape[1]
    tokens = context.shape[0] // groups

    def body(d_ref, r_ref, c_ref, *rest):
        g_refs = rest[:groups]
        taps_ref, sums_ref, en_ref, token_ref, keys, values = rest[groups:]
        for s in range(groups):
            cut = slice(s * tokens, (s + 1) * tokens)
            keys[cut] = g_refs[s][points : points + tokens]
            values[cut] = g_refs[s][points + tokens : points + 2 * tokens]
        token_ref[:, :width] = dot_tn(c_ref[...], keys[...]).astype(BF)
        token_ref[:, width:] = dot_tn(c_ref[...], values[...]).astype(BF)
        for s in range(groups):
            part = g_refs[s][:points].astype(F)
            demod = d_ref[s]
            grad_demod = jnp.sum(part * r_ref[s].astype(F), axis=0, keepdims=True)
            en = -0.5 * grad_demod * demod * demod * demod
            for i in range(copies):
                en_ref[i, s : s + 1] = en
            taps_ref[s] = (part * demod).astype(BF)
            g = taps_ref[s].astype(F).reshape(2, 2, side, side, width)
            for ty in range(3):
                lines = [line_sums((g[0, px], g[1, px]), ty, 0) for px in range(2)]
                for tx in range(3):
                    v = line_sums(lines, tx, 1).reshape(low, width).astype(BF)
                    sums_ref[3 * ty + tx, s * low : (s + 1) * low] = v

    return pl.pallas_call(
        body,
        out_shape=[
            jax.ShapeDtypeStruct((groups, points, width), BF),
            jax.ShapeDtypeStruct((9, groups * low, width), BF),
            jax.ShapeDtypeStruct((copies, groups, width), F),
            jax.ShapeDtypeStruct((channels, 2 * width), BF),
        ],
        scratch_shapes=[pltpu.VMEM((groups * tokens, width), BF)] * 2,
        compiler_params=params(),
        name="tap_sums",
    )(demod, raw, context, *grads)


def rms(field, gain):
    inverse = lax.rsqrt(jnp.mean(field * field, axis=-1, keepdims=True) + EPS)
    return field * inverse * gain, inverse


def rms_back(field, gain, grad_out):
    inverse = lax.rsqrt(jnp.mean(field * field, axis=-1, keepdims=True) + EPS)
    scaled = grad_out * gain
    grad_gain = jnp.sum(grad_out * field * inverse, axis=0, keepdims=True)
    mean = jnp.mean(scaled * field, axis=-1, keepdims=True)
    return inverse * scaled - field * inverse**3 * mean, grad_gain


def sigmoid(v):
    return 1.0 / (1.0 + jnp.exp(-v))


def silu_slope(v):
    q = sigmoid(v)
    return q * (1.0 + v * (1.0 - q))


def self_prob(q, k):
    kf = k.astype(F)
    square = jnp.sum(kf * kf, axis=1, keepdims=True)
    scores = (2.0 * dot_nt(k, q) - square) * (1.0 / math.sqrt(HD))
    e = jnp.exp(scores - jnp.max(scores, axis=0, keepdims=True))
    return e * (1.0 / jnp.sum(e, axis=0, keepdims=True))


def cross_prob(q, k):
    scores = dot_nt(k, q) * (1.0 / math.sqrt(HD))
    e = jnp.exp(scores - jnp.max(scores, axis=0, keepdims=True))
    return e * (1.0 / jnp.sum(e, axis=0, keepdims=True))


def side_slot(own_ref, send_ref, j, start, width):
    at = start + j // 2 * width
    return (send_ref if j % 2 else own_ref), slice(at, at + width)


def smem():
    return pl.BlockSpec(memory_space=pltpu.SMEM)


def vmem(count):
    return [pl.BlockSpec(memory_space=pltpu.VMEM)] * count


def attn_forward(place, conv_parts, noise, gains, wqkv, wo):
    n = len(wo)
    points, width = conv_parts[0].shape
    share, channels = wo[0].shape

    def body(place_ref, noise_ref, gains_ref, *rest):
        part_r, wqkv_r, wo_r = (rest[i * n : (i + 1) * n] for i in range(3))
        conv_ref, two_ref, qkv_ref, own_ref, send_ref = rest[3 * n :]
        here = place_ref[0]
        for j in range(n):
            start = pl.multiple_of(lax.bitwise_xor(here, j) * width, width)
            conv_ref[:, pl.ds(start, width)] = part_r[j][...]
        out = conv_ref[...].astype(F) + gains_ref[0:1] * noise_ref[...] + gains_ref[1:2]
        one = out * sigmoid(out)
        normed = rms(one, gains_ref[2:3])[0].astype(BF)
        own_ref[:, :channels] = normed
        send_ref[:, :channels] = normed
        two_ref[...] = one
        for j in range(n):
            qkv_ref[j] = dot_nn(normed, wqkv_r[j][...]).astype(BF)
            heads = []
            for h in range(share // HD):
                q, k, v = (
                    qkv_ref[j, :, i * share + h * HD : i * share + (h + 1) * HD] for i in range(3)
                )
                heads.append(dot_tn(v, self_prob(q, k).astype(BF)))
            side_ref, cut = side_slot(own_ref, send_ref, j, channels, share)
            side_ref[:, cut] = jnp.concatenate(heads).T.astype(BF)
            two_ref[...] += dot_nn(side_ref[:, cut], wo_r[j][...])

    return pl.pallas_call(
        body,
        in_specs=[smem()] + vmem(2 + 3 * n),
        out_shape=[
            jax.ShapeDtypeStruct((points, channels), BF),
            jax.ShapeDtypeStruct((points, channels), F),
            jax.ShapeDtypeStruct((n, points, 3 * share), BF),
        ]
        + [jax.ShapeDtypeStruct((points, channels + n // 2 * share), BF)] * 2,
        compiler_params=params(),
        cost_estimate=pl.CostEstimate(
            flops=10 * points * channels * channels,
            bytes_accessed=16 * channels * channels,
            transcendentals=points * points * channels // HD,
        ),
        name="attn_forward",
    )(place, noise, gains, *conv_parts, *wqkv, *wo)


def cross_forward(two, gains, cq, co, ckv):
    points, channels = two.shape
    n = len(cq)
    share = cq[0].shape[1]

    def body(two_ref, gains_ref, *rest):
        cq_r, co_r, ckv_r = (rest[i * n : (i + 1) * n] for i in range(3))
        three_ref, mlp_ref, xq_ref, own_ref, send_ref = rest[3 * n :]
        normed = rms(two_ref[...], gains_ref[3:4])[0].astype(BF)
        own_ref[:, :channels] = normed
        send_ref[:, :channels] = normed
        three_ref[...] = two_ref[...]
        for j in range(n):
            xq_ref[j] = dot_nn(normed, cq_r[j][...]).astype(BF)
            heads = []
            for h in range(share // HD):
                q = xq_ref[j, :, h * HD : (h + 1) * HD]
                k = ckv_r[j][:, h * HD : (h + 1) * HD]
                v = ckv_r[j][:, share + h * HD : share + (h + 1) * HD]
                heads.append(dot_tn(v, cross_prob(q, k).astype(BF)))
            side_ref, cut = side_slot(own_ref, send_ref, j, channels, share)
            side_ref[:, cut] = jnp.concatenate(heads).T.astype(BF)
            three_ref[...] += dot_nn(side_ref[:, cut], co_r[j][...])
        mlp_ref[...] = rms(three_ref[...], gains_ref[4:5])[0].astype(BF)

    return pl.pallas_call(
        body,
        out_shape=[
            jax.ShapeDtypeStruct((points, channels), F),
            jax.ShapeDtypeStruct((points, channels), BF),
            jax.ShapeDtypeStruct((n, points, share), BF),
        ]
        + [jax.ShapeDtypeStruct((points, channels + n // 2 * share), BF)] * 2,
        compiler_params=params(),
        cost_estimate=pl.CostEstimate(
            flops=5 * points * channels * channels,
            bytes_accessed=8 * channels * channels,
            transcendentals=points * channels,
        ),
        name="cross_forward",
    )(two, gains, *cq, *co, *ckv)


def mlp_core(inputs, grad_out, up, down):
    count = len(inputs)
    points, channels = inputs[0].shape
    hidden = up.shape[1]
    tile = min(hidden, 256)
    steps = hidden // tile
    rows = count * points

    def body(*refs):
        x_r, g_r = refs[:count], refs[count : 2 * count]
        up_ref, down_ref, act_ref, gi_ref = refs[2 * count : 2 * count + 4]
        back_r = refs[2 * count + 4 : 3 * count + 4]
        x_all, g_all, acc = refs[3 * count + 4 :]
        step = pl.program_id(0)

        @pl.when(step == 0)
        def _():
            for j in range(count):
                x_all[j * points : (j + 1) * points] = x_r[j][...]
                g_all[j * points : (j + 1) * points] = g_r[j][...]
            acc[...] = jnp.zeros_like(acc)

        inner = dot_nn(x_all[...], up_ref[...])
        gate = sigmoid(inner)
        act_ref[...] = (inner * gate).astype(BF)
        grad_act = dot_nt(g_all[...], down_ref[...])
        gi_ref[...] = (grad_act * (gate * (1.0 + inner * (1.0 - gate)))).astype(BF)
        acc[...] += dot_nt(gi_ref[...], up_ref[...])

        @pl.when(step == steps - 1)
        def _():
            for j in range(count):
                back_r[j][...] = acc[j * points : (j + 1) * points].astype(BF)

    block = pl.BlockSpec((points, channels), lambda i: (0, 0))
    return pl.pallas_call(
        body,
        grid=(steps,),
        in_specs=[block] * (2 * count)
        + [
            pl.BlockSpec((channels, tile), lambda i: (0, i)),
            pl.BlockSpec((tile, channels), lambda i: (i, 0)),
        ],
        out_specs=[pl.BlockSpec((rows, tile), lambda i: (0, i))] * 2 + [block] * count,
        out_shape=[jax.ShapeDtypeStruct((rows, hidden), BF)] * 2
        + [jax.ShapeDtypeStruct((points, channels), BF)] * count,
        scratch_shapes=[
            pltpu.VMEM((rows, channels), BF),
            pltpu.VMEM((rows, channels), BF),
            pltpu.VMEM((rows, channels), F),
        ],
        compiler_params=params(),
        cost_estimate=pl.CostEstimate(
            flops=6 * rows * channels * hidden,
            bytes_accessed=4 * channels * hidden,
            transcendentals=rows * hidden,
        ),
        name="mlp_core",
    )(*inputs, *grad_out, up, down)


def mlp_rest(inputs, grad_out, grad_inner, acts, down):
    n = len(inputs)
    points, channels = inputs[0].shape
    hidden = acts[0].shape[1]
    tile = min(hidden, 256)
    groups = len(acts)
    each = n // groups

    def body(down_ref, *rest):
        x_r, go_r = rest[:n], rest[n : 2 * n]
        gi_r, act_r = rest[2 * n : 2 * n + groups], rest[2 * n + groups : 2 * n + 2 * groups]
        outs, dw_ref = rest[2 * n + 2 * groups : 3 * n + 2 * groups], rest[3 * n + 2 * groups]
        turned = rest[3 * n + 2 * groups + 1]
        for j in range(n):
            cut = slice(j % each * points, (j % each + 1) * points)
            outs[j][...] = dot_nn(act_r[j // each][cut], down_ref[...]).astype(BF)
        for side, refs, other in ((0, x_r, gi_r), (1, go_r, act_r)):
            for j in range(n):
                turned[:, j * points : (j + 1) * points] = refs[j][...].T
            for c in range(hidden // tile):
                cut = slice(c * tile, (c + 1) * tile)
                total = None
                for g in range(groups):
                    span = each * points
                    p = dot_nn(turned[:, g * span : (g + 1) * span], other[g][:, cut])
                    total = p if total is None else total + p
                at = side * hidden + c * tile
                dw_ref[:, at : at + tile] = total.astype(BF)

    return pl.pallas_call(
        body,
        out_shape=[jax.ShapeDtypeStruct((points, channels), BF)] * n
        + [jax.ShapeDtypeStruct((channels, 2 * hidden), BF)],
        scratch_shapes=[pltpu.VMEM((channels, n * points), BF)],
        compiler_params=params(),
        cost_estimate=pl.CostEstimate(
            flops=6 * n * points * channels * hidden,
            bytes_accessed=16 * channels * hidden,
            transcendentals=0,
        ),
        name="mlp_rest",
    )(down, *inputs, *grad_out, *grad_inner, *acts)


def cross_backward(grad_norm, grad_four, three, two, gains, xq, cq, co, ckv):
    points, channels = three.shape
    n, _, share = xq.shape
    tokens = ckv[0].shape[0]

    def body(gn_ref, g4_ref, three_ref, two_ref, in_ref, xq_ref, *rest):
        cq_r, co_r, ckv_r = (rest[i * n : (i + 1) * n] for i in range(3))
        two_out, gains_ref, own_ref, send_ref = rest[3 * n : 3 * n + 4]
        dkv_r = rest[3 * n + 4 : 4 * n + 4]
        back, gain = rms_back(three_ref[...], in_ref[4:5], gn_ref[...])
        gains_ref[0:1] = gain
        grad_three = g4_ref[...] + back
        gb = grad_three.astype(BF)
        own_ref[:, :channels] = gb
        send_ref[:, :channels] = gb
        grad_norm2 = jnp.zeros((points, channels), F)
        for j in range(n):
            ga = dot_nt(gb, co_r[j][...]).astype(BF)
            kv = ckv_r[j][...]
            gq, gk, gv = [], [], []
            for h in range(share // HD):
                q = xq_ref[j, :, h * HD : (h + 1) * HD]
                k = kv[:, h * HD : (h + 1) * HD]
                v = kv[:, share + h * HD : share + (h + 1) * HD]
                g = ga[:, h * HD : (h + 1) * HD]
                p = cross_prob(q, k)
                gp = dot_nt(v, g)
                gs = p * (gp - jnp.sum(p * gp, axis=0, keepdims=True))
                raw = (gs * (1.0 / math.sqrt(HD))).astype(BF)
                gq.append(dot_tn(k, raw))
                gk.append(dot_nn(raw, q).astype(BF))
                gv.append(dot_nn(p.astype(BF), g).astype(BF))
            side_ref, cut = side_slot(own_ref, send_ref, j, 2 * channels, share)
            side_ref[:, cut] = jnp.concatenate(gq).T.astype(BF)
            dkv_r[j][...] = jnp.concatenate(gk + gv, axis=1)
            grad_norm2 = grad_norm2 + dot_nt(side_ref[:, cut], cq_r[j][...])
        back, gain = rms_back(two_ref[...], in_ref[3:4], grad_norm2)
        gains_ref[1:2] = gain
        two_out[...] = grad_three + back
        gb = two_out[...].astype(BF)
        own_ref[:, channels : 2 * channels] = gb
        send_ref[:, channels : 2 * channels] = gb

    return pl.pallas_call(
        body,
        out_shape=[
            jax.ShapeDtypeStruct((points, channels), F),
            jax.ShapeDtypeStruct((2, channels), F),
        ]
        + [jax.ShapeDtypeStruct((points, 2 * channels + n // 2 * share), BF)] * 2
        + [jax.ShapeDtypeStruct((tokens, 2 * share), BF)] * n,
        compiler_params=params(),
        cost_estimate=pl.CostEstimate(
            flops=8 * points * channels * channels,
            bytes_accessed=12 * channels * channels,
            transcendentals=points * channels,
        ),
        name="cross_backward",
    )(grad_norm, grad_four, three, two, gains, xq, *cq, *co, *ckv)


def attn_backward(place, grad_two, conv, noise, gains, qkv, token_grads, wqkv, wo, width):
    points, channels = grad_two.shape
    n = len(wo)
    share = wo[0].shape[0]
    tokens = token_grads[0].shape[0]

    def body(place_ref, g2_ref, conv_ref, noise_ref, gains_ref, qkv_ref, *rest):
        wqkv_r, wo_r, token_r = (rest[i * n : (i + 1) * n] for i in range(3))
        sums_ref = rest[3 * n]
        share_r = rest[3 * n + 1 : 4 * n + 1]
        own_ref, send_ref, gc_ref = rest[4 * n + 1 :]
        here = place_ref[0]
        grad_two = g2_ref[...]
        gb = grad_two.astype(BF)
        out = conv_ref[...].astype(F) + gains_ref[0:1] * noise_ref[...] + gains_ref[1:2]
        one = out * sigmoid(out)
        grad_norm = jnp.zeros((points, channels), F)
        for j in range(n):
            ga = dot_nt(gb, wo_r[j][...]).astype(BF)
            gq, gk, gv = [], [], []
            for h in range(share // HD):
                q, k, v = (
                    qkv_ref[j, :, i * share + h * HD : i * share + (h + 1) * HD] for i in range(3)
                )
                g = ga[:, h * HD : (h + 1) * HD]
                p = self_prob(q, k)
                gp = dot_nt(v, g)
                gs = p * (gp - jnp.sum(p * gp, axis=0, keepdims=True))
                square = jnp.sum(gs, axis=1, keepdims=True) * (-1.0 / math.sqrt(HD))
                raw = (gs * (2.0 / math.sqrt(HD))).astype(BF)
                gq.append(dot_tn(k, raw))
                gk.append((dot_nn(raw, q) + 2.0 * k.astype(F) * square).astype(BF))
                gv.append(dot_nn(p.astype(BF), g).astype(BF))
            side_ref, cut = side_slot(own_ref, send_ref, j, 0, 3 * share)
            gq = jnp.concatenate(gq).T.astype(BF)
            side_ref[:, cut] = jnp.concatenate([gq] + gk + gv, axis=1)
            grad_norm = grad_norm + dot_nt(side_ref[:, cut], wqkv_r[j][...])
        back, gain = rms_back(one, gains_ref[2:3], grad_norm)
        grad_conv = (grad_two + back) * silu_slope(out)
        gc_ref[...] = grad_conv.astype(BF)
        for j in range(n):
            start = pl.multiple_of(lax.bitwise_xor(here, j) * width, width)
            share_r[j][:points] = gc_ref[:, pl.ds(start, width)]
            for i in range(2):
                rows = slice(points + i * tokens, points + (i + 1) * tokens)
                share_r[j][rows] = token_r[j][:, i * width : (i + 1) * width]
        sums_ref[0:1] = gain
        sums_ref[1:2] = jnp.sum(grad_conv, axis=0, keepdims=True)
        sums_ref[2:3] = jnp.sum(grad_conv * noise_ref[...], axis=0, keepdims=True)

    return pl.pallas_call(
        body,
        out_shape=[
            jax.ShapeDtypeStruct((3, channels), F),
        ]
        + [jax.ShapeDtypeStruct((points + 2 * tokens, width), BF)] * n
        + [jax.ShapeDtypeStruct((points, n // 2 * 3 * share), BF)] * 2,
        in_specs=[smem()] + vmem(5 + 3 * n),
        scratch_shapes=[pltpu.VMEM((points, channels), BF)],
        compiler_params=params(),
        cost_estimate=pl.CostEstimate(
            flops=24 * points * channels * channels,
            bytes_accessed=24 * channels * channels,
            transcendentals=points * points * channels // HD,
        ),
        name="attn_backward",
    )(place, grad_two, conv, noise, gains, qkv, *wqkv, *wo, *token_grads)


def turn(turned, blocks, start, channels):
    points = blocks[0].shape[0]
    for i, block in enumerate(blocks):
        turned[:, i * points : (i + 1) * points] = block[:, start : start + channels].T


def pair_product(turned, blocks, cut):
    points = blocks[0].shape[0]
    total = None
    for i, block in enumerate(blocks):
        p = dot_nn(turned[:, i * points : (i + 1) * points], block[:, cut])
        total = p if total is None else total + p
    return total.astype(BF)


def cross_weights(attn_pair, cross_pair, grad_pair, count, share):
    points = attn_pair[0].shape[0]
    channels = attn_pair[0].shape[1] - count * share

    def body(*refs):
        attn, cross, grad = refs[:2], refs[2:4], refs[4:6]
        out, last = refs[6 : 6 + count], refs[6 + count : 6 + 2 * count]
        turned = refs[-1]
        turn(turned, cross, 0, channels)
        for i in range(count):
            cut = slice(2 * channels + i * share, 2 * channels + (i + 1) * share)
            out[i][:, :share] = pair_product(turned, grad, cut)
        turn(turned, grad, 0, channels)
        for i in range(count):
            cut = slice(channels + i * share, channels + (i + 1) * share)
            out[i][:, share:] = pair_product(turned, cross, cut)
        turn(turned, grad, channels, channels)
        for i in range(count):
            cut = slice(channels + i * share, channels + (i + 1) * share)
            last[i][...] = pair_product(turned, attn, cut)

    return pl.pallas_call(
        body,
        out_shape=[jax.ShapeDtypeStruct((channels, 2 * share), BF)] * count
        + [jax.ShapeDtypeStruct((channels, share), BF)] * count,
        scratch_shapes=[pltpu.VMEM((channels, 2 * points), BF)],
        compiler_params=params(),
        cost_estimate=pl.CostEstimate(
            flops=12 * count * points * channels * share,
            bytes_accessed=20 * points * channels,
            transcendentals=0,
        ),
        name="cross_weights",
    )(*attn_pair, *cross_pair, *grad_pair)


def attn_weights(attn_pair, grad_pair, count, share):
    points = attn_pair[0].shape[0]
    channels = attn_pair[0].shape[1] - count * share

    def body(*refs):
        attn, grad = refs[:2], refs[2:4]
        out, last, turned = refs[4 : 4 + count], refs[4 + count : 4 + 2 * count], refs[-1]
        turn(turned, attn, 0, channels)
        for i in range(count):
            at = 3 * i * share
            out[i][...] = pair_product(turned, grad, slice(at, at + 2 * share))
            last[i][...] = pair_product(turned, grad, slice(at + 2 * share, at + 3 * share))

    return pl.pallas_call(
        body,
        out_shape=[jax.ShapeDtypeStruct((channels, 2 * share), BF)] * count
        + [jax.ShapeDtypeStruct((channels, share), BF)] * count,
        scratch_shapes=[pltpu.VMEM((channels, 2 * points), BF)],
        compiler_params=params(),
        cost_estimate=pl.CostEstimate(
            flops=12 * count * points * channels * share,
            bytes_accessed=16 * points * channels,
            transcendentals=0,
        ),
        name="attn_weights",
    )(*attn_pair, *grad_pair)


def phase_order(points, side):
    row = lax.broadcasted_iota(jnp.int32, (points, points), 0)
    lane = lax.broadcasted_iota(jnp.int32, (points, points), 1)
    line, place = phase_place(row, side)
    return lane == 2 * side * line + place


def phase_place(row, side):
    phase, spot = row // (side * side), row % (side * side)
    return 2 * (spot // side) + phase // 2, 2 * (spot % side) + phase % 2


def phase_masks(side):
    shape = (4 * side * side, 2 * side)
    row = lax.broadcasted_iota(jnp.int32, shape, 0)
    lane = lax.broadcasted_iota(jnp.int32, shape, 1)
    line, place = phase_place(row, side)
    return jnp.where(lane == line, 1.0, 0.0), jnp.where(lane == place, 1.0, 0.0)


def cotangents(place, counts, features, image, noise, vectors, colors, code, rgb, side):
    points, channels = features.shape
    count = len(vectors)
    exact = dict(precision=lax.Precision.HIGHEST, preferred_element_type=F)
    along = (((1,), (0,)), ((), ()))

    def body(place_ref, live_ref, f_ref, im_ref, n_ref, col_ref, c_ref, rgb_ref, *rest):
        vec_r = rest[:count]
        four_ref, low_ref, gi_ref, no_ref, cs_ref, gains_ref = rest[count:]
        for i in range(count):
            gains_ref[i : i + 1] = vec_r[i][...].astype(F).reshape(1, channels)
        order = jnp.where(phase_order(points, side), 1.0, 0.0).astype(BF)
        by = live_ref[place_ref[0]].astype(F)
        lines, places = phase_masks(side)

        def column(v):
            rows = lax.dot_general(lines, v, along, **exact)
            return jnp.sum(rows * places, axis=1, keepdims=True)

        no_ref[...] = column(n_ref[0].astype(F))
        scale = dot_nn(c_ref[...], rgb_ref[...])[:1] + 1.0
        cs_ref[...] = scale
        four = dot_nn(order, f_ref[...]) * by
        col = col_ref[...].astype(F)
        for c in range(3):
            gi = column(im_ref[0, c]) * by
            gi_ref[:, c : c + 1] = gi
            four = four + gi * (col[c : c + 1] * scale)
        four_ref[...] = four
        low_ref[...] = four.astype(BF)

    return pl.pallas_call(
        body,
        in_specs=[smem(), smem()] + vmem(6 + count),
        out_shape=[
            jax.ShapeDtypeStruct((points, channels), F),
            jax.ShapeDtypeStruct((points, channels), BF),
            jax.ShapeDtypeStruct((points, 3), F),
            jax.ShapeDtypeStruct((points, 1), F),
            jax.ShapeDtypeStruct((1, channels), F),
            jax.ShapeDtypeStruct((count, channels), F),
        ],
        compiler_params=params(),
        name="cotangents",
    )(place, counts, features, image, noise, colors, code, rgb, *vectors)


def class_tokens(rows, pos, ck, cv):
    n = rows.shape[0]
    tokens, channels = pos.shape
    share = ck.shape[1]

    def body(r_ref, p_ref, ck_ref, cv_ref, ctx_ref, *out_r):
        pos = p_ref[...].astype(F)
        rows = r_ref[...].astype(F)
        for j in range(n):
            ctx_ref[j * tokens : (j + 1) * tokens] = (rows[j : j + 1] + pos).astype(BF)
        for w, at in ((ck_ref, 0), (cv_ref, share)):
            product = dot_nn(ctx_ref[...], w[...])
            for j in range(n):
                out_r[j][:, at : at + share] = product[j * tokens : (j + 1) * tokens].astype(BF)

    return pl.pallas_call(
        body,
        out_shape=[jax.ShapeDtypeStruct((n * tokens, channels), BF)]
        + [jax.ShapeDtypeStruct((tokens, 2 * share), BF)] * n,
        compiler_params=params(),
        name="class_tokens",
    )(rows, pos, ck, cv)


def band_prepare(place, received, codes, select, style, points_low):
    n_dp, _, band = received.shape
    samples, depth = codes.shape
    kernels = select.shape[0]
    low = n_dp * points_low // samples
    columns = samples * low
    step = 8

    def body(place_ref, x_ref, c_ref, sel_ref, sty_ref, at_ref, mix_ref, scale_ref, left_ref, turned):
        logits = dot_nt(c_ref[...], sel_ref[...])
        e = jnp.exp(logits - jnp.max(logits, axis=1, keepdims=True))
        mixing = e / jnp.sum(e, axis=1, keepdims=True)
        mix_ref[...] = mixing
        scale_ref[...] = dot_nn(c_ref[...], sty_ref[...]) + 1.0
        scale_turned = scale_ref[...].T
        mix_turned = mixing.T
        for r in range(kernels // 2 + 1):
            ahead = jnp.concatenate([mix_turned[r:], mix_turned[:r]]) if r else mix_turned
            both = 2.0 * mix_turned * ahead
            left = (scale_turned * scale_turned)[:, None, :] * both[None]
            left_ref[r] = left.reshape(band * kernels, samples).astype(BF)
        for b in range(n_dp):
            turned[:, b * points_low : (b + 1) * points_low] = x_ref[b, :points_low].astype(F).T
        row = lax.broadcasted_iota(jnp.int32, (samples, columns), 0)
        lane = lax.broadcasted_iota(jnp.int32, (samples, columns), 1)
        repeat = jnp.where(lane // low == row, 1.0, 0.0).astype(BF)
        high = mixing.astype(BF)
        rest = (mixing - high.astype(F)).astype(BF)
        wide = dot_tn(high, repeat) + dot_tn(rest, repeat)
        for i in range(band // step):
            x = turned[i * step : (i + 1) * step]
            a = (x[:, None, :] * wide[None]).reshape(step * kernels, columns)
            at_ref[i * step * kernels : (i + 1) * step * kernels] = a.astype(BF)

    return pl.pallas_call(
        body,
        in_specs=[smem()] + vmem(4),
        out_shape=[
            jax.ShapeDtypeStruct((band * kernels, columns), BF),
            jax.ShapeDtypeStruct((samples, kernels), F),
            jax.ShapeDtypeStruct((samples, band), F),
            jax.ShapeDtypeStruct((kernels // 2 + 1, band * kernels, samples), BF),
        ],
        scratch_shapes=[pltpu.VMEM((band, columns), F)],
        compiler_params=params(),
        name="band_prepare",
    )(place, received, codes, select, style)


def side_outputs(place, three, branch, image_grad, color_scale, colors, bias, tokens, shares, ck, cv, gains, late, count_sums, count_all, side):
    points, channels = three.shape
    n, parts = len(shares), len(branch)
    share = ck.shape[1]
    low = side * side
    exact = dict(precision=lax.Precision.HIGHEST, preferred_element_type=F)

    def body(place_ref, bias_ref, three_ref, gi_ref, cs_ref, col_ref, ck_ref, cv_ref, gains_ref, late_ref, *rest):
        branch_r, share_r = rest[:parts], rest[parts : parts + n]
        feat_ref, color_ref, pack_ref, four_ref, keys, values = rest[parts + n :]
        here = place_ref[0]
        four = three_ref[...]
        for b in branch_r:
            four = four + b[...].astype(F)
        four_ref[...] = four
        order = jnp.where(phase_order(points, side), 1.0, 0.0)
        moved = lax.dot_general(order, four, (((0,), (0,)), ((), ())), **exact)
        feat_ref[...] = moved.reshape(1, 2 * side, 2 * side, channels)
        scale, col = cs_ref[...], col_ref[...].astype(F)
        tint = col * scale
        color = lax.dot_general(four_ref[...], tint, (((1,), (1,)), ((), ())), **exact)
        lines, places = phase_masks(side)
        for c in range(3):
            spread_out = color[:, c : c + 1] * places
            color_ref[0, c] = bias_ref[c] + lax.dot_general(
                lines, spread_out, (((0,), (0,)), ((), ())), **exact
            )
        gi = gi_ref[...]
        image = lax.dot_general(gi, four_ref[...], (((0,), (0,)), ((), ())), **exact)
        for j in range(n):
            cut = slice(j * tokens, (j + 1) * tokens)
            keys[cut] = share_r[j][points : points + tokens]
            values[cut] = share_r[j][points + tokens : points + 2 * tokens]
        grad = dot_nt(keys[...], ck_ref[...]) + dot_nt(values[...], cv_ref[...])
        pack_ref[...] = jnp.zeros_like(pack_ref)
        total = None
        for j in range(n):
            part = grad[j * tokens : (j + 1) * tokens]
            total = part if total is None else total + part
            row = count_sums + 2 * n + lax.bitwise_xor(here, j)
            pack_ref[pl.ds(row, 1)] = jnp.sum(part, axis=0, keepdims=True)
        pack_ref[:tokens] = total
        pack_ref[tokens : tokens + 2] = gains_ref[...]
        pack_ref[tokens + 2 : tokens + 5] = image * scale
        lane = lax.broadcasted_iota(jnp.int32, (1, channels), 1)
        row = jnp.zeros((1, channels), F)
        for c in range(3):
            row = jnp.where(lane == c, jnp.sum(gi[:, c : c + 1]), row)
        pack_ref[tokens + 5 : tokens + 6] = row
        pack_ref[tokens + 6 : tokens + 9] = late_ref[...]
        pack_ref[pl.ds(count_sums + 3 * n + here, 1)] = jnp.sum(image * col, axis=0, keepdims=True)

    return pl.pallas_call(
        body,
        in_specs=[smem(), smem()] + vmem(8 + parts + n),
        out_shape=[
            jax.ShapeDtypeStruct((1, 2 * side, 2 * side, channels), F),
            jax.ShapeDtypeStruct((1, 3, 2 * side, 2 * side), F),
            jax.ShapeDtypeStruct((count_all, channels), F),
        ],
        scratch_shapes=[
            pltpu.VMEM((points, channels), F),
            pltpu.VMEM((n * tokens, share), BF),
            pltpu.VMEM((n * tokens, share), BF),
        ],
        compiler_params=params(),
        name="side_outputs",
    )(place, bias, three, image_grad, color_scale, colors, ck, cv, gains, late, *branch, *shares)


def late_sums_kernel(place, scale, pack, low_parts, images, own_scale, energy, mixing_sum, mixing, count_sums, at_sum):
    low, channels = images.shape
    parts = len(low_parts)
    n, kernels = mixing.shape
    rows = mixing_sum.shape[0]

    def body(place_ref, scale_ref, pack_ref, im_ref, own_ref, en_ref, ms_ref, mix_ref, *rest):
        low_r, (out_ref, grad_ref) = rest[:parts], rest[parts:]
        here = place_ref[0]
        total = low_r[0][...].astype(F)
        for v in low_r[1:]:
            total = total + v[...].astype(F)
        grad_ref[...] = total * (own_ref[0:1] * scale_ref[0])
        out_ref[...] = pack_ref[...]
        line = jnp.sum(total * im_ref[...].astype(F), axis=0, keepdims=True)
        out_ref[pl.ds(count_sums + here, 1)] = line
        out_ref[count_sums + n : count_sums + 2 * n] = en_ref[...]
        out_ref[at_sum : at_sum + rows] = ms_ref[...]
        wide = split_dot(mix_ref[...], tile_mask(channels // kernels, kernels))
        lane = lax.broadcasted_iota(jnp.int32, (n, channels), 1) // kernels
        row = lax.bitwise_xor(lax.broadcasted_iota(jnp.int32, (n, channels), 0), here)
        line = jnp.sum(jnp.where(lane == row, wide, 0.0), axis=0, keepdims=True)
        out_ref[count_sums + 4 * n : count_sums + 4 * n + 1] = line

    return pl.pallas_call(
        body,
        in_specs=[smem(), smem()] + vmem(6 + parts),
        out_shape=[
            jax.ShapeDtypeStruct(pack.shape, F),
            jax.ShapeDtypeStruct((low, channels), F),
        ],
        compiler_params=params(),
        name="late_sums",
    )(place, scale, pack, images, own_scale, energy, mixing_sum, mixing, *low_parts)


def style_final(places, scale, mixing_grad, scale_grad, rgb_grad, tokens, codes, labels, select, style, rgb, classes, group):
    samples, channels = scale_grad.shape
    kernels, depth = select.shape

    def body(place_ref, s_ref, mg_ref, sg_ref, rg_ref, t_ref, c_ref, l_ref, sel_ref, sty_ref, rgb_ref, *outs):
        dsel_ref, dsty_ref, drgb_ref, dcodes_ref, table_ref, held = outs
        by = s_ref[0]
        codes = c_ref[...]
        logits = dot_nt(codes, sel_ref[...])
        e = jnp.exp(logits - jnp.max(logits, axis=1, keepdims=True))
        mixing = e / jnp.sum(e, axis=1, keepdims=True)
        mg = mg_ref[...] * by
        logit = (mixing * (mg - jnp.sum(mixing * mg, axis=1, keepdims=True))).astype(BF)
        sg = (sg_ref[...] * by).astype(BF)
        rg = (rg_ref[...] * by).astype(BF)
        dsel_ref[...] = dot_tn(logit, codes)
        dsty_ref[...] = dot_tn(codes, sg)
        drgb_ref[...] = dot_tn(codes, rg)
        held[...] = (
            dot_nn(logit, sel_ref[...]) + dot_nt(sg, sty_ref[...]) + dot_nt(rg, rgb_ref[...])
        )
        for j in range(group):
            dcodes_ref[j : j + 1] = held[pl.ds(place_ref[1] * group + j, 1)]
        ids = lax.broadcasted_iota(jnp.int32, (samples, classes), 1)
        one_hot = jnp.where(ids == l_ref[...], 1.0, 0.0).astype(BF)
        t = t_ref[...] * by
        high = t.astype(BF)
        rest = (t - high.astype(F)).astype(BF)
        table_ref[...] = dot_tn(one_hot, high) + dot_tn(one_hot, rest)

    return pl.pallas_call(
        body,
        in_specs=[smem(), smem()] + vmem(9),
        out_shape=[
            jax.ShapeDtypeStruct((kernels, depth), F),
            jax.ShapeDtypeStruct((depth, channels), F),
            jax.ShapeDtypeStruct((depth, channels), F),
            jax.ShapeDtypeStruct((group, depth), F),
            jax.ShapeDtypeStruct((classes, channels), F),
        ],
        scratch_shapes=[pltpu.VMEM((samples, depth), F)],
        compiler_params=params(),
        name="style_final",
    )(places, scale, mixing_grad, scale_grad, rgb_grad, tokens, codes, labels, select, style, rgb)


def local(
    images,
    styles,
    labels,
    noise_map,
    counts,
    cot_features,
    cot_image,
    kernel_bank,
    select_proj,
    style_proj,
    conv_bias,
    noise_gain,
    norm_attn,
    query_proj,
    key_proj,
    value_proj,
    out_proj,
    norm_cross,
    cross_query,
    cross_key,
    cross_value,
    cross_out,
    class_table,
    class_pos,
    norm_mlp,
    up_proj,
    down_proj,
    rgb_style,
    color_projection,
    color_bias,
):
    n, n_dp = lax.axis_size("rows"), lax.axis_size("dp")
    r, d = lax.axis_index("rows"), lax.axis_index("dp")
    side, channels = images.shape[1], images.shape[3]
    low = side * side
    points = 4 * low
    kernels, width = kernel_bank.shape[3], kernel_bank.shape[4]
    tokens = class_pos.shape[0]
    share = query_proj.shape[1]
    band = channels // n_dp
    samples = n * n_dp

    def by_phase(field):
        rest = field.shape[2:]
        split = field.reshape((side, 2, side, 2) + rest)
        order = (1, 3, 0, 2) + tuple(range(4, 4 + len(rest)))
        return split.transpose(order).reshape((points,) + rest)

    group_order = jnp.arange(n, dtype=jnp.int32) ^ r
    slots = jnp.arange(n_dp, dtype=jnp.int32)

    def tie_lists(*lists):
        flat = tie(*[v for part in lists for v in part])
        out = []
        for part in lists:
            out.append(list(flat[: len(part)]))
            flat = flat[len(part) :]
        return out

    def far_swaps(m):
        return [swap(m, "rows", j) for j in range(2, n, 2)]

    def near_swaps(blocks):
        return [swap(b, "rows", 1) for b in blocks]

    def whole(m, far_m, near_m):
        out = [None] * n
        out[::2] = [m] + far_m
        out[1::2] = near_m
        return out

    half = n // 2
    own_images = images[0].reshape(low, channels)
    codes = jnp.take(styles, jnp.arange(max(n, 8), dtype=jnp.int32) % n ^ r, axis=0)
    image_blocks = spread(own_images)
    depth, points_low = styles.shape[1], n * low
    label_rows = jnp.stack([labels // 256, labels % 256, counts]).astype(BF)
    payload = jnp.concatenate([styles.reshape(-1), label_rows.reshape(-1)])
    block = min(channels, 128)
    payload = jnp.pad(payload, (0, -payload.shape[0] % (16 * block))).reshape(-1, block)
    qkv_proj = jnp.concatenate([query_proj, key_proj, value_proj], axis=1)
    image_blocks, (codes, qkv_proj) = tie_lists(image_blocks, [codes, qkv_proj])
    qkv_far = far_swaps(qkv_proj)
    near = [near_swaps([m])[0] for m in (qkv_proj, out_proj, cross_query, cross_out)]
    select_turned = select_proj.T
    *conv_part, conv_raw, demod, xs, mixing, scale_in = conv_forward(
        codes, select_turned, style_proj, payload, image_blocks, kernel_bank, side
    )

    places = jnp.stack([r, d]).astype(jnp.int32)
    conv_part[0], places = tie(conv_part[0], places)
    pairs = bank_pairs(places, kernel_bank, band)

    later = [styles, labels, counts, cot_features, cot_image, noise_map, conv_bias, noise_gain]
    later += [norm_attn, norm_cross, norm_mlp, class_table, class_pos, cross_key, cross_value]
    later += [rgb_style, color_projection, color_bias, out_proj, cross_query, cross_out, xs]
    conv_part, (pairs,), later, qkv_far, near = tie_lists(
        conv_part, [pairs], later, qkv_far, near
    )
    styles, labels, counts, cot_features, cot_image, noise_map, conv_bias, noise_gain = later[:8]
    norm_attn, norm_cross, norm_mlp, class_table, class_pos, cross_key, cross_value = later[8:15]
    rgb_style, color_projection, color_bias, out_proj, cross_query, cross_out, xs = later[15:]

    parts = [conv_part[0]] + [swap(conv_part[j], "rows", j) for j in range(1, n)]
    qkv_near = near[:1] + near_swaps(qkv_far)
    place = r.astype(jnp.int32).reshape(1)
    colors = color_projection.T
    grad_four, grad_four_low, grad_image, noise, color_scale, gains = cotangents(
        place,
        counts,
        cot_features.reshape(points, channels),
        cot_image,
        noise_map,
        (noise_gain, conv_bias, norm_attn, norm_cross, norm_mlp),
        colors,
        codes,
        rgb_style,
        side,
    )
    parts, qkv_near, rest = tie_lists(
        parts,
        qkv_near,
        [grad_four, grad_four_low, grad_image, color_scale, noise, gains]
        + [xs, labels, class_table, out_proj],
    )
    grad_four, grad_four_low, grad_image, color_scale, noise, gains = rest[:6]
    xs, labels, class_table, out_proj = rest[6:]
    wo_far = far_swaps(out_proj)

    if band == block:
        bands = xs
    else:
        split = xs[:, :points_low].reshape(xs.shape[0], points_low, block // band, band)
        split = split.transpose(0, 2, 1, 3).reshape(n_dp, points_low, band)
        rest = jnp.broadcast_to(payload.reshape(1, -1, band), (n_dp, payload.size // band, band))
        bands = jnp.concatenate([split, rest], axis=1)
    received = lax.all_to_all(bands, "dp", 0, 0, tiled=True)
    wo_near = near[1:2] + near_swaps(wo_far)
    wqkv = whole(qkv_proj, qkv_far, qkv_near)
    wo = whole(out_proj, wo_far, wo_near)
    conv, two, qkv, attn_own, attn_sent = attn_forward(place, parts, noise, gains, wqkv, wo)
    cq_far = far_swaps(cross_query)
    (two, received, labels, class_table), cq_far = tie_lists(
        [two, received, labels, class_table], cq_far
    )

    co_far = far_swaps(cross_out)
    flat_context, *ckv = class_tokens(
        jnp.take(class_table, jnp.take(labels, group_order), axis=0), class_pos, cross_key, cross_value
    )
    ckv = [ckv[0]] + [swap(ckv[j], "rows", j) for j in range(1, n)]
    cq = whole(cross_query, cq_far, near[2:3] + near_swaps(cq_far))
    codes_back = received[:, points_low:].reshape(n_dp, -1)
    styles_all = codes_back[:, : n * depth].reshape(samples, depth)
    label_back = codes_back[:, n * depth : n * depth + 3 * n]
    label_back = label_back.reshape(n_dp, 3, n).astype(jnp.int32)
    inverse = (1.0 / jnp.sum(label_back[:, 2]).astype(F)).reshape(1)
    labels_all = (label_back[:, 0] * 256 + label_back[:, 1]).reshape(samples, 1)
    codes_all = jnp.take(styles_all.reshape(n_dp, n, depth), group_order, axis=1)
    band_proj = lax.dynamic_slice_in_dim(style_proj, d * band, band, axis=1)
    bands_ready = band_prepare(
        place, received, codes_all.reshape(samples, depth), select_turned, band_proj, points_low
    )
    (two,), co_far, cq, ckv, bands_ready, ready = tie_lists(
        [two], co_far, cq, ckv, bands_ready, [styles_all, labels_all, inverse]
    )
    at, mixing_all, scale_band, lefts = bands_ready
    styles_all, labels_all, inverse = ready
    co = whole(cross_out, co_far, near[3:4] + near_swaps(co_far))
    three, normed_mlp, xq, cross_own, cross_sent = cross_forward(two, gains, cq, co, ckv)
    grad_far = far_swaps(grad_four_low)
    grad_near = near_swaps([grad_four_low])
    attn_near = near_swaps([attn_sent])
    (three, normed_mlp), grad_far, grad_near, attn_near = tie_lists(
        [three, normed_mlp], grad_far, grad_near, attn_near
    )

    normed_near = near_swaps([normed_mlp])
    grad_near += near_swaps(grad_far)
    (normed_mlp,), normed_near, grad_near = tie_lists([normed_mlp], normed_near, grad_near)
    grad_pairs = list(zip([grad_four_low] + grad_far, grad_near))
    normed_far = far_swaps(normed_mlp)
    mlp_in = [normed_mlp] + normed_near
    act, inner, *backward = mlp_core(mlp_in, grad_pairs[0], up_proj, down_proj)
    cross_near = near_swaps([cross_sent])
    (act, inner), backward, normed_far, cross_near = tie_lists(
        [act, inner], backward, normed_far, cross_near
    )
    acts, inners = [act], [inner]
    for i, block in enumerate(normed_far):
        pair = [block] + near_swaps([block])
        act, inner, *back = mlp_core(pair, grad_pairs[i + 1], up_proj, down_proj)
        acts.append(act)
        inners.append(inner)
        mlp_in += pair
        backward += back
    backward, acts, inners = tie_lists(near_sums(backward), acts, inners)
    grad_norm = far_sum(backward)
    grad_group = [g for p in grad_pairs for g in p]
    *forward, d_mlp = mlp_rest(mlp_in, grad_group, inners, acts, down_proj)
    (grad_norm, d_mlp), forward = tie_lists([grad_norm, d_mlp], forward)
    g_mlp = lax.psum_scatter(d_mlp, "dp", scatter_dimension=0, tiled=True)

    back = cross_backward(grad_norm, grad_four, three, two, gains, xq, cq, co, ckv)
    grad_two, d_gains, grads_own, grads_sent = back[:4]
    dkv = list(back[4:])
    forward_near = near_swaps(forward[1::2])
    (grad_two, grads_sent), forward_near = tie_lists([grad_two, grads_sent], forward_near)

    def pair_sums(blocks, near_blocks):
        return [
            (a.astype(F) + b.astype(F)).astype(BF) for a, b in zip(blocks[::2], near_blocks)
        ]

    def far_parts(sums):
        return sums[:1] + [swap(v, "rows", 2 * j) for j, v in enumerate(sums) if j]

    def add_all(blocks):
        total = blocks[0].astype(F)
        for v in blocks[1:]:
            total = total + v.astype(F)
        return total

    branch = far_parts(pair_sums(forward, forward_near))
    grads_near = near_swaps([grads_sent])
    back = attn_backward(place, grad_two, conv, noise, gains, qkv, dkv, wqkv, wo, width)
    late_sums, shares, (qkv_own, qkv_sent) = back[0], list(back[1 : 1 + n]), back[1 + n :]
    (late_sums, qkv_sent), shares, grads_near, branch = tie_lists(
        [late_sums, qkv_sent], shares, grads_near, branch
    )

    shares = [shares[0]] + [swap(shares[j], "rows", j) for j in range(1, n)]
    sent_near = near_swaps([qkv_sent])
    back = cross_weights(
        [attn_own] + attn_near, [cross_own] + cross_near, [grads_own] + grads_near, half, share
    )
    d_cross, d_out = list(back[:half]), list(back[half:])
    shares, d_cross, d_out, sent_near = tie_lists(shares, d_cross, d_out, sent_near)
    grad_taps, gs, grad_energy, d_tokens = tap_sums(
        shares, demod, conv_raw, flat_context, side, n_dp
    )

    rest, branch, d_cross, d_out, shares = tie_lists(
        [grad_taps, gs, grad_energy, d_tokens, late_sums, d_gains],
        branch,
        d_cross,
        d_out,
        shares,
    )
    grad_taps, gs, grad_energy, d_tokens, late_sums, d_gains = rest
    lines = n_dp // 2
    ring = [grad_taps]
    flipped = []

    def ring_step(*work):
        flipped.append(lax.ppermute(ring[-1], "dp", ring_perm(n_dp, 0, 1)))
        if len(ring) < lines:
            ring.append(lax.ppermute(ring[-1], "dp", ring_perm(n_dp, 1, 0)))
        (ring[-1], flipped[-1]), *work = tie_lists([ring[-1], flipped[-1]], *work)
        return work

    ge_all = lax.all_to_all(grad_energy, "dp", 0, 0, tiled=True).reshape(samples, width)
    d_cross = far_parts(d_cross)
    back = attn_weights([attn_own] + attn_near, [qkv_own] + sent_near, half, share)
    d_attn, d_value = list(back[:half]), list(back[half:])
    low_first, mix_first = conv_back(gs, xs, mixing, kernel_bank, n, 0, 2)
    (low_first, mix_first, ge_all, gs, d_tokens), d_cross, d_attn, d_value, d_out = ring_step(
        [low_first, mix_first, ge_all, gs, d_tokens], d_cross, d_attn, d_value, d_out
    )
    d_out = far_parts(d_out)
    token_side = scatter_side(d_tokens)
    low_last, mix_last = conv_back(gs, xs, mixing, kernel_bank, n, 1, 2)
    ready, d_out, d_cross, d_attn, shares, token_side = ring_step(
        [low_last, mix_last],
        d_out,
        d_cross,
        d_attn,
        shares,
        token_side,
    )
    low_last, mix_last = ready
    low_part = jnp.concatenate([low_first, low_last], axis=2)
    mixing_conv = mix_first + mix_last

    cross_grads = jnp.concatenate([add_all(d_cross), add_all(d_out)], axis=1).astype(BF)
    token_parts = scatter_lines(*token_side)
    d_attn = far_parts(d_attn)
    low_near = near_sums([low_part[j] for j in range(n)])
    done = energy_sums(place, mixing_all, scale_band, ge_all, pairs, n)
    count_sums = -(-(tokens + 9 + -(-samples * kernels // channels)) // 8) * 8
    count_all = -(-(count_sums + 4 * n + 1) // 8) * 8
    features, color_image, pack = side_outputs(
        place,
        three,
        branch,
        grad_image,
        color_scale,
        colors,
        color_bias.astype(F),
        tokens,
        shares,
        cross_key,
        cross_value,
        d_gains,
        late_sums,
        count_sums,
        count_all,
        side,
    )
    done, d_attn, low_near, (g_mlp, pack, lefts, cross_grads), d_value, token_parts = ring_step(
        list(done), d_attn, low_near, [g_mlp, pack, lefts, cross_grads], d_value, token_parts
    )
    cross_grads = scatter(cross_grads)
    scale_energy, mixing_energy = done

    def as_rows(v):
        v = v.reshape(1, -1)
        v = jnp.pad(v, ((0, 0), (0, -v.shape[1] % channels)))
        return v.reshape(-1, channels)

    low_parts = far_parts(low_near)
    pack, grad_images = late_sums_kernel(
        place,
        inverse,
        pack,
        low_parts,
        own_images,
        scale_in,
        scale_energy.reshape(n, channels),
        as_rows(mixing_energy),
        mixing_conv,
        count_sums,
        tokens + 9,
    )
    pack = add_over(pack, "rows")
    d_value = far_parts(d_value)
    energy = bank_energy(places, lefts, ge_all, kernel_bank)
    (grad_images, pack, energy), d_value, d_attn = ring_step(
        [grad_images, pack, energy], d_value, d_attn
    )
    while len(flipped) < lines:
        ((pack,),) = ring_step([pack])

    everyone_rows = jnp.broadcast_to(pack.astype(BF)[None], (n_dp,) + pack.shape)
    everyone_rows = lax.all_to_all(everyone_rows, "dp", 0, 0, tiled=True)
    attn_side = jnp.concatenate([add_all(d_attn), add_all(d_value)], axis=1).astype(BF)
    attn_side = scatter_side(attn_side)
    blocks = [None] * n_dp
    for t in range(lines):
        for e, v in enumerate((ring[t], flipped[t])):
            blocks[2 * t + e] = v
    grad_bank = bank_main(places, inverse, at, blocks, energy, side)
    (grad_bank, everyone_rows), attn_side = tie_lists([grad_bank, everyone_rows], attn_side)
    attn_parts = scatter_lines(*attn_side)
    sums = jnp.sum(everyone_rows[:, :count_sums].astype(F), axis=0)
    gathered = everyone_rows[:, count_sums:].astype(F)
    scale_grad, bands_grad, token_all, rgb_all = (
        gathered[:, i * n : (i + 1) * n].reshape(samples, channels) for i in range(4)
    )
    bands_grad = bands_grad.reshape(n_dp, samples, band).transpose(1, 0, 2)
    scale_grad = scale_grad + bands_grad.reshape(samples, channels)
    mixing_grad = gathered[:, 4 * n, : n * kernels].reshape(samples, kernels)
    mixing_sum = sums[tokens + 9 :].reshape(-1)[: samples * kernels]
    mixing_grad = mixing_grad + mixing_sum.reshape(samples, kernels)
    sums = sums[: tokens + 9] * inverse
    grad_images = grad_images.reshape(1, side, side, channels)

    d_select, d_style, d_rgb, styles_grad, d_table = style_final(
        places,
        inverse,
        mixing_grad,
        scale_grad,
        rgb_all,
        token_all,
        styles_all,
        labels_all,
        select_turned,
        style_proj,
        rgb_style,
        class_table.shape[0],
        n,
    )

    cross_grads, attn_grads, token_grads = tie(
        *(add_all(v) * inverse for v in ([cross_grads], attn_parts, token_parts))
    )
    g_mlp = g_mlp.astype(F) * inverse
    wide = up_proj.shape[1]

    def column(grads, i):
        return grads[:, i * share : (i + 1) * share]

    return (
        features,
        color_image,
        grad_images,
        styles_grad,
        grad_bank,
        d_select.T,
        d_style,
        sums[tokens + 7],
        sums[tokens + 8],
        sums[tokens + 6],
        column(attn_grads, 0),
        column(attn_grads, 1),
        column(attn_grads, 2),
        column(cross_grads, 2).T,
        sums[tokens + 1],
        column(cross_grads, 0),
        column(token_grads, 0),
        column(token_grads, 1),
        column(cross_grads, 1).T,
        d_table,
        sums[:tokens],
        sums[tokens],
        g_mlp[:, :wide],
        g_mlp[:, wide:].T,
        d_rgb,
        sums[tokens + 2 : tokens + 5].T,
        sums[tokens + 5, :3],
    )


def solution(mesh):
    whole = P()
    columns = P(None, "rows")
    lines = P("rows", None)
    both = P(("dp", "rows"), None, None, None)
    placed = (
        both,
        P("dp", None),
        P("dp"),
        P(("dp", "rows"), None, None),
        P("dp"),
        both,
        both,
        P(None, None, None, None, "rows"),
        whole,
        whole,
        whole,
        whole,
        whole,
        columns,
        columns,
        columns,
        lines,
        whole,
        columns,
        columns,
        columns,
        lines,
        whole,
        whole,
        whole,
        columns,
        lines,
        whole,
        whole,
        whole,
    )
    given = (
        both,
        both,
        both,
        P("dp", None),
        P(None, None, "dp", None, "rows"),
        whole,
        whole,
        whole,
        whole,
        whole,
        P("dp", "rows"),
        P("dp", "rows"),
        P("dp", "rows"),
        P("rows", "dp"),
        whole,
        P("dp", "rows"),
        P("dp", "rows"),
        P("dp", "rows"),
        P("rows", "dp"),
        whole,
        whole,
        whole,
        P("dp", "rows"),
        P("rows", "dp"),
        whole,
        whole,
        whole,
    )
    return jax.shard_map(local, mesh=mesh, in_specs=placed, out_specs=given, check_vma=False)
```

```python
import functools
import math

import jax
import jax.numpy as jnp
from jax import lax
from jax.experimental import pallas as pl
from jax.experimental.pallas import tpu as pltpu
from jax.sharding import PartitionSpec as P

HD = 64
SUB = 32
BF = jnp.bfloat16
F = jnp.float32
VMEM_LIMIT = 56 * 2**20
EPS = 1e-6


def dot_nn(a, b):
    return lax.dot_general(a, b, (((1,), (0,)), ((), ())), preferred_element_type=F)


def dot_nt(a, b):
    return lax.dot_general(a, b, (((1,), (1,)), ((), ())), preferred_element_type=F)


def dot_tn(a, b):
    return lax.dot_general(a, b, (((0,), (0,)), ((), ())), preferred_element_type=F)


def params():
    return pltpu.CompilerParams(vmem_limit_bytes=VMEM_LIMIT)


def swap(x, axis, delta):
    n = lax.axis_size(axis)
    return lax.ppermute(x, axis, [(i, i ^ delta) for i in range(n)])


def spread(x):
    n = lax.axis_size("rows")
    blocks = [None] * n
    blocks[0] = x
    for j in range(2, n, 2):
        blocks[j] = swap(x, "rows", j)
    for j in range(0, n, 2):
        blocks[j + 1] = swap(blocks[j], "rows", 1)
    return blocks


def near_sums(blocks):
    out = []
    for j in range(0, len(blocks), 2):
        near = blocks[j].astype(F) + swap(blocks[j + 1], "rows", 1).astype(F)
        out.append(near.astype(BF))
    return out


def far_sum(near):
    total = near[0].astype(F)
    for j in range(1, len(near)):
        total = total + swap(near[j], "rows", 2 * j).astype(F)
    return total


def collect(blocks):
    return far_sum(near_sums(blocks))


def double(x, axis, place):
    delta = 1
    while delta < lax.axis_size(axis):
        other = swap(x, axis, delta)
        high = (place & delta) != 0
        x = jnp.where(high, jnp.concatenate([other, x]), jnp.concatenate([x, other]))
        delta *= 2
    return x


def merge_step(sums, gathered, axis, place, delta):
    rows = sums.shape[0]
    other = swap(jnp.concatenate([sums, gathered]), axis, delta)
    high = (place & delta) != 0
    theirs = other[rows:]
    gathered = jnp.where(
        high, jnp.concatenate([theirs, gathered]), jnp.concatenate([gathered, theirs])
    )
    return sums + other[:rows], gathered


def add_over(sums, axis):
    delta = 1
    while delta < lax.axis_size(axis):
        sums = sums + swap(sums, axis, delta)
        delta *= 2
    return sums


def tree(parts):
    while len(parts) > 1:
        parts = [a + b for a, b in zip(parts[::2], parts[1::2])]
    return parts[0]


def everyone(x, axis):
    return [x] + [swap(x, axis, j) for j in range(1, lax.axis_size(axis))]


def in_order(blocks, place):
    stacked = jnp.stack(blocks)
    return jnp.take(stacked, jnp.arange(len(blocks), dtype=jnp.int32) ^ place, axis=0)


def ring_perm(n, step, flip):
    lines = n // 2
    return [(i, ((i // 2 + step) % lines) * 2 + ((i % 2) ^ flip)) for i in range(n)]


def ring_gather(x):
    n = lax.axis_size("dp")
    out = []
    held = x
    for step in range(n // 2):
        if step:
            held = lax.ppermute(held, "dp", ring_perm(n, 1, 0))
        out.append(held)
        out.append(lax.ppermute(held, "dp", ring_perm(n, 0, 1)))
    return out


def ring_source(n, place, slot):
    lines = n // 2
    return ((place // 2 - slot // 2) % lines) * 2 + ((place % 2) ^ (slot % 2))


def ring_target(n, place, slot):
    lines = n // 2
    return ((place // 2 + slot // 2) % lines) * 2 + ((place % 2) ^ (slot % 2))


def scatter(grads):
    return lax.psum_scatter(grads, "dp", scatter_dimension=0, tiled=True)


def scatter_side(grads):
    n = lax.axis_size("dp")
    side = lax.axis_index("dp") % 2
    bands = grads.reshape(n // 2, 2, grads.shape[0] // n, grads.shape[1])
    mine = lax.dynamic_index_in_dim(bands, side, 1, keepdims=False)
    theirs = lax.dynamic_index_in_dim(bands, 1 - side, 1, keepdims=False)
    return mine, lax.ppermute(theirs, "dp", ring_perm(n, 0, 1))


def scatter_lines(mine, theirs):
    n = lax.axis_size("dp")
    lines = n // 2
    line = lax.axis_index("dp") // 2
    half = (mine.astype(F) + theirs.astype(F)).astype(BF)
    pieces = [lax.dynamic_index_in_dim(half, line, 0, keepdims=False)]
    for step in range(1, lines):
        piece = lax.dynamic_index_in_dim(half, (line + step) % lines, 0, keepdims=False)
        pieces.append(lax.ppermute(piece, "dp", ring_perm(n, step, 0)))
    return pieces


def tie(*values):
    return lax.optimization_barrier(values)


def move_up(v, axis):
    shape = list(v.shape)
    shape[axis] = 1
    kept = lax.slice_in_dim(v, 0, v.shape[axis] - 1, axis=axis)
    return jnp.concatenate([jnp.zeros(shape, v.dtype), kept], axis=axis)


def move_down(v, axis):
    shape = list(v.shape)
    shape[axis] = 1
    kept = lax.slice_in_dim(v, 1, v.shape[axis], axis=axis)
    return jnp.concatenate([kept, jnp.zeros(shape, v.dtype)], axis=axis)


def band_mask(kernels):
    width = SUB * kernels
    row = lax.broadcasted_iota(jnp.int32, (SUB, width), 0)
    lane = lax.broadcasted_iota(jnp.int32, (SUB, width), 1)
    return (lane // kernels) == row


def split_dot(a, b):
    high = a.astype(BF)
    rest = (a - high.astype(F)).astype(BF)
    return dot_nn(high, b) + dot_nn(rest, b)


def widen_mask(block, kernels):
    row = lax.broadcasted_iota(jnp.int32, (block, block * kernels), 0)
    lane = lax.broadcasted_iota(jnp.int32, (block, block * kernels), 1)
    return jnp.where(lane // kernels == row, 1.0, 0.0).astype(BF)


def tile_mask(block, kernels):
    row = lax.broadcasted_iota(jnp.int32, (kernels, block * kernels), 0)
    lane = lax.broadcasted_iota(jnp.int32, (kernels, block * kernels), 1)
    return jnp.where(lane % kernels == row, 1.0, 0.0).astype(BF)


def conv_forward(codes, select, style, payload, images, bank, side):
    groups = len(images)
    low, channels = images[0].shape
    rows = groups * low
    kernels, width = bank.shape[3], bank.shape[4]
    pad, depth = codes.shape
    block = min(channels, 128)
    steps = channels // block
    parts = block // SUB
    span = SUB * kernels

    extra = payload.shape[0]

    def body(c_ref, sel_ref, sty_ref, pay_ref, *rest):
        x_refs = rest[:groups]
        b_ref, out_r = rest[groups], rest[groups + 1 : 2 * groups + 1]
        raw_ref, dem_ref, xs_ref, mix_ref, sc_ref = rest[2 * groups + 1 : 2 * groups + 6]
        acc, en, scale, mix_row, widen = rest[2 * groups + 6 :]
        step = pl.program_id(0)

        @pl.when(step == 0)
        def _():
            acc[...] = jnp.zeros_like(acc)
            en[...] = jnp.zeros_like(en)
            logits = dot_nt(c_ref[...], sel_ref[...])
            e = jnp.exp(logits - jnp.max(logits, axis=1, keepdims=True))
            mixing = e / jnp.sum(e, axis=1, keepdims=True)
            mix_ref[...] = mixing
            mix_row[...] = split_dot(mixing, tile_mask(block, kernels))
            scale[...] = dot_nn(c_ref[...], sty_ref[...]) + 1.0
            sc_ref[...] = scale[...]
            widen[...] = widen_mask(block, kernels)

        here = scale[:, pl.ds(pl.multiple_of(step * block, block), block)]
        wide_scale = split_dot(here, widen[...]) * mix_row[...]
        mask = band_mask(kernels)
        xs = []
        for s in range(groups):
            xs.append((x_refs[s][...].astype(F) * here[s : s + 1]).astype(BF))
            xs_ref[0, s * low : (s + 1) * low] = xs[s]
        xs_ref[0, rows:] = pay_ref[...]
        a = []
        for s in range(groups):
            a.append((dot_nn(xs[s], widen[...]) * mix_row[s : s + 1]).astype(BF))
        left = []
        for u in range(parts):
            cut = slice(u * span, (u + 1) * span)
            pieces = [v[:, cut] for v in a]
            for s in range(groups):
                pieces.append(jnp.where(mask, wide_scale[s : s + 1, cut], 0.0).astype(BF))
            left.append(jnp.concatenate(pieces))
        energy = en[...]
        for t in range(9):
            b = b_ref[t // 3, t % 3].reshape(block * kernels, width)
            total = acc[t]
            for u in range(parts):
                p = dot_nn(left[u], b[u * span : (u + 1) * span])
                total = total + p[:rows]
                m = p[rows:]
                energy = energy + jnp.sum((m * m).reshape(groups, SUB // 8, 8, width), axis=1)
            acc[t] = total
        en[...] = energy

        @pl.when(step == steps - 1)
        def _():
            demod = lax.rsqrt(jnp.sum(en[...], axis=1, keepdims=True) + 1e-8)
            dem_ref[...] = demod
            for s in range(groups):
                v = [acc[t, s * low : (s + 1) * low].reshape(side, side, width) for t in range(9)]
                for py in range(2):
                    h = []
                    for tx in range(3):
                        if py == 0:
                            h.append(move_up(v[tx], 0) + v[3 + tx] + v[6 + tx])
                        else:
                            h.append(v[tx] + v[3 + tx] + move_down(v[6 + tx], 0))
                    for px in range(2):
                        if px == 0:
                            o = move_up(h[0], 1) + h[1] + h[2]
                        else:
                            o = h[0] + h[1] + move_down(h[2], 1)
                        o = o.reshape(low, width)
                        q = (py * 2 + px) * low
                        raw_ref[s, q : q + low] = o.astype(raw_ref.dtype)
                        out_r[s][q : q + low] = (o * demod[s]).astype(BF)

    return pl.pallas_call(
        body,
        grid=(steps,),
        in_specs=[
            pl.BlockSpec((pad, depth), lambda i: (0, 0)),
            pl.BlockSpec((kernels, depth), lambda i: (0, 0)),
            pl.BlockSpec((depth, channels), lambda i: (0, 0)),
            pl.BlockSpec((extra, block), lambda i: (0, 0)),
        ]
        + [pl.BlockSpec((low, block), lambda i: (0, i))] * groups
        + [pl.BlockSpec((3, 3, block, kernels, width), lambda i: (0, 0, i, 0, 0))],
        out_specs=[pl.BlockSpec((4 * low, width), lambda i: (0, 0))] * groups
        + [
            pl.BlockSpec((groups, 4 * low, width), lambda i: (0, 0, 0)),
            pl.BlockSpec((groups, 1, width), lambda i: (0, 0, 0)),
            pl.BlockSpec((1, rows + extra, block), lambda i: (i, 0, 0)),
            pl.BlockSpec((pad, kernels), lambda i: (0, 0)),
            pl.BlockSpec((pad, channels), lambda i: (0, 0)),
        ],
        out_shape=[jax.ShapeDtypeStruct((4 * low, width), BF)] * groups
        + [
            jax.ShapeDtypeStruct((groups, 4 * low, width), BF),
            jax.ShapeDtypeStruct((groups, 1, width), F),
            jax.ShapeDtypeStruct((steps, rows + extra, block), BF),
            jax.ShapeDtypeStruct((pad, kernels), F),
            jax.ShapeDtypeStruct((pad, channels), F),
        ],
        scratch_shapes=[
            pltpu.VMEM((9, rows, width), F),
            pltpu.VMEM((groups, 8, width), F),
            pltpu.VMEM((pad, channels), F),
            pltpu.VMEM((pad, block * kernels), F),
            pltpu.VMEM((block, block * kernels), BF),
        ],
        compiler_params=params(),
        cost_estimate=pl.CostEstimate(
            flops=27 * rows * channels * kernels * width,
            bytes_accessed=18 * channels * kernels * width,
            transcendentals=0,
        ),
        name="conv_forward",
    )(codes, select, style, payload, *images, bank)


def conv_back(gs, xs, mixing, bank, groups, part, parts):
    _, rows, width = gs.shape
    blocks, held, block = xs.shape
    steps = blocks // parts
    first = part * steps
    channels, kernels = steps * block, bank.shape[3]
    pad = mixing.shape[0]
    low = rows // groups

    def body(g_ref, x_ref, m_ref, b_ref, low_ref, mix_ref, acc, mix_row, widen):
        step = pl.program_id(0)

        @pl.when(step == 0)
        def _():
            acc[...] = jnp.zeros_like(acc)
            mix_row[...] = split_dot(m_ref[...], tile_mask(block, kernels))
            widen[...] = widen_mask(block, kernels)

        total = None
        for t in range(9):
            p = dot_nt(g_ref[t], b_ref[t // 3, t % 3].reshape(block * kernels, width))
            total = p if total is None else total + p
        wide = dot_nn(x_ref[0, :rows], widen[...])
        acc[...] += jnp.sum((wide * total).reshape(groups, low // 8, 8, block * kernels), axis=1)
        for s in range(groups):
            cut = slice(s * low, (s + 1) * low)
            mixed = (total[cut] * mix_row[s : s + 1]).astype(BF)
            low_ref[s] = dot_nt(mixed, widen[...]).astype(BF)

        @pl.when(step == steps - 1)
        def _():
            sums = jnp.sum(acc[...], axis=1)
            mix_ref[...] = lax.dot_general(
                sums,
                tile_mask(block, kernels).astype(F),
                (((1,), (1,)), ((), ())),
                precision=lax.Precision.HIGHEST,
                preferred_element_type=F,
            )

    return pl.pallas_call(
        body,
        grid=(steps,),
        in_specs=[
            pl.BlockSpec((9, rows, width), lambda i: (0, 0, 0)),
            pl.BlockSpec((1, held, block), lambda i: (first + i, 0, 0)),
            pl.BlockSpec((pad, kernels), lambda i: (0, 0)),
            pl.BlockSpec((3, 3, block, kernels, width), lambda i: (0, 0, first + i, 0, 0)),
        ],
        out_specs=[
            pl.BlockSpec((groups, low, block), lambda i: (0, 0, i)),
            pl.BlockSpec((groups, kernels), lambda i: (0, 0)),
        ],
        out_shape=[
            jax.ShapeDtypeStruct((groups, low, channels), BF),
            jax.ShapeDtypeStruct((groups, kernels), F),
        ],
        scratch_shapes=[
            pltpu.VMEM((groups, 8, block * kernels), F),
            pltpu.VMEM((pad, block * kernels), F),
            pltpu.VMEM((block, block * kernels), BF),
        ],
        compiler_params=params(),
        cost_estimate=pl.CostEstimate(
            flops=18 * rows * channels * kernels * width,
            bytes_accessed=18 * channels * kernels * width,
            transcendentals=0,
        ),
        name="conv_back",
    )(gs, xs, mixing, bank)


def roll_kernels(v, shift):
    n = v.shape[-2]
    return pltpu.roll(v, shift % n, v.ndim - 2) if shift % n else v


def bank_pairs(place, bank, band):
    kernels, width = bank.shape[3], bank.shape[4]
    count = kernels // 2 + 1
    block = min(band, SUB)

    def body(place_ref, b_ref, q_ref):
        for c in range(block // 8):
            cut = slice(c * 8, (c + 1) * 8)
            total = [None] * count
            for t in range(9):
                b = b_ref[t // 3, t % 3, cut].astype(F)
                for r in range(count):
                    p = b * roll_kernels(b, -r)
                    total[r] = p if t == 0 else total[r] + p
            for r in range(count):
                q_ref[r, c * 8 * kernels : (c + 1) * 8 * kernels] = (
                    total[r].reshape(8 * kernels, width).astype(BF)
                )

    return pl.pallas_call(
        body,
        grid_spec=pltpu.PrefetchScalarGridSpec(
            num_scalar_prefetch=1,
            grid=(band // block,),
            in_specs=[
                pl.BlockSpec(
                    (3, 3, block, kernels, width),
                    lambda i, s: (0, 0, s[1] * (band // block) + i, 0, 0),
                )
            ],
            out_specs=pl.BlockSpec((count, block * kernels, width), lambda i, s: (0, i, 0)),
        ),
        out_shape=jax.ShapeDtypeStruct((count, band * kernels, width), BF),
        compiler_params=params(),
        cost_estimate=pl.CostEstimate(
            flops=20 * count * band * kernels * width,
            bytes_accessed=18 * band * kernels * width,
            transcendentals=0,
        ),
        name="bank_pairs",
    )(place, bank)


def energy_sums(place, mixing, scale, ge, pairs, group):
    samples, kernels = mixing.shape
    band = scale.shape[1]
    count = pairs.shape[0]
    exact = dict(precision=lax.Precision.HIGHEST, preferred_element_type=F)
    along = (((1,), (0,)), ((), ()))

    def fold(a, mask):
        high = a.astype(BF)
        rest = (a - high.astype(F)).astype(BF)
        return dot_nt(high, mask) + dot_nt(rest, mask)

    def body(place_ref, m_ref, s_ref, g_ref, q_ref, se_ref, me_ref):
        m = m_ref[...]
        wides = split_dot(s_ref[...], widen_mask(band, kernels))
        ge = (2.0 * g_ref[...]).astype(BF)
        row = lax.broadcasted_iota(jnp.int32, (kernels, kernels), 0)
        lane = lax.broadcasted_iota(jnp.int32, (kernels, kernels), 1)
        tile = tile_mask(band, kernels)
        square = wides * wides
        se, me = None, None
        for r in range(count):
            g = dot_nt(ge, q_ref[r])
            ahead = jnp.where(row == (lane + r) % kernels, 1.0, 0.0)
            behind = jnp.where(row == (lane + kernels - r) % kernels, 1.0, 0.0)
            next_m = lax.dot_general(m, ahead, along, **exact)
            both = split_dot(m * next_m, tile)
            weight = 1.0 if r == 0 or 2 * r == kernels else 2.0
            part = (weight * both) * g
            se = part if se is None else se + part
            h = fold(g * square, tile)
            part = next_m * h
            if weight == 2.0:
                part = part + lax.dot_general(m * h, behind, along, **exact)
            me = part if me is None else me + part
        se = fold(se * wides, widen_mask(band, kernels))
        for s in range(samples):
            to = pl.ds(s // group * group + lax.bitwise_xor(place_ref[0], s % group), 1)
            se_ref[to] = se[s : s + 1]
            me_ref[to] = me[s : s + 1]

    return pl.pallas_call(
        body,
        in_specs=[smem()] + vmem(4),
        out_shape=[
            jax.ShapeDtypeStruct((samples, band), F),
            jax.ShapeDtypeStruct((samples, kernels), F),
        ],
        compiler_params=params(),
        name="energy_sums",
    )(place, mixing, scale, ge, pairs)


def bank_energy(place, lefts, ge, bank):
    kernels, width = bank.shape[3], bank.shape[4]
    count, rows_all, samples = lefts.shape
    band = rows_all // kernels
    step = min(band, 16)

    def body(place_ref, l_ref, ge_ref, b_ref, o_ref, rights):
        @pl.when(pl.program_id(0) == 0)
        def _():
            ge = ge_ref[...].astype(BF)
            for r in range(count):
                rights[r] = dot_nn(l_ref[r], ge)

        for tx in range(3):
            for i in range(band // step):
                cut = slice(i * step * kernels, (i + 1) * step * kernels)
                b = b_ref[0, tx, i * step : (i + 1) * step].astype(F)
                e = rights[0, cut].reshape(step, kernels, width) * b
                for r in range(1, count):
                    right = rights[r, cut].reshape(step, kernels, width)
                    e = e + right * roll_kernels(b, -r)
                    if 2 * r != kernels:
                        e = e + roll_kernels(right * b, r)
                o_ref[0, tx, i * step : (i + 1) * step] = e.astype(BF)

    return pl.pallas_call(
        body,
        grid_spec=pltpu.PrefetchScalarGridSpec(
            num_scalar_prefetch=1,
            grid=(3,),
            in_specs=[
                pl.BlockSpec((count, band * kernels, samples), lambda t, s: (0, 0, 0)),
                pl.BlockSpec((samples, width), lambda t, s: (0, 0)),
                pl.BlockSpec((1, 3, band, kernels, width), lambda t, s: (t, 0, s[1], 0, 0)),
            ],
            out_specs=pl.BlockSpec((1, 3, band, kernels, width), lambda t, s: (t, 0, 0, 0, 0)),
            scratch_shapes=[pltpu.VMEM((count, band * kernels, width), F)],
        ),
        out_shape=jax.ShapeDtypeStruct((3, 3, band, kernels, width), BF),
        compiler_params=params(),
        cost_estimate=pl.CostEstimate(
            flops=400 * band * kernels * width,
            bytes_accessed=36 * band * kernels * width,
            transcendentals=0,
        ),
        name="bank_energy",
    )(place, lefts, ge, bank)


def line_sums(g, tap, axis):
    if tap == 0:
        return g[1] + move_down(g[0], axis)
    if tap == 1:
        return g[0] + g[1]
    return g[0] + move_up(g[1], axis)


def bank_main(places, scale, at, context, taps, energy, side):
    blocks = len(taps)
    groups, rows, width = taps[0].shape
    low = side * side
    points = 4 * low
    tokens = (rows - points) // 2
    held = blocks * groups * low
    band, kernels = energy.shape[2], energy.shape[3]

    def body(place_ref, scale_ref, a_ref, c_ref, *rest):
        here = place_ref[1]
        g_refs = rest[:blocks]
        e_ref, o_ref, token_ref, lines, sums, keyval = rest[blocks:]
        ty = pl.program_id(0)

        def source(b):
            line = lax.rem(here // 2 + blocks // 2 - b // 2, blocks // 2)
            return 2 * line + lax.bitwise_xor(lax.rem(here, 2), b % 2)

        @pl.when(ty == 0)
        def _():
            for b in range(blocks):
                for s in range(groups):
                    at_row = pl.multiple_of((source(b) * groups + s) * tokens, tokens)
                    for i in range(2):
                        cut = slice(points + i * tokens, points + (i + 1) * tokens)
                        keyval[i, pl.ds(at_row, tokens)] = g_refs[b][s, cut]
            for i in range(2):
                token_ref[:, i * width : (i + 1) * width] = (
                    dot_nn(c_ref[...], keyval[i]) * scale_ref[0]
                )
        for tap in range(3):

            @pl.when(ty == tap)
            def _():
                for b in range(blocks):
                    for s in range(groups):
                        g = g_refs[b][s, :points].astype(F).reshape(2, 2, side, side, width)
                        for px in range(2):
                            v = line_sums((g[0, px], g[1, px]), tap, 0)
                            at_row = (source(b) * groups + s) * low
                            at_row = pl.multiple_of(at_row, low)
                            lines[px, pl.ds(at_row, low)] = v.reshape(low, width)

        for tx in range(3):
            for b in range(blocks * groups):
                cut = slice(b * low, (b + 1) * low)
                pair = [lines[px, cut].reshape(side, side, width) for px in range(2)]
                sums[cut] = line_sums(pair, tx, 1).reshape(low, width).astype(BF)
            p = dot_nn(a_ref[...], sums[...]).reshape(band, kernels, width)
            o_ref[0, tx] = (p + e_ref[0, tx].astype(F)) * scale_ref[0]

    return pl.pallas_call(
        body,
        grid=(3,),
        in_specs=[
            smem(),
            smem(),
            pl.BlockSpec((band * kernels, held), lambda t: (0, 0)),
            pl.BlockSpec(context.shape, lambda t: (0, 0)),
        ]
        + [pl.BlockSpec((groups, rows, width), lambda t: (0, 0, 0))] * blocks
        + [pl.BlockSpec((1, 3, band, kernels, width), lambda t: (t, 0, 0, 0, 0))],
        out_specs=[
            pl.BlockSpec((1, 3, band, kernels, width), lambda t: (t, 0, 0, 0, 0)),
            pl.BlockSpec((band, 2 * width), lambda t: (0, 0)),
        ],
        out_shape=[
            jax.ShapeDtypeStruct((3, 3, band, kernels, width), F),
            jax.ShapeDtypeStruct((band, 2 * width), F),
        ],
        scratch_shapes=[
            pltpu.VMEM((2, held, width), F),
            pltpu.VMEM((held, width), BF),
            pltpu.VMEM((2, blocks * groups * tokens, width), BF),
        ],
        compiler_params=params(),
        cost_estimate=pl.CostEstimate(
            flops=18 * band * kernels * held * width,
            bytes_accessed=18 * held * width + 54 * band * kernels * width,
            transcendentals=0,
        ),
        name="bank_main",
    )(places, scale, at, context, *taps, energy)


def tap_sums(grads, demod, raw, side, copies):
    groups = len(grads)
    _, points, width = raw.shape
    low = side * side

    held = grads[0].shape[0]

    def body(d_ref, r_ref, *rest):
        g_refs = rest[:groups]
        taps_ref, sums_ref, en_ref = rest[groups:]
        for s in range(groups):
            part = g_refs[s][:points].astype(F)
            demod = d_ref[s]
            grad_demod = jnp.sum(part * r_ref[s].astype(F), axis=0, keepdims=True)
            en = -0.5 * grad_demod * demod * demod * demod
            for i in range(copies):
                en_ref[i, s : s + 1] = en
            taps_ref[s, :points] = (part * demod).astype(BF)
            taps_ref[s, points:] = g_refs[s][points:]
            g = taps_ref[s, :points].astype(F).reshape(2, 2, side, side, width)
            for ty in range(3):
                lines = [line_sums((g[0, px], g[1, px]), ty, 0) for px in range(2)]
                for tx in range(3):
                    v = line_sums(lines, tx, 1).reshape(low, width).astype(BF)
                    sums_ref[3 * ty + tx, s * low : (s + 1) * low] = v

    return pl.pallas_call(
        body,
        out_shape=[
            jax.ShapeDtypeStruct((groups, held, width), BF),
            jax.ShapeDtypeStruct((9, groups * low, width), BF),
            jax.ShapeDtypeStruct((copies, groups, width), F),
        ],
        compiler_params=params(),
        name="tap_sums",
    )(demod, raw, *grads)


def rms(field, gain):
    inverse = lax.rsqrt(jnp.mean(field * field, axis=-1, keepdims=True) + EPS)
    return field * inverse * gain, inverse


def rms_back(field, gain, grad_out):
    inverse = lax.rsqrt(jnp.mean(field * field, axis=-1, keepdims=True) + EPS)
    scaled = grad_out * gain
    grad_gain = jnp.sum(grad_out * field * inverse, axis=0, keepdims=True)
    mean = jnp.mean(scaled * field, axis=-1, keepdims=True)
    return inverse * scaled - field * inverse**3 * mean, grad_gain


def sigmoid(v):
    return 1.0 / (1.0 + jnp.exp(-v))


def silu_slope(v):
    q = sigmoid(v)
    return q * (1.0 + v * (1.0 - q))


def self_prob(q, k):
    kf = k.astype(F)
    square = jnp.sum(kf * kf, axis=1, keepdims=True)
    scores = (2.0 * dot_nt(k, q) - square) * (1.0 / math.sqrt(HD))
    e = jnp.exp(scores - jnp.max(scores, axis=0, keepdims=True))
    return e * (1.0 / jnp.sum(e, axis=0, keepdims=True))


def cross_prob(q, k):
    scores = dot_nt(k, q) * (1.0 / math.sqrt(HD))
    e = jnp.exp(scores - jnp.max(scores, axis=0, keepdims=True))
    return e * (1.0 / jnp.sum(e, axis=0, keepdims=True))


def side_slot(own_ref, send_ref, j, start, width):
    at = start + j // 2 * width
    return (send_ref if j % 2 else own_ref), slice(at, at + width)


def fetch(refs, buffer, sems):
    copies = [pltpu.make_async_copy(r, buffer.at[i], sems.at[i]) for i, r in enumerate(refs)]

    def take(i):
        copies[i].wait()
        return buffer[i]

    return copies, take


def anywhere(count):
    return [pl.BlockSpec(memory_space=pl.ANY)] * count


def smem():
    return pl.BlockSpec(memory_space=pltpu.SMEM)


def vmem(count):
    return [pl.BlockSpec(memory_space=pltpu.VMEM)] * count


def attn_forward(place, conv_parts, noise, gains, wqkv, wo):
    n = len(wo)
    points, width = conv_parts[0].shape
    share, channels = wo[0].shape

    def body(place_ref, noise_ref, gains_ref, *rest):
        part_r, wqkv_r, wo_r = (rest[i * n : (i + 1) * n] for i in range(3))
        conv_ref, two_ref, qkv_ref, own_ref, send_ref = rest[3 * n : 3 * n + 5]
        wide, out_w, wide_sem, out_sem = rest[3 * n + 5 :]
        wide_copies, take_wide = fetch(wqkv_r, wide, wide_sem)
        out_copies, take_out = fetch(wo_r, out_w, out_sem)
        for a, b in zip(wide_copies, out_copies):
            a.start()
            b.start()
        here = place_ref[0]
        for j in range(n):
            start = pl.multiple_of(lax.bitwise_xor(here, j) * width, width)
            conv_ref[:, pl.ds(start, width)] = part_r[j][...]
        out = conv_ref[...].astype(F) + gains_ref[0:1] * noise_ref[...] + gains_ref[1:2]
        one = out * sigmoid(out)
        normed = rms(one, gains_ref[2:3])[0].astype(BF)
        own_ref[:, :channels] = normed
        send_ref[:, :channels] = normed
        two_ref[...] = one
        for j in range(n):
            qkv_ref[j] = dot_nn(normed, take_wide(j)).astype(BF)
            heads = []
            for h in range(share // HD):
                q, k, v = (
                    qkv_ref[j, :, i * share + h * HD : i * share + (h + 1) * HD] for i in range(3)
                )
                heads.append(dot_tn(v, self_prob(q, k).astype(BF)))
            side_ref, cut = side_slot(own_ref, send_ref, j, channels, share)
            side_ref[:, cut] = jnp.concatenate(heads).T.astype(BF)
            two_ref[...] += dot_nn(side_ref[:, cut], take_out(j))

    return pl.pallas_call(
        body,
        in_specs=[smem()] + vmem(2 + n) + anywhere(2 * n),
        scratch_shapes=[
            pltpu.VMEM((n, channels, 3 * share), BF),
            pltpu.VMEM((n, share, channels), BF),
            pltpu.SemaphoreType.DMA((n,)),
            pltpu.SemaphoreType.DMA((n,)),
        ],
        out_shape=[
            jax.ShapeDtypeStruct((points, channels), BF),
            jax.ShapeDtypeStruct((points, channels), F),
            jax.ShapeDtypeStruct((n, points, 3 * share), BF),
        ]
        + [jax.ShapeDtypeStruct((points, channels + n // 2 * share), BF)] * 2,
        compiler_params=params(),
        cost_estimate=pl.CostEstimate(
            flops=10 * points * channels * channels,
            bytes_accessed=16 * channels * channels,
            transcendentals=points * points * channels // HD,
        ),
        name="attn_forward",
    )(place, noise, gains, *conv_parts, *wqkv, *wo)


def cross_forward(two, gains, cq, co, ckv):
    points, channels = two.shape
    n = len(cq)
    share = cq[0].shape[1]

    def body(two_ref, gains_ref, *rest):
        cq_r, co_r, ckv_r = (rest[i * n : (i + 1) * n] for i in range(3))
        three_ref, mlp_ref, xq_ref, own_ref, send_ref = rest[3 * n :]
        normed = rms(two_ref[...], gains_ref[3:4])[0].astype(BF)
        own_ref[:, :channels] = normed
        send_ref[:, :channels] = normed
        three_ref[...] = two_ref[...]
        for j in range(n):
            xq_ref[j] = dot_nn(normed, cq_r[j][...]).astype(BF)
            heads = []
            for h in range(share // HD):
                q = xq_ref[j, :, h * HD : (h + 1) * HD]
                k = ckv_r[j][:, h * HD : (h + 1) * HD]
                v = ckv_r[j][:, share + h * HD : share + (h + 1) * HD]
                heads.append(dot_tn(v, cross_prob(q, k).astype(BF)))
            side_ref, cut = side_slot(own_ref, send_ref, j, channels, share)
            side_ref[:, cut] = jnp.concatenate(heads).T.astype(BF)
            three_ref[...] += dot_nn(side_ref[:, cut], co_r[j][...])
        mlp_ref[...] = rms(three_ref[...], gains_ref[4:5])[0].astype(BF)

    return pl.pallas_call(
        body,
        out_shape=[
            jax.ShapeDtypeStruct((points, channels), F),
            jax.ShapeDtypeStruct((points, channels), BF),
            jax.ShapeDtypeStruct((n, points, share), BF),
        ]
        + [jax.ShapeDtypeStruct((points, channels + n // 2 * share), BF)] * 2,
        compiler_params=params(),
        cost_estimate=pl.CostEstimate(
            flops=5 * points * channels * channels,
            bytes_accessed=8 * channels * channels,
            transcendentals=points * channels,
        ),
        name="cross_forward",
    )(two, gains, *cq, *co, *ckv)


def mlp_core(inputs, grad_out, up, down):
    count = len(inputs)
    points, channels = inputs[0].shape
    hidden = up.shape[1]
    tile = min(hidden, 256)
    steps = hidden // tile
    rows = count * points

    def body(*refs):
        x_r, g_r = refs[:count], refs[count : 2 * count]
        up_ref, down_ref, act_ref, gi_ref = refs[2 * count : 2 * count + 4]
        back_r = refs[2 * count + 4 : 3 * count + 4]
        x_all, g_all, acc = refs[3 * count + 4 :]
        step = pl.program_id(0)

        @pl.when(step == 0)
        def _():
            for j in range(count):
                x_all[j * points : (j + 1) * points] = x_r[j][...]
                g_all[j * points : (j + 1) * points] = g_r[j][...]
            acc[...] = jnp.zeros_like(acc)

        inner = dot_nn(x_all[...], up_ref[...])
        gate = sigmoid(inner)
        act_ref[...] = (inner * gate).astype(BF)
        grad_act = dot_nt(g_all[...], down_ref[...])
        gi_ref[...] = (grad_act * (gate * (1.0 + inner * (1.0 - gate)))).astype(BF)
        acc[...] += dot_nt(gi_ref[...], up_ref[...])

        @pl.when(step == steps - 1)
        def _():
            for j in range(count):
                back_r[j][...] = acc[j * points : (j + 1) * points].astype(BF)

    block = pl.BlockSpec((points, channels), lambda i: (0, 0))
    return pl.pallas_call(
        body,
        grid=(steps,),
        in_specs=[block] * (2 * count)
        + [
            pl.BlockSpec((channels, tile), lambda i: (0, i)),
            pl.BlockSpec((tile, channels), lambda i: (i, 0)),
        ],
        out_specs=[pl.BlockSpec((rows, tile), lambda i: (0, i))] * 2 + [block] * count,
        out_shape=[jax.ShapeDtypeStruct((rows, hidden), BF)] * 2
        + [jax.ShapeDtypeStruct((points, channels), BF)] * count,
        scratch_shapes=[
            pltpu.VMEM((rows, channels), BF),
            pltpu.VMEM((rows, channels), BF),
            pltpu.VMEM((rows, channels), F),
        ],
        compiler_params=params(),
        cost_estimate=pl.CostEstimate(
            flops=6 * rows * channels * hidden,
            bytes_accessed=4 * channels * hidden,
            transcendentals=rows * hidden,
        ),
        name="mlp_core",
    )(*inputs, *grad_out, up, down)


def mlp_rest(inputs, grad_out, grad_inner, acts, down):
    n = len(inputs)
    points, channels = inputs[0].shape
    hidden = acts[0].shape[1]
    tile = min(hidden, 256)
    groups = len(acts)
    each = n // groups

    def body(down_ref, *rest):
        x_r, go_r = rest[:n], rest[n : 2 * n]
        gi_r, act_r = rest[2 * n : 2 * n + groups], rest[2 * n + groups : 2 * n + 2 * groups]
        outs, dw_ref = rest[2 * n + 2 * groups : 3 * n + 2 * groups], rest[3 * n + 2 * groups]
        turned = rest[3 * n + 2 * groups + 1]
        for j in range(n):
            cut = slice(j % each * points, (j % each + 1) * points)
            outs[j][...] = dot_nn(act_r[j // each][cut], down_ref[...]).astype(BF)
        for side, refs, other in ((0, x_r, gi_r), (1, go_r, act_r)):
            for j in range(n):
                turned[:, j * points : (j + 1) * points] = refs[j][...].T
            for c in range(hidden // tile):
                cut = slice(c * tile, (c + 1) * tile)
                total = None
                for g in range(groups):
                    span = each * points
                    p = dot_nn(turned[:, g * span : (g + 1) * span], other[g][:, cut])
                    total = p if total is None else total + p
                at = side * hidden + c * tile
                dw_ref[:, at : at + tile] = total.astype(BF)

    return pl.pallas_call(
        body,
        out_shape=[jax.ShapeDtypeStruct((points, channels), BF)] * n
        + [jax.ShapeDtypeStruct((channels, 2 * hidden), BF)],
        scratch_shapes=[pltpu.VMEM((channels, n * points), BF)],
        compiler_params=params(),
        cost_estimate=pl.CostEstimate(
            flops=6 * n * points * channels * hidden,
            bytes_accessed=16 * channels * hidden,
            transcendentals=0,
        ),
        name="mlp_rest",
    )(down, *inputs, *grad_out, *grad_inner, *acts)


def cross_backward(grad_norm, grad_four, three, two, gains, xq, cq, co, ckv):
    points, channels = three.shape
    n, _, share = xq.shape
    tokens = ckv[0].shape[0]

    def body(gn_ref, g4_ref, three_ref, two_ref, in_ref, xq_ref, *rest):
        cq_r, co_r, ckv_r = (rest[i * n : (i + 1) * n] for i in range(3))
        two_out, gains_ref, own_ref, send_ref = rest[3 * n : 3 * n + 4]
        dkv_r = rest[3 * n + 4 : 4 * n + 4]
        back, gain = rms_back(three_ref[...], in_ref[4:5], gn_ref[...])
        gains_ref[0:1] = gain
        grad_three = g4_ref[...] + back
        gb = grad_three.astype(BF)
        own_ref[:, :channels] = gb
        send_ref[:, :channels] = gb
        grad_norm2 = jnp.zeros((points, channels), F)
        for j in range(n):
            ga = dot_nt(gb, co_r[j][...]).astype(BF)
            kv = ckv_r[j][...]
            gq, gk, gv = [], [], []
            for h in range(share // HD):
                q = xq_ref[j, :, h * HD : (h + 1) * HD]
                k = kv[:, h * HD : (h + 1) * HD]
                v = kv[:, share + h * HD : share + (h + 1) * HD]
                g = ga[:, h * HD : (h + 1) * HD]
                p = cross_prob(q, k)
                gp = dot_nt(v, g)
                gs = p * (gp - jnp.sum(p * gp, axis=0, keepdims=True))
                raw = (gs * (1.0 / math.sqrt(HD))).astype(BF)
                gq.append(dot_tn(k, raw))
                gk.append(dot_nn(raw, q).astype(BF))
                gv.append(dot_nn(p.astype(BF), g).astype(BF))
            side_ref, cut = side_slot(own_ref, send_ref, j, 2 * channels, share)
            side_ref[:, cut] = jnp.concatenate(gq).T.astype(BF)
            dkv_r[j][...] = jnp.concatenate(gk + gv, axis=1)
            grad_norm2 = grad_norm2 + dot_nt(side_ref[:, cut], cq_r[j][...])
        back, gain = rms_back(two_ref[...], in_ref[3:4], grad_norm2)
        gains_ref[1:2] = gain
        two_out[...] = grad_three + back
        gb = two_out[...].astype(BF)
        own_ref[:, channels : 2 * channels] = gb
        send_ref[:, channels : 2 * channels] = gb

    return pl.pallas_call(
        body,
        out_shape=[
            jax.ShapeDtypeStruct((points, channels), F),
            jax.ShapeDtypeStruct((2, channels), F),
        ]
        + [jax.ShapeDtypeStruct((points, 2 * channels + n // 2 * share), BF)] * 2
        + [jax.ShapeDtypeStruct((tokens, 2 * share), BF)] * n,
        compiler_params=params(),
        cost_estimate=pl.CostEstimate(
            flops=8 * points * channels * channels,
            bytes_accessed=12 * channels * channels,
            transcendentals=points * channels,
        ),
        name="cross_backward",
    )(grad_norm, grad_four, three, two, gains, xq, *cq, *co, *ckv)


def attn_backward(place, grad_two, conv, noise, gains, qkv, token_grads, wqkv, wo, width):
    points, channels = grad_two.shape
    n = len(wo)
    share = wo[0].shape[0]
    tokens = token_grads[0].shape[0]

    def body(place_ref, g2_ref, conv_ref, noise_ref, gains_ref, qkv_ref, *rest):
        wqkv_r, wo_r, token_r = (rest[i * n : (i + 1) * n] for i in range(3))
        sums_ref = rest[3 * n]
        share_r = rest[3 * n + 1 : 4 * n + 1]
        own_ref, send_ref, gc_ref, wide, out_w, saved, wide_sem, out_sem, saved_sem = rest[4 * n + 1 :]
        wide_copies, take_wide = fetch(wqkv_r, wide, wide_sem)
        out_copies, take_out = fetch(wo_r, out_w, out_sem)
        saved_copies, take_saved = fetch([qkv_ref.at[j] for j in range(n)], saved, saved_sem)
        for trio in zip(out_copies, saved_copies, wide_copies):
            for c in trio:
                c.start()
        here = place_ref[0]
        grad_two = g2_ref[...]
        gb = grad_two.astype(BF)
        out = conv_ref[...].astype(F) + gains_ref[0:1] * noise_ref[...] + gains_ref[1:2]
        one = out * sigmoid(out)
        grad_norm = jnp.zeros((points, channels), F)
        for j in range(n):
            ga = dot_nt(gb, take_out(j)).astype(BF)
            take_saved(j)
            gq, gk, gv = [], [], []
            for h in range(share // HD):
                q, k, v = (
                    saved[j, :, i * share + h * HD : i * share + (h + 1) * HD] for i in range(3)
                )
                g = ga[:, h * HD : (h + 1) * HD]
                p = self_prob(q, k)
                gp = dot_nt(v, g)
                gs = p * (gp - jnp.sum(p * gp, axis=0, keepdims=True))
                square = jnp.sum(gs, axis=1, keepdims=True) * (-1.0 / math.sqrt(HD))
                raw = (gs * (2.0 / math.sqrt(HD))).astype(BF)
                gq.append(dot_tn(k, raw))
                gk.append((dot_nn(raw, q) + 2.0 * k.astype(F) * square).astype(BF))
                gv.append(dot_nn(p.astype(BF), g).astype(BF))
            side_ref, cut = side_slot(own_ref, send_ref, j, 0, 3 * share)
            gq = jnp.concatenate(gq).T.astype(BF)
            side_ref[:, cut] = jnp.concatenate([gq] + gk + gv, axis=1)
            grad_norm = grad_norm + dot_nt(side_ref[:, cut], take_wide(j))
        back, gain = rms_back(one, gains_ref[2:3], grad_norm)
        grad_conv = (grad_two + back) * silu_slope(out)
        gc_ref[...] = grad_conv.astype(BF)
        for j in range(n):
            start = pl.multiple_of(lax.bitwise_xor(here, j) * width, width)
            share_r[j][:points] = gc_ref[:, pl.ds(start, width)]
            for i in range(2):
                rows = slice(points + i * tokens, points + (i + 1) * tokens)
                share_r[j][rows] = token_r[j][:, i * width : (i + 1) * width]
        sums_ref[0:1] = gain
        sums_ref[1:2] = jnp.sum(grad_conv, axis=0, keepdims=True)
        sums_ref[2:3] = jnp.sum(grad_conv * noise_ref[...], axis=0, keepdims=True)

    return pl.pallas_call(
        body,
        out_shape=[
            jax.ShapeDtypeStruct((3, channels), F),
        ]
        + [jax.ShapeDtypeStruct((points + 2 * tokens, width), BF)] * n
        + [jax.ShapeDtypeStruct((points, n // 2 * 3 * share), BF)] * 2,
        in_specs=[smem()] + vmem(4) + anywhere(1 + 2 * n) + vmem(n),
        scratch_shapes=[
            pltpu.VMEM((points, channels), BF),
            pltpu.VMEM((n, channels, 3 * share), BF),
            pltpu.VMEM((n, share, channels), BF),
            pltpu.VMEM((n, points, 3 * share), BF),
            pltpu.SemaphoreType.DMA((n,)),
            pltpu.SemaphoreType.DMA((n,)),
            pltpu.SemaphoreType.DMA((n,)),
        ],
        compiler_params=params(),
        cost_estimate=pl.CostEstimate(
            flops=24 * points * channels * channels,
            bytes_accessed=24 * channels * channels,
            transcendentals=points * points * channels // HD,
        ),
        name="attn_backward",
    )(place, grad_two, conv, noise, gains, qkv, *wqkv, *wo, *token_grads)


def turn(turned, blocks, start, channels):
    points = blocks[0].shape[0]
    for i, block in enumerate(blocks):
        turned[:, i * points : (i + 1) * points] = block[:, start : start + channels].T


def pair_product(turned, blocks, cut):
    points = blocks[0].shape[0]
    total = None
    for i, block in enumerate(blocks):
        p = dot_nn(turned[:, i * points : (i + 1) * points], block[:, cut])
        total = p if total is None else total + p
    return total.astype(BF)


def cross_weights(attn_pair, cross_pair, grad_pair, count, share):
    points = attn_pair[0].shape[0]
    channels = attn_pair[0].shape[1] - count * share

    def body(*refs):
        attn, cross, grad = refs[:2], refs[2:4], refs[4:6]
        out, last = refs[6 : 6 + count], refs[6 + count : 6 + 2 * count]
        turned = refs[-1]
        turn(turned, cross, 0, channels)
        for i in range(count):
            cut = slice(2 * channels + i * share, 2 * channels + (i + 1) * share)
            out[i][:, :share] = pair_product(turned, grad, cut)
        turn(turned, grad, 0, channels)
        for i in range(count):
            cut = slice(channels + i * share, channels + (i + 1) * share)
            out[i][:, share:] = pair_product(turned, cross, cut)
        turn(turned, grad, channels, channels)
        for i in range(count):
            cut = slice(channels + i * share, channels + (i + 1) * share)
            last[i][...] = pair_product(turned, attn, cut)

    return pl.pallas_call(
        body,
        out_shape=[jax.ShapeDtypeStruct((channels, 2 * share), BF)] * count
        + [jax.ShapeDtypeStruct((channels, share), BF)] * count,
        scratch_shapes=[pltpu.VMEM((channels, 2 * points), BF)],
        compiler_params=params(),
        cost_estimate=pl.CostEstimate(
            flops=12 * count * points * channels * share,
            bytes_accessed=20 * points * channels,
            transcendentals=0,
        ),
        name="cross_weights",
    )(*attn_pair, *cross_pair, *grad_pair)


def attn_weights(attn_pair, grad_pair, count, share):
    points = attn_pair[0].shape[0]
    channels = attn_pair[0].shape[1] - count * share

    def body(*refs):
        attn, grad = refs[:2], refs[2:4]
        out, last, turned = refs[4 : 4 + count], refs[4 + count : 4 + 2 * count], refs[-1]
        turn(turned, attn, 0, channels)
        for i in range(count):
            at = 3 * i * share
            out[i][...] = pair_product(turned, grad, slice(at, at + 2 * share))
            last[i][...] = pair_product(turned, grad, slice(at + 2 * share, at + 3 * share))

    return pl.pallas_call(
        body,
        out_shape=[jax.ShapeDtypeStruct((channels, 2 * share), BF)] * count
        + [jax.ShapeDtypeStruct((channels, share), BF)] * count,
        scratch_shapes=[pltpu.VMEM((channels, 2 * points), BF)],
        compiler_params=params(),
        cost_estimate=pl.CostEstimate(
            flops=12 * count * points * channels * share,
            bytes_accessed=16 * points * channels,
            transcendentals=0,
        ),
        name="attn_weights",
    )(*attn_pair, *grad_pair)


def phase_order(points, side):
    row = lax.broadcasted_iota(jnp.int32, (points, points), 0)
    lane = lax.broadcasted_iota(jnp.int32, (points, points), 1)
    line, place = phase_place(row, side)
    return lane == 2 * side * line + place


def phase_place(row, side):
    phase, spot = row // (side * side), row % (side * side)
    return 2 * (spot // side) + phase // 2, 2 * (spot % side) + phase % 2


def phase_masks(side):
    shape = (4 * side * side, 2 * side)
    row = lax.broadcasted_iota(jnp.int32, shape, 0)
    lane = lax.broadcasted_iota(jnp.int32, shape, 1)
    line, place = phase_place(row, side)
    return jnp.where(lane == line, 1.0, 0.0), jnp.where(lane == place, 1.0, 0.0)


def cotangents(place, counts, features, image, noise, vectors, colors, code, rgb, side):
    points, channels = features.shape
    count = len(vectors)
    exact = dict(precision=lax.Precision.HIGHEST, preferred_element_type=F)
    along = (((1,), (0,)), ((), ()))

    def body(place_ref, live_ref, f_ref, im_ref, n_ref, col_ref, c_ref, rgb_ref, *rest):
        vec_r = rest[:count]
        four_ref, low_ref, gi_ref, no_ref, cs_ref, gains_ref = rest[count:]
        for i in range(count):
            gains_ref[i : i + 1] = vec_r[i][...].astype(F).reshape(1, channels)
        order = jnp.where(phase_order(points, side), 1.0, 0.0).astype(BF)
        by = live_ref[place_ref[0]].astype(F)
        lines, places = phase_masks(side)

        def column(v):
            rows = lax.dot_general(lines, v, along, **exact)
            return jnp.sum(rows * places, axis=1, keepdims=True)

        no_ref[...] = column(n_ref[0].astype(F))
        scale = dot_nn(c_ref[...], rgb_ref[...])[:1] + 1.0
        cs_ref[...] = scale
        four = dot_nn(order, f_ref[...]) * by
        col = col_ref[...].astype(F)
        for c in range(3):
            gi = column(im_ref[0, c]) * by
            gi_ref[:, c : c + 1] = gi
            four = four + gi * (col[c : c + 1] * scale)
        four_ref[...] = four
        low_ref[...] = four.astype(BF)

    return pl.pallas_call(
        body,
        in_specs=[smem(), smem()] + vmem(6 + count),
        out_shape=[
            jax.ShapeDtypeStruct((points, channels), F),
            jax.ShapeDtypeStruct((points, channels), BF),
            jax.ShapeDtypeStruct((points, 3), F),
            jax.ShapeDtypeStruct((points, 1), F),
            jax.ShapeDtypeStruct((1, channels), F),
            jax.ShapeDtypeStruct((count, channels), F),
        ],
        compiler_params=params(),
        name="cotangents",
    )(place, counts, features, image, noise, colors, code, rgb, *vectors)


def class_tokens(rows, pos, ck, cv):
    n = rows.shape[0]
    tokens, channels = pos.shape
    share = ck.shape[1]

    def body(r_ref, p_ref, ck_ref, cv_ref, ctx_ref, *out_r):
        pos = p_ref[...].astype(F)
        rows = r_ref[...].astype(F)
        for j in range(n):
            ctx_ref[j * tokens : (j + 1) * tokens] = (rows[j : j + 1] + pos).astype(BF)
        for w, at in ((ck_ref, 0), (cv_ref, share)):
            product = dot_nn(ctx_ref[...], w[...])
            for j in range(n):
                out_r[j][:, at : at + share] = product[j * tokens : (j + 1) * tokens].astype(BF)

    return pl.pallas_call(
        body,
        out_shape=[jax.ShapeDtypeStruct((n * tokens, channels), BF)]
        + [jax.ShapeDtypeStruct((tokens, 2 * share), BF)] * n,
        compiler_params=params(),
        name="class_tokens",
    )(rows, pos, ck, cv)


def band_prepare(place, received, codes, select, style, rows, pos, points_low):
    n_dp, _, band = received.shape
    samples, depth = codes.shape
    kernels = select.shape[0]
    low = n_dp * points_low // samples
    columns = samples * low
    step = 8

    tokens = pos.shape[0]

    def body(place_ref, x_ref, c_ref, sel_ref, sty_ref, r_ref, p_ref, *rest):
        at_ref, mix_ref, scale_ref, left_ref, ctx_ref, turned, held = rest
        pos_rows = p_ref[...].astype(F)
        class_rows = r_ref[...].astype(F)
        for s in range(samples):
            both = class_rows[s : s + 1] + pos_rows
            held[s * tokens : (s + 1) * tokens] = both.astype(BF).astype(F)
        ctx_ref[...] = held[...].T.astype(BF)
        logits = dot_nt(c_ref[...], sel_ref[...])
        e = jnp.exp(logits - jnp.max(logits, axis=1, keepdims=True))
        mixing = e / jnp.sum(e, axis=1, keepdims=True)
        mix_ref[...] = mixing
        scale_ref[...] = dot_nn(c_ref[...], sty_ref[...]) + 1.0
        scale_turned = scale_ref[...].T
        mix_turned = mixing.T
        for r in range(kernels // 2 + 1):
            ahead = jnp.concatenate([mix_turned[r:], mix_turned[:r]]) if r else mix_turned
            both = 2.0 * mix_turned * ahead
            left = (scale_turned * scale_turned)[:, None, :] * both[None]
            left_ref[r] = left.reshape(band * kernels, samples).astype(BF)
        for b in range(n_dp):
            turned[:, b * points_low : (b + 1) * points_low] = x_ref[b, :points_low].astype(F).T
        row = lax.broadcasted_iota(jnp.int32, (samples, columns), 0)
        lane = lax.broadcasted_iota(jnp.int32, (samples, columns), 1)
        repeat = jnp.where(lane // low == row, 1.0, 0.0).astype(BF)
        high = mixing.astype(BF)
        rest = (mixing - high.astype(F)).astype(BF)
        wide = dot_tn(high, repeat) + dot_tn(rest, repeat)
        for i in range(band // step):
            x = turned[i * step : (i + 1) * step]
            a = (x[:, None, :] * wide[None]).reshape(step * kernels, columns)
            at_ref[i * step * kernels : (i + 1) * step * kernels] = a.astype(BF)

    return pl.pallas_call(
        body,
        in_specs=[smem()] + vmem(6),
        out_shape=[
            jax.ShapeDtypeStruct((band * kernels, columns), BF),
            jax.ShapeDtypeStruct((samples, kernels), F),
            jax.ShapeDtypeStruct((samples, band), F),
            jax.ShapeDtypeStruct((kernels // 2 + 1, band * kernels, samples), BF),
            jax.ShapeDtypeStruct((band, samples * tokens), BF),
        ],
        scratch_shapes=[pltpu.VMEM((band, columns), F), pltpu.VMEM((samples * tokens, band), F)],
        compiler_params=params(),
        name="band_prepare",
    )(place, received, codes, select, style, rows, pos)


def side_outputs(place, three, branch, image_grad, color_scale, colors, bias, tokens, shares, ck, cv, gains, late, count_sums, count_all, side):
    points, channels = three.shape
    n, parts = len(shares), len(branch)
    share = ck.shape[1]
    low = side * side
    exact = dict(precision=lax.Precision.HIGHEST, preferred_element_type=F)

    def body(place_ref, bias_ref, three_ref, gi_ref, cs_ref, col_ref, ck_ref, cv_ref, gains_ref, late_ref, *rest):
        branch_r, share_r = rest[:parts], rest[parts : parts + n]
        feat_ref, color_ref, pack_ref, four_ref, keys, values = rest[parts + n :]
        here = place_ref[0]
        four = three_ref[...]
        for b in branch_r:
            four = four + b[...].astype(F)
        four_ref[...] = four
        order = jnp.where(phase_order(points, side), 1.0, 0.0)
        moved = lax.dot_general(order, four, (((0,), (0,)), ((), ())), **exact)
        feat_ref[...] = moved.reshape(1, 2 * side, 2 * side, channels)
        scale, col = cs_ref[...], col_ref[...].astype(F)
        tint = col * scale
        color = lax.dot_general(four_ref[...], tint, (((1,), (1,)), ((), ())), **exact)
        lines, places = phase_masks(side)
        for c in range(3):
            spread_out = color[:, c : c + 1] * places
            color_ref[0, c] = bias_ref[c] + lax.dot_general(
                lines, spread_out, (((0,), (0,)), ((), ())), **exact
            )
        gi = gi_ref[...]
        image = lax.dot_general(gi, four_ref[...], (((0,), (0,)), ((), ())), **exact)
        for j in range(n):
            cut = slice(j * tokens, (j + 1) * tokens)
            keys[cut] = share_r[j][points : points + tokens]
            values[cut] = share_r[j][points + tokens : points + 2 * tokens]
        grad = dot_nt(keys[...], ck_ref[...]) + dot_nt(values[...], cv_ref[...])
        pack_ref[...] = jnp.zeros_like(pack_ref)
        total = None
        for j in range(n):
            part = grad[j * tokens : (j + 1) * tokens]
            total = part if total is None else total + part
            row = count_sums + 2 * n + lax.bitwise_xor(here, j)
            pack_ref[pl.ds(row, 1)] = jnp.sum(part, axis=0, keepdims=True)
        pack_ref[:tokens] = total
        pack_ref[tokens : tokens + 2] = gains_ref[...]
        pack_ref[tokens + 2 : tokens + 5] = image * scale
        lane = lax.broadcasted_iota(jnp.int32, (1, channels), 1)
        row = jnp.zeros((1, channels), F)
        for c in range(3):
            row = jnp.where(lane == c, jnp.sum(gi[:, c : c + 1]), row)
        pack_ref[tokens + 5 : tokens + 6] = row
        pack_ref[tokens + 6 : tokens + 9] = late_ref[...]
        pack_ref[pl.ds(count_sums + 3 * n + here, 1)] = jnp.sum(image * col, axis=0, keepdims=True)

    return pl.pallas_call(
        body,
        in_specs=[smem(), smem()] + vmem(8 + parts + n),
        out_shape=[
            jax.ShapeDtypeStruct((1, 2 * side, 2 * side, channels), F),
            jax.ShapeDtypeStruct((1, 3, 2 * side, 2 * side), F),
            jax.ShapeDtypeStruct((count_all, channels), F),
        ],
        scratch_shapes=[
            pltpu.VMEM((points, channels), F),
            pltpu.VMEM((n * tokens, share), BF),
            pltpu.VMEM((n * tokens, share), BF),
        ],
        compiler_params=params(),
        name="side_outputs",
    )(place, bias, three, image_grad, color_scale, colors, ck, cv, gains, late, *branch, *shares)


def late_sums_kernel(place, scale, pack, low_parts, images, own_scale, energy, mixing_sum, mixing, count_sums, at_sum):
    low, channels = images.shape
    parts = len(low_parts)
    n, kernels = mixing.shape
    rows = mixing_sum.shape[0]

    def body(place_ref, scale_ref, pack_ref, im_ref, own_ref, en_ref, ms_ref, mix_ref, *rest):
        low_r, (out_ref, grad_ref) = rest[:parts], rest[parts:]
        here = place_ref[0]
        total = low_r[0][...].astype(F)
        for v in low_r[1:]:
            total = total + v[...].astype(F)
        grad_ref[...] = total * (own_ref[0:1] * scale_ref[0])
        out_ref[...] = pack_ref[...]
        line = jnp.sum(total * im_ref[...].astype(F), axis=0, keepdims=True)
        out_ref[pl.ds(count_sums + here, 1)] = line
        out_ref[count_sums + n : count_sums + 2 * n] = en_ref[...]
        out_ref[at_sum : at_sum + rows] = ms_ref[...]
        wide = split_dot(mix_ref[...], tile_mask(channels // kernels, kernels))
        lane = lax.broadcasted_iota(jnp.int32, (n, channels), 1) // kernels
        row = lax.bitwise_xor(lax.broadcasted_iota(jnp.int32, (n, channels), 0), here)
        line = jnp.sum(jnp.where(lane == row, wide, 0.0), axis=0, keepdims=True)
        out_ref[count_sums + 4 * n : count_sums + 4 * n + 1] = line

    return pl.pallas_call(
        body,
        in_specs=[smem(), smem()] + vmem(6 + parts),
        out_shape=[
            jax.ShapeDtypeStruct(pack.shape, F),
            jax.ShapeDtypeStruct((low, channels), F),
        ],
        compiler_params=params(),
        name="late_sums",
    )(place, scale, pack, images, own_scale, energy, mixing_sum, mixing, *low_parts)


def style_final(places, scale, mixing_grad, scale_grad, rgb_grad, tokens, codes, labels, select, style, rgb, classes, group):
    samples, channels = scale_grad.shape
    kernels, depth = select.shape

    def body(place_ref, s_ref, mg_ref, sg_ref, rg_ref, t_ref, c_ref, l_ref, sel_ref, sty_ref, rgb_ref, *outs):
        dsel_ref, dsty_ref, drgb_ref, dcodes_ref, table_ref, held = outs
        by = s_ref[0]
        codes = c_ref[...]
        logits = dot_nt(codes, sel_ref[...])
        e = jnp.exp(logits - jnp.max(logits, axis=1, keepdims=True))
        mixing = e / jnp.sum(e, axis=1, keepdims=True)
        mg = mg_ref[...] * by
        logit = (mixing * (mg - jnp.sum(mixing * mg, axis=1, keepdims=True))).astype(BF)
        sg = (sg_ref[...] * by).astype(BF)
        rg = (rg_ref[...] * by).astype(BF)
        dsel_ref[...] = dot_tn(logit, codes)
        dsty_ref[...] = dot_tn(codes, sg)
        drgb_ref[...] = dot_tn(codes, rg)
        held[...] = (
            dot_nn(logit, sel_ref[...]) + dot_nt(sg, sty_ref[...]) + dot_nt(rg, rgb_ref[...])
        )
        for j in range(group):
            dcodes_ref[j : j + 1] = held[pl.ds(place_ref[1] * group + j, 1)]
        ids = lax.broadcasted_iota(jnp.int32, (samples, classes), 1)
        one_hot = jnp.where(ids == l_ref[...], 1.0, 0.0).astype(BF)
        t = t_ref[...] * by
        high = t.astype(BF)
        rest = (t - high.astype(F)).astype(BF)
        table_ref[...] = dot_tn(one_hot, high) + dot_tn(one_hot, rest)

    return pl.pallas_call(
        body,
        in_specs=[smem(), smem()] + vmem(9),
        out_shape=[
            jax.ShapeDtypeStruct((kernels, depth), F),
            jax.ShapeDtypeStruct((depth, channels), F),
            jax.ShapeDtypeStruct((depth, channels), F),
            jax.ShapeDtypeStruct((group, depth), F),
            jax.ShapeDtypeStruct((classes, channels), F),
        ],
        scratch_shapes=[pltpu.VMEM((samples, depth), F)],
        compiler_params=params(),
        name="style_final",
    )(places, scale, mixing_grad, scale_grad, rgb_grad, tokens, codes, labels, select, style, rgb)


def local(
    images,
    styles,
    labels,
    noise_map,
    counts,
    cot_features,
    cot_image,
    kernel_bank,
    select_proj,
    style_proj,
    conv_bias,
    noise_gain,
    norm_attn,
    query_proj,
    key_proj,
    value_proj,
    out_proj,
    norm_cross,
    cross_query,
    cross_key,
    cross_value,
    cross_out,
    class_table,
    class_pos,
    norm_mlp,
    up_proj,
    down_proj,
    rgb_style,
    color_projection,
    color_bias,
):
    n, n_dp = lax.axis_size("rows"), lax.axis_size("dp")
    r, d = lax.axis_index("rows"), lax.axis_index("dp")
    side, channels = images.shape[1], images.shape[3]
    low = side * side
    points = 4 * low
    kernels, width = kernel_bank.shape[3], kernel_bank.shape[4]
    tokens = class_pos.shape[0]
    share = query_proj.shape[1]
    band = channels // n_dp
    samples = n * n_dp

    def by_phase(field):
        rest = field.shape[2:]
        split = field.reshape((side, 2, side, 2) + rest)
        order = (1, 3, 0, 2) + tuple(range(4, 4 + len(rest)))
        return split.transpose(order).reshape((points,) + rest)

    group_order = jnp.arange(n, dtype=jnp.int32) ^ r
    slots = jnp.arange(n_dp, dtype=jnp.int32)

    def tie_lists(*lists):
        flat = tie(*[v for part in lists for v in part])
        out = []
        for part in lists:
            out.append(list(flat[: len(part)]))
            flat = flat[len(part) :]
        return out

    def far_swaps(m):
        return [swap(m, "rows", j) for j in range(2, n, 2)]

    def near_swaps(blocks):
        return [swap(b, "rows", 1) for b in blocks]

    def whole(m, far_m, near_m):
        out = [None] * n
        out[::2] = [m] + far_m
        out[1::2] = near_m
        return out

    half = n // 2
    own_images = images[0].reshape(low, channels)
    codes = jnp.take(styles, jnp.arange(max(n, 8), dtype=jnp.int32) % n ^ r, axis=0)
    image_blocks = spread(own_images)
    depth, points_low = styles.shape[1], n * low
    label_rows = jnp.stack([labels // 256, labels % 256, counts]).astype(BF)
    payload = jnp.concatenate([styles.reshape(-1), label_rows.reshape(-1)])
    block = min(channels, 128)
    payload = jnp.pad(payload, (0, -payload.shape[0] % (16 * block))).reshape(-1, block)
    qkv_proj = jnp.concatenate([query_proj, key_proj, value_proj], axis=1)
    image_blocks, (codes, qkv_proj) = tie_lists(image_blocks, [codes, qkv_proj])
    qkv_far = far_swaps(qkv_proj)
    wo_far = far_swaps(out_proj)
    near = [near_swaps([m])[0] for m in (qkv_proj, out_proj)]
    select_turned = select_proj.T
    *conv_part, conv_raw, demod, xs, mixing, scale_in = conv_forward(
        codes, select_turned, style_proj, payload, image_blocks, kernel_bank, side
    )

    places = jnp.stack([r, d]).astype(jnp.int32)
    conv_part[0], places = tie(conv_part[0], places)
    pairs = bank_pairs(places, kernel_bank, band)

    later = [styles, labels, counts, cot_features, cot_image, noise_map, conv_bias, noise_gain]
    later += [norm_attn, norm_cross, norm_mlp, class_table, class_pos, cross_key, cross_value]
    later += [rgb_style, color_projection, color_bias, out_proj, cross_query, cross_out, xs]
    conv_part, (pairs,), later, qkv_far, wo_far, near = tie_lists(
        conv_part, [pairs], later, qkv_far, wo_far, near
    )
    styles, labels, counts, cot_features, cot_image, noise_map, conv_bias, noise_gain = later[:8]
    norm_attn, norm_cross, norm_mlp, class_table, class_pos, cross_key, cross_value = later[8:15]
    rgb_style, color_projection, color_bias, out_proj, cross_query, cross_out, xs = later[15:]

    parts = [conv_part[0]] + [swap(conv_part[j], "rows", j) for j in range(1, n)]
    qkv_near = near[:1] + near_swaps(qkv_far)
    wo_near = near[1:2] + near_swaps(wo_far)
    place = r.astype(jnp.int32).reshape(1)
    colors = color_projection.T
    grad_four, grad_four_low, grad_image, noise, color_scale, gains = cotangents(
        place,
        counts,
        cot_features.reshape(points, channels),
        cot_image,
        noise_map,
        (noise_gain, conv_bias, norm_attn, norm_cross, norm_mlp),
        colors,
        codes,
        rgb_style,
        side,
    )
    parts, qkv_near, wo_near, rest = tie_lists(
        parts,
        qkv_near,
        wo_near,
        [grad_four, grad_four_low, grad_image, color_scale, noise, gains]
        + [xs, labels, class_table, out_proj],
    )
    grad_four, grad_four_low, grad_image, color_scale, noise, gains = rest[:6]
    xs, labels, class_table, out_proj = rest[6:]

    if band == block:
        bands = xs
    else:
        split = xs[:, :points_low].reshape(xs.shape[0], points_low, block // band, band)
        split = split.transpose(0, 2, 1, 3).reshape(n_dp, points_low, band)
        rest = jnp.broadcast_to(payload.reshape(1, -1, band), (n_dp, payload.size // band, band))
        bands = jnp.concatenate([split, rest], axis=1)
    received = lax.all_to_all(bands, "dp", 0, 0, tiled=True)
    wqkv = whole(qkv_proj, qkv_far, qkv_near)
    wo = whole(out_proj, wo_far, wo_near)
    conv, two, qkv, attn_own, attn_sent = attn_forward(place, parts, noise, gains, wqkv, wo)
    cq_far = far_swaps(cross_query)
    cross_near_own = near_swaps([cross_query, cross_out])
    (two, received, labels, class_table), cq_far, cross_near_own = tie_lists(
        [two, received, labels, class_table], cq_far, cross_near_own
    )

    co_far = far_swaps(cross_out)
    flat_context, *ckv = class_tokens(
        jnp.take(class_table, jnp.take(labels, group_order), axis=0), class_pos, cross_key, cross_value
    )
    ckv = [ckv[0]] + [swap(ckv[j], "rows", j) for j in range(1, n)]
    cq = whole(cross_query, cq_far, cross_near_own[:1] + near_swaps(cq_far))
    codes_back = received[:, points_low:].reshape(n_dp, -1)
    styles_all = codes_back[:, : n * depth].reshape(samples, depth)
    label_back = codes_back[:, n * depth : n * depth + 3 * n]
    label_back = label_back.reshape(n_dp, 3, n).astype(jnp.int32)
    inverse = (1.0 / jnp.sum(label_back[:, 2]).astype(F)).reshape(1)
    labels_all = (label_back[:, 0] * 256 + label_back[:, 1]).reshape(samples, 1)
    codes_all = jnp.take(styles_all.reshape(n_dp, n, depth), group_order, axis=1)
    band_proj = lax.dynamic_slice_in_dim(style_proj, d * band, band, axis=1)
    labels_ring = jnp.take(labels_all.reshape(n_dp, n), group_order, axis=1).reshape(samples)
    rows_band = jnp.take(class_table, labels_ring, axis=0)
    rows_band = lax.dynamic_slice_in_dim(rows_band, d * band, band, axis=1)
    pos_band = lax.dynamic_slice_in_dim(class_pos, d * band, band, axis=1)
    bands_ready = band_prepare(
        place, received, codes_all.reshape(samples, depth), select_turned, band_proj, rows_band, pos_band, points_low
    )
    (two,), co_far, cq, ckv, bands_ready, ready = tie_lists(
        [two], co_far, cq, ckv, bands_ready, [styles_all, labels_all, inverse]
    )
    at, mixing_all, scale_band, lefts, context_band = bands_ready
    styles_all, labels_all, inverse = ready
    co = whole(cross_out, co_far, cross_near_own[1:] + near_swaps(co_far))
    three, normed_mlp, xq, cross_own, cross_sent = cross_forward(two, gains, cq, co, ckv)
    grad_far = far_swaps(grad_four_low)
    grad_near = near_swaps([grad_four_low])
    attn_near = near_swaps([attn_sent])
    (three, normed_mlp), grad_far, grad_near, attn_near = tie_lists(
        [three, normed_mlp], grad_far, grad_near, attn_near
    )

    normed_near = near_swaps([normed_mlp])
    grad_near += near_swaps(grad_far)
    (normed_mlp,), normed_near, grad_near = tie_lists([normed_mlp], normed_near, grad_near)
    grad_pairs = list(zip([grad_four_low] + grad_far, grad_near))
    normed_far = far_swaps(normed_mlp)
    mlp_in = [normed_mlp] + normed_near
    act, inner, *backward = mlp_core(mlp_in, grad_pairs[0], up_proj, down_proj)
    cross_near = near_swaps([cross_sent])
    (act, inner), backward, normed_far, cross_near = tie_lists(
        [act, inner], backward, normed_far, cross_near
    )
    acts, inners = [act], [inner]
    for i, block in enumerate(normed_far):
        pair = [block] + near_swaps([block])
        act, inner, *back = mlp_core(pair, grad_pairs[i + 1], up_proj, down_proj)
        acts.append(act)
        inners.append(inner)
        mlp_in += pair
        backward += back
    backward, acts, inners = tie_lists(near_sums(backward), acts, inners)
    grad_norm = far_sum(backward)
    grad_group = [g for p in grad_pairs for g in p]
    *forward, d_mlp = mlp_rest(mlp_in, grad_group, inners, acts, down_proj)
    (grad_norm, d_mlp), forward = tie_lists([grad_norm, d_mlp], forward)
    g_mlp = lax.psum_scatter(d_mlp, "dp", scatter_dimension=0, tiled=True)

    back = cross_backward(grad_norm, grad_four, three, two, gains, xq, cq, co, ckv)
    grad_two, d_gains, grads_own, grads_sent = back[:4]
    dkv = list(back[4:])
    forward_near = near_swaps(forward[1::2])
    (grad_two, grads_sent), forward_near = tie_lists([grad_two, grads_sent], forward_near)

    def pair_sums(blocks, near_blocks):
        return [
            (a.astype(F) + b.astype(F)).astype(BF) for a, b in zip(blocks[::2], near_blocks)
        ]

    def far_parts(sums):
        return sums[:1] + [swap(v, "rows", 2 * j) for j, v in enumerate(sums) if j]

    def add_all(blocks):
        total = blocks[0].astype(F)
        for v in blocks[1:]:
            total = total + v.astype(F)
        return total

    branch = far_parts(pair_sums(forward, forward_near))
    grads_near = near_swaps([grads_sent])
    back = attn_backward(place, grad_two, conv, noise, gains, qkv, dkv, wqkv, wo, width)
    late_sums, shares, (qkv_own, qkv_sent) = back[0], list(back[1 : 1 + n]), back[1 + n :]
    (late_sums, qkv_sent), shares, grads_near, branch = tie_lists(
        [late_sums, qkv_sent], shares, grads_near, branch
    )

    shares = [shares[0]] + [swap(shares[j], "rows", j) for j in range(1, n)]
    sent_near = near_swaps([qkv_sent])
    back = cross_weights(
        [attn_own] + attn_near, [cross_own] + cross_near, [grads_own] + grads_near, half, share
    )
    d_cross, d_out = list(back[:half]), list(back[half:])
    shares, d_cross, d_out, sent_near = tie_lists(shares, d_cross, d_out, sent_near)
    grad_taps, gs, grad_energy = tap_sums(shares, demod, conv_raw, side, n_dp)

    rest, branch, d_cross, d_out, shares = tie_lists(
        [grad_taps, gs, grad_energy, late_sums, d_gains],
        branch,
        d_cross,
        d_out,
        shares,
    )
    grad_taps, gs, grad_energy, late_sums, d_gains = rest
    lines = n_dp // 2
    ring = [grad_taps]
    flipped = []

    def ring_step(*work):
        flipped.append(lax.ppermute(ring[-1], "dp", ring_perm(n_dp, 0, 1)))
        if len(ring) < lines:
            ring.append(lax.ppermute(ring[-1], "dp", ring_perm(n_dp, 1, 0)))
        (ring[-1], flipped[-1]), *work = tie_lists([ring[-1], flipped[-1]], *work)
        return work

    ge_all = lax.all_to_all(grad_energy, "dp", 0, 0, tiled=True).reshape(samples, width)
    d_cross = far_parts(d_cross)
    back = attn_weights([attn_own] + attn_near, [qkv_own] + sent_near, half, share)
    d_attn, d_value = list(back[:half]), list(back[half:])
    low_first, mix_first = conv_back(gs, xs, mixing, kernel_bank, n, 0, 2)
    (low_first, mix_first, ge_all, gs), d_cross, d_attn, d_value, d_out = ring_step(
        [low_first, mix_first, ge_all, gs], d_cross, d_attn, d_value, d_out
    )
    d_out = far_parts(d_out)
    low_last, mix_last = conv_back(gs, xs, mixing, kernel_bank, n, 1, 2)
    (low_last, mix_last, g_mlp), d_out, d_cross, d_attn, shares = ring_step(
        [low_last, mix_last, g_mlp], d_out, d_cross, d_attn, shares
    )
    low_part = jnp.concatenate([low_first, low_last], axis=2)
    mixing_conv = mix_first + mix_last

    cross_grads = scatter(add_all(d_cross).astype(BF))
    d_attn = far_parts(d_attn)
    low_near = near_sums([low_part[j] for j in range(n)])
    done = energy_sums(place, mixing_all, scale_band, ge_all, pairs, n)
    count_sums = -(-(tokens + 9 + -(-samples * kernels // channels)) // 8) * 8
    count_all = -(-(count_sums + 4 * n + 1) // 8) * 8
    features, color_image, pack = side_outputs(
        place,
        three,
        branch,
        grad_image,
        color_scale,
        colors,
        color_bias.astype(F),
        tokens,
        shares,
        cross_key,
        cross_value,
        d_gains,
        late_sums,
        count_sums,
        count_all,
        side,
    )
    done, d_attn, low_near, (pack, lefts), d_value = ring_step(
        list(done), d_attn, low_near, [pack, lefts], d_value
    )
    scale_energy, mixing_energy = done

    def as_rows(v):
        v = v.reshape(1, -1)
        v = jnp.pad(v, ((0, 0), (0, -v.shape[1] % channels)))
        return v.reshape(-1, channels)

    low_parts = far_parts(low_near)
    pack, grad_images = late_sums_kernel(
        place,
        inverse,
        pack,
        low_parts,
        own_images,
        scale_in,
        scale_energy.reshape(n, channels),
        as_rows(mixing_energy),
        mixing_conv,
        count_sums,
        tokens + 9,
    )
    pack = add_over(pack, "rows")
    d_value = far_parts(d_value)
    energy = bank_energy(places, lefts, ge_all, kernel_bank)
    attn_side = scatter_side(add_all(d_attn).astype(BF))
    (grad_images, pack, energy), d_value, attn_side = ring_step(
        [grad_images, pack, energy], d_value, attn_side
    )
    while len(flipped) < lines:
        ((pack,),) = ring_step([pack])

    everyone_rows = jnp.broadcast_to(pack.astype(BF)[None], (n_dp,) + pack.shape)
    everyone_rows = lax.all_to_all(everyone_rows, "dp", 0, 0, tiled=True)
    out_side = jnp.concatenate([add_all(d_out), add_all(d_value)], axis=1).astype(BF)
    out_side = scatter_side(out_side)
    blocks = [None] * n_dp
    for t in range(lines):
        for e, v in enumerate((ring[t], flipped[t])):
            blocks[2 * t + e] = v
    grad_bank, token_grads = bank_main(places, inverse, at, context_band, blocks, energy, side)
    (grad_bank, everyone_rows), out_side = tie_lists([grad_bank, everyone_rows], out_side)
    attn_parts = scatter_lines(
        *(jnp.concatenate(pair, axis=2) for pair in zip(attn_side, out_side))
    )
    sums = jnp.sum(everyone_rows[:, :count_sums].astype(F), axis=0)
    gathered = everyone_rows[:, count_sums:].astype(F)
    scale_grad, bands_grad, token_all, rgb_all = (
        gathered[:, i * n : (i + 1) * n].reshape(samples, channels) for i in range(4)
    )
    bands_grad = bands_grad.reshape(n_dp, samples, band).transpose(1, 0, 2)
    scale_grad = scale_grad + bands_grad.reshape(samples, channels)
    mixing_grad = gathered[:, 4 * n, : n * kernels].reshape(samples, kernels)
    mixing_sum = sums[tokens + 9 :].reshape(-1)[: samples * kernels]
    mixing_grad = mixing_grad + mixing_sum.reshape(samples, kernels)
    sums = sums[: tokens + 9] * inverse
    grad_images = grad_images.reshape(1, side, side, channels)

    d_select, d_style, d_rgb, styles_grad, d_table = style_final(
        places,
        inverse,
        mixing_grad,
        scale_grad,
        rgb_all,
        token_all,
        styles_all,
        labels_all,
        select_turned,
        style_proj,
        rgb_style,
        class_table.shape[0],
        n,
    )

    cross_grads, attn_grads = tie(
        *(add_all(v) * inverse for v in ([cross_grads], attn_parts))
    )
    g_mlp = g_mlp.astype(F) * inverse
    wide = up_proj.shape[1]

    def column(grads, i):
        return grads[:, i * share : (i + 1) * share]

    return (
        features,
        color_image,
        grad_images,
        styles_grad,
        grad_bank,
        d_select.T,
        d_style,
        sums[tokens + 7],
        sums[tokens + 8],
        sums[tokens + 6],
        column(attn_grads, 0),
        column(attn_grads, 1),
        column(attn_grads, 3),
        column(attn_grads, 2).T,
        sums[tokens + 1],
        column(cross_grads, 0),
        column(token_grads, 0),
        column(token_grads, 1),
        column(cross_grads, 1).T,
        d_table,
        sums[:tokens],
        sums[tokens],
        g_mlp[:, :wide],
        g_mlp[:, wide:].T,
        d_rgb,
        sums[tokens + 2 : tokens + 5].T,
        sums[tokens + 5, :3],
    )


def solution(mesh):
    whole = P()
    columns = P(None, "rows")
    lines = P("rows", None)
    both = P(("dp", "rows"), None, None, None)
    placed = (
        both,
        P("dp", None),
        P("dp"),
        P(("dp", "rows"), None, None),
        P("dp"),
        both,
        both,
        P(None, None, None, None, "rows"),
        whole,
        whole,
        whole,
        whole,
        whole,
        columns,
        columns,
        columns,
        lines,
        whole,
        columns,
        columns,
        columns,
        lines,
        whole,
        whole,
        whole,
        columns,
        lines,
        whole,
        whole,
        whole,
    )
    given = (
        both,
        both,
        both,
        P("dp", None),
        P(None, None, "dp", None, "rows"),
        whole,
        whole,
        whole,
        whole,
        whole,
        P("dp", "rows"),
        P("dp", "rows"),
        P("dp", "rows"),
        P("rows", "dp"),
        whole,
        P("dp", "rows"),
        P("dp", "rows"),
        P("dp", "rows"),
        P("rows", "dp"),
        whole,
        whole,
        whole,
        P("dp", "rows"),
        P("rows", "dp"),
        whole,
        whole,
        whole,
    )
    return jax.shard_map(local, mesh=mesh, in_specs=placed, out_specs=given, check_vma=False)
```

```python
import functools
import math

import jax
import jax.numpy as jnp
from jax import lax
from jax.experimental import pallas as pl
from jax.experimental.pallas import tpu as pltpu
from jax.sharding import PartitionSpec as P

HD = 64
SUB = 32
BF = jnp.bfloat16
F = jnp.float32
VMEM_LIMIT = 56 * 2**20
EPS = 1e-6


def dot_nn(a, b):
    return lax.dot_general(a, b, (((1,), (0,)), ((), ())), preferred_element_type=F)


def dot_nt(a, b):
    return lax.dot_general(a, b, (((1,), (1,)), ((), ())), preferred_element_type=F)


def dot_tn(a, b):
    return lax.dot_general(a, b, (((0,), (0,)), ((), ())), preferred_element_type=F)


def params():
    return pltpu.CompilerParams(vmem_limit_bytes=VMEM_LIMIT)


def swap(x, axis, delta):
    n = lax.axis_size(axis)
    return lax.ppermute(x, axis, [(i, i ^ delta) for i in range(n)])


def spread(x):
    n = lax.axis_size("rows")
    blocks = [None] * n
    blocks[0] = x
    for j in range(2, n, 2):
        blocks[j] = swap(x, "rows", j)
    for j in range(0, n, 2):
        blocks[j + 1] = swap(blocks[j], "rows", 1)
    return blocks


def near_sums(blocks):
    out = []
    for j in range(0, len(blocks), 2):
        near = blocks[j].astype(F) + swap(blocks[j + 1], "rows", 1).astype(F)
        out.append(near.astype(BF))
    return out


def far_sum(near):
    total = near[0].astype(F)
    for j in range(1, len(near)):
        total = total + swap(near[j], "rows", 2 * j).astype(F)
    return total


def collect(blocks):
    return far_sum(near_sums(blocks))


def double(x, axis, place):
    delta = 1
    while delta < lax.axis_size(axis):
        other = swap(x, axis, delta)
        high = (place & delta) != 0
        x = jnp.where(high, jnp.concatenate([other, x]), jnp.concatenate([x, other]))
        delta *= 2
    return x


def merge_step(sums, gathered, axis, place, delta):
    rows = sums.shape[0]
    other = swap(jnp.concatenate([sums, gathered]), axis, delta)
    high = (place & delta) != 0
    theirs = other[rows:]
    gathered = jnp.where(
        high, jnp.concatenate([theirs, gathered]), jnp.concatenate([gathered, theirs])
    )
    return sums + other[:rows], gathered


def add_over(sums, axis):
    delta = 1
    while delta < lax.axis_size(axis):
        sums = sums + swap(sums, axis, delta)
        delta *= 2
    return sums


def tree(parts):
    while len(parts) > 1:
        parts = [a + b for a, b in zip(parts[::2], parts[1::2])]
    return parts[0]


def everyone(x, axis):
    return [x] + [swap(x, axis, j) for j in range(1, lax.axis_size(axis))]


def in_order(blocks, place):
    stacked = jnp.stack(blocks)
    return jnp.take(stacked, jnp.arange(len(blocks), dtype=jnp.int32) ^ place, axis=0)


def ring_perm(n, step, flip):
    lines = n // 2
    return [(i, ((i // 2 + step) % lines) * 2 + ((i % 2) ^ flip)) for i in range(n)]


def ring_gather(x):
    n = lax.axis_size("dp")
    out = []
    held = x
    for step in range(n // 2):
        if step:
            held = lax.ppermute(held, "dp", ring_perm(n, 1, 0))
        out.append(held)
        out.append(lax.ppermute(held, "dp", ring_perm(n, 0, 1)))
    return out


def ring_source(n, place, slot):
    lines = n // 2
    return ((place // 2 - slot // 2) % lines) * 2 + ((place % 2) ^ (slot % 2))


def ring_target(n, place, slot):
    lines = n // 2
    return ((place // 2 + slot // 2) % lines) * 2 + ((place % 2) ^ (slot % 2))


def scatter(grads):
    return lax.psum_scatter(grads, "dp", scatter_dimension=0, tiled=True)


def scatter_side(grads):
    n = lax.axis_size("dp")
    side = lax.axis_index("dp") % 2
    bands = grads.reshape(n // 2, 2, grads.shape[0] // n, grads.shape[1])
    mine = lax.dynamic_index_in_dim(bands, side, 1, keepdims=False)
    theirs = lax.dynamic_index_in_dim(bands, 1 - side, 1, keepdims=False)
    return mine, lax.ppermute(theirs, "dp", ring_perm(n, 0, 1))


def scatter_lines(mine, theirs):
    n = lax.axis_size("dp")
    lines = n // 2
    line = lax.axis_index("dp") // 2
    half = (mine.astype(F) + theirs.astype(F)).astype(BF)
    pieces = [lax.dynamic_index_in_dim(half, line, 0, keepdims=False)]
    for step in range(1, lines):
        piece = lax.dynamic_index_in_dim(half, (line + step) % lines, 0, keepdims=False)
        pieces.append(lax.ppermute(piece, "dp", ring_perm(n, step, 0)))
    return pieces


def tie(*values):
    return lax.optimization_barrier(values)


def move_up(v, axis):
    shape = list(v.shape)
    shape[axis] = 1
    kept = lax.slice_in_dim(v, 0, v.shape[axis] - 1, axis=axis)
    return jnp.concatenate([jnp.zeros(shape, v.dtype), kept], axis=axis)


def move_down(v, axis):
    shape = list(v.shape)
    shape[axis] = 1
    kept = lax.slice_in_dim(v, 1, v.shape[axis], axis=axis)
    return jnp.concatenate([kept, jnp.zeros(shape, v.dtype)], axis=axis)


def band_mask(kernels):
    width = SUB * kernels
    row = lax.broadcasted_iota(jnp.int32, (SUB, width), 0)
    lane = lax.broadcasted_iota(jnp.int32, (SUB, width), 1)
    return (lane // kernels) == row


def split_dot(a, b):
    high = a.astype(BF)
    rest = (a - high.astype(F)).astype(BF)
    return dot_nn(high, b) + dot_nn(rest, b)


def widen_mask(block, kernels):
    row = lax.broadcasted_iota(jnp.int32, (block, block * kernels), 0)
    lane = lax.broadcasted_iota(jnp.int32, (block, block * kernels), 1)
    return jnp.where(lane // kernels == row, 1.0, 0.0).astype(BF)


def tile_mask(block, kernels):
    row = lax.broadcasted_iota(jnp.int32, (kernels, block * kernels), 0)
    lane = lax.broadcasted_iota(jnp.int32, (kernels, block * kernels), 1)
    return jnp.where(lane % kernels == row, 1.0, 0.0).astype(BF)


def conv_forward(codes, select, style, payload, images, bank, side):
    groups = len(images)
    low, channels = images[0].shape
    rows = groups * low
    kernels, width = bank.shape[3], bank.shape[4]
    pad, depth = codes.shape
    block = min(channels, 128)
    steps = channels // block
    parts = block // SUB
    span = SUB * kernels

    extra = payload.shape[0]

    def body(c_ref, sel_ref, sty_ref, pay_ref, *rest):
        x_refs = rest[:groups]
        b_ref, out_r = rest[groups], rest[groups + 1 : 2 * groups + 1]
        raw_ref, dem_ref, xs_ref, mix_ref, sc_ref = rest[2 * groups + 1 : 2 * groups + 6]
        acc, en, scale, mix_row, widen = rest[2 * groups + 6 :]
        step = pl.program_id(0)

        @pl.when(step == 0)
        def _():
            acc[...] = jnp.zeros_like(acc)
            en[...] = jnp.zeros_like(en)
            logits = dot_nt(c_ref[...], sel_ref[...])
            e = jnp.exp(logits - jnp.max(logits, axis=1, keepdims=True))
            mixing = e / jnp.sum(e, axis=1, keepdims=True)
            mix_ref[...] = mixing
            mix_row[...] = split_dot(mixing, tile_mask(block, kernels))
            scale[...] = dot_nn(c_ref[...], sty_ref[...]) + 1.0
            sc_ref[...] = scale[...]
            widen[...] = widen_mask(block, kernels)

        here = scale[:, pl.ds(pl.multiple_of(step * block, block), block)]
        wide_scale = split_dot(here, widen[...]) * mix_row[...]
        mask = band_mask(kernels)
        xs = []
        for s in range(groups):
            xs.append((x_refs[s][...].astype(F) * here[s : s + 1]).astype(BF))
            xs_ref[0, s * low : (s + 1) * low] = xs[s]
        xs_ref[0, rows:] = pay_ref[...]
        a = []
        for s in range(groups):
            a.append((dot_nn(xs[s], widen[...]) * mix_row[s : s + 1]).astype(BF))
        left = []
        for u in range(parts):
            cut = slice(u * span, (u + 1) * span)
            pieces = [v[:, cut] for v in a]
            for s in range(groups):
                pieces.append(jnp.where(mask, wide_scale[s : s + 1, cut], 0.0).astype(BF))
            left.append(jnp.concatenate(pieces))
        energy = en[...]
        for t in range(9):
            b = b_ref[t // 3, t % 3].reshape(block * kernels, width)
            total = acc[t]
            for u in range(parts):
                p = dot_nn(left[u], b[u * span : (u + 1) * span])
                total = total + p[:rows]
                m = p[rows:]
                energy = energy + jnp.sum((m * m).reshape(groups, SUB // 8, 8, width), axis=1)
            acc[t] = total
        en[...] = energy

        @pl.when(step == steps - 1)
        def _():
            demod = lax.rsqrt(jnp.sum(en[...], axis=1, keepdims=True) + 1e-8)
            dem_ref[...] = demod
            for s in range(groups):
                v = [acc[t, s * low : (s + 1) * low].reshape(side, side, width) for t in range(9)]
                for py in range(2):
                    h = []
                    for tx in range(3):
                        if py == 0:
                            h.append(move_up(v[tx], 0) + v[3 + tx] + v[6 + tx])
                        else:
                            h.append(v[tx] + v[3 + tx] + move_down(v[6 + tx], 0))
                    for px in range(2):
                        if px == 0:
                            o = move_up(h[0], 1) + h[1] + h[2]
                        else:
                            o = h[0] + h[1] + move_down(h[2], 1)
                        o = o.reshape(low, width)
                        q = (py * 2 + px) * low
                        raw_ref[s, q : q + low] = o.astype(raw_ref.dtype)
                        out_r[s][q : q + low] = (o * demod[s]).astype(BF)

    return pl.pallas_call(
        body,
        grid=(steps,),
        in_specs=[
            pl.BlockSpec((pad, depth), lambda i: (0, 0)),
            pl.BlockSpec((kernels, depth), lambda i: (0, 0)),
            pl.BlockSpec((depth, channels), lambda i: (0, 0)),
            pl.BlockSpec((extra, block), lambda i: (0, 0)),
        ]
        + [pl.BlockSpec((low, block), lambda i: (0, i))] * groups
        + [pl.BlockSpec((3, 3, block, kernels, width), lambda i: (0, 0, i, 0, 0))],
        out_specs=[pl.BlockSpec((4 * low, width), lambda i: (0, 0))] * groups
        + [
            pl.BlockSpec((groups, 4 * low, width), lambda i: (0, 0, 0)),
            pl.BlockSpec((groups, 1, width), lambda i: (0, 0, 0)),
            pl.BlockSpec((1, rows + extra, block), lambda i: (i, 0, 0)),
            pl.BlockSpec((pad, kernels), lambda i: (0, 0)),
            pl.BlockSpec((pad, channels), lambda i: (0, 0)),
        ],
        out_shape=[jax.ShapeDtypeStruct((4 * low, width), BF)] * groups
        + [
            jax.ShapeDtypeStruct((groups, 4 * low, width), BF),
            jax.ShapeDtypeStruct((groups, 1, width), F),
            jax.ShapeDtypeStruct((steps, rows + extra, block), BF),
            jax.ShapeDtypeStruct((pad, kernels), F),
            jax.ShapeDtypeStruct((pad, channels), F),
        ],
        scratch_shapes=[
            pltpu.VMEM((9, rows, width), F),
            pltpu.VMEM((groups, 8, width), F),
            pltpu.VMEM((pad, channels), F),
            pltpu.VMEM((pad, block * kernels), F),
            pltpu.VMEM((block, block * kernels), BF),
        ],
        compiler_params=params(),
        cost_estimate=pl.CostEstimate(
            flops=27 * rows * channels * kernels * width,
            bytes_accessed=18 * channels * kernels * width,
            transcendentals=0,
        ),
        name="conv_forward",
    )(codes, select, style, payload, *images, bank)


def conv_back(gs, xs, mixing, bank, groups, part, parts):
    _, rows, width = gs.shape
    blocks, held, block = xs.shape
    steps = blocks // parts
    first = part * steps
    channels, kernels = steps * block, bank.shape[3]
    pad = mixing.shape[0]
    low = rows // groups

    def body(g_ref, x_ref, m_ref, b_ref, low_ref, mix_ref, acc, mix_row, widen):
        step = pl.program_id(0)

        @pl.when(step == 0)
        def _():
            acc[...] = jnp.zeros_like(acc)
            mix_row[...] = split_dot(m_ref[...], tile_mask(block, kernels))
            widen[...] = widen_mask(block, kernels)

        total = None
        for t in range(9):
            p = dot_nt(g_ref[t], b_ref[t // 3, t % 3].reshape(block * kernels, width))
            total = p if total is None else total + p
        wide = dot_nn(x_ref[0, :rows], widen[...])
        acc[...] += jnp.sum((wide * total).reshape(groups, low // 8, 8, block * kernels), axis=1)
        for s in range(groups):
            cut = slice(s * low, (s + 1) * low)
            mixed = (total[cut] * mix_row[s : s + 1]).astype(BF)
            low_ref[s] = dot_nt(mixed, widen[...]).astype(BF)

        @pl.when(step == steps - 1)
        def _():
            sums = jnp.sum(acc[...], axis=1)
            mix_ref[...] = lax.dot_general(
                sums,
                tile_mask(block, kernels).astype(F),
                (((1,), (1,)), ((), ())),
                precision=lax.Precision.HIGHEST,
                preferred_element_type=F,
            )

    return pl.pallas_call(
        body,
        grid=(steps,),
        in_specs=[
            pl.BlockSpec((9, rows, width), lambda i: (0, 0, 0)),
            pl.BlockSpec((1, held, block), lambda i: (first + i, 0, 0)),
            pl.BlockSpec((pad, kernels), lambda i: (0, 0)),
            pl.BlockSpec((3, 3, block, kernels, width), lambda i: (0, 0, first + i, 0, 0)),
        ],
        out_specs=[
            pl.BlockSpec((groups, low, block), lambda i: (0, 0, i)),
            pl.BlockSpec((groups, kernels), lambda i: (0, 0)),
        ],
        out_shape=[
            jax.ShapeDtypeStruct((groups, low, channels), BF),
            jax.ShapeDtypeStruct((groups, kernels), F),
        ],
        scratch_shapes=[
            pltpu.VMEM((groups, 8, block * kernels), F),
            pltpu.VMEM((pad, block * kernels), F),
            pltpu.VMEM((block, block * kernels), BF),
        ],
        compiler_params=params(),
        cost_estimate=pl.CostEstimate(
            flops=18 * rows * channels * kernels * width,
            bytes_accessed=18 * channels * kernels * width,
            transcendentals=0,
        ),
        name="conv_back",
    )(gs, xs, mixing, bank)


def roll_kernels(v, shift):
    n = v.shape[-2]
    return pltpu.roll(v, shift % n, v.ndim - 2) if shift % n else v


def bank_pairs(place, bank, band):
    kernels, width = bank.shape[3], bank.shape[4]
    count = kernels // 2 + 1
    block = min(band, SUB)

    def body(place_ref, b_ref, q_ref):
        for c in range(block // 8):
            cut = slice(c * 8, (c + 1) * 8)
            total = [None] * count
            for t in range(9):
                b = b_ref[t // 3, t % 3, cut].astype(F)
                for r in range(count):
                    p = b * roll_kernels(b, -r)
                    total[r] = p if t == 0 else total[r] + p
            for r in range(count):
                q_ref[r, c * 8 * kernels : (c + 1) * 8 * kernels] = (
                    total[r].reshape(8 * kernels, width).astype(BF)
                )

    return pl.pallas_call(
        body,
        grid_spec=pltpu.PrefetchScalarGridSpec(
            num_scalar_prefetch=1,
            grid=(band // block,),
            in_specs=[
                pl.BlockSpec(
                    (3, 3, block, kernels, width),
                    lambda i, s: (0, 0, s[1] * (band // block) + i, 0, 0),
                )
            ],
            out_specs=pl.BlockSpec((count, block * kernels, width), lambda i, s: (0, i, 0)),
        ),
        out_shape=jax.ShapeDtypeStruct((count, band * kernels, width), BF),
        compiler_params=params(),
        cost_estimate=pl.CostEstimate(
            flops=20 * count * band * kernels * width,
            bytes_accessed=18 * band * kernels * width,
            transcendentals=0,
        ),
        name="bank_pairs",
    )(place, bank)


def energy_sums(place, mixing, scale, ge, pairs, group):
    samples, kernels = mixing.shape
    band = scale.shape[1]
    count = pairs.shape[0]
    exact = dict(precision=lax.Precision.HIGHEST, preferred_element_type=F)
    along = (((1,), (0,)), ((), ()))

    def fold(a, mask):
        high = a.astype(BF)
        rest = (a - high.astype(F)).astype(BF)
        return dot_nt(high, mask) + dot_nt(rest, mask)

    def body(place_ref, m_ref, s_ref, g_ref, q_ref, se_ref, me_ref):
        m = m_ref[...]
        wides = split_dot(s_ref[...], widen_mask(band, kernels))
        ge = (2.0 * g_ref[...]).astype(BF)
        row = lax.broadcasted_iota(jnp.int32, (kernels, kernels), 0)
        lane = lax.broadcasted_iota(jnp.int32, (kernels, kernels), 1)
        tile = tile_mask(band, kernels)
        square = wides * wides
        se, me = None, None
        for r in range(count):
            g = dot_nt(ge, q_ref[r])
            ahead = jnp.where(row == (lane + r) % kernels, 1.0, 0.0)
            behind = jnp.where(row == (lane + kernels - r) % kernels, 1.0, 0.0)
            next_m = lax.dot_general(m, ahead, along, **exact)
            both = split_dot(m * next_m, tile)
            weight = 1.0 if r == 0 or 2 * r == kernels else 2.0
            part = (weight * both) * g
            se = part if se is None else se + part
            h = fold(g * square, tile)
            part = next_m * h
            if weight == 2.0:
                part = part + lax.dot_general(m * h, behind, along, **exact)
            me = part if me is None else me + part
        se = fold(se * wides, widen_mask(band, kernels))
        for s in range(samples):
            to = pl.ds(s // group * group + lax.bitwise_xor(place_ref[0], s % group), 1)
            se_ref[to] = se[s : s + 1]
            me_ref[to] = me[s : s + 1]

    return pl.pallas_call(
        body,
        in_specs=[smem()] + vmem(4),
        out_shape=[
            jax.ShapeDtypeStruct((samples, band), F),
            jax.ShapeDtypeStruct((samples, kernels), F),
        ],
        compiler_params=params(),
        name="energy_sums",
    )(place, mixing, scale, ge, pairs)


def bank_energy(place, lefts, ge, bank):
    kernels, width = bank.shape[3], bank.shape[4]
    count, rows_all, samples = lefts.shape
    band = rows_all // kernels
    step = min(band, 16)

    def body(place_ref, l_ref, ge_ref, b_ref, o_ref, rights):
        @pl.when(pl.program_id(0) == 0)
        def _():
            ge = ge_ref[...].astype(BF)
            for r in range(count):
                rights[r] = dot_nn(l_ref[r], ge)

        for tx in range(3):
            for i in range(band // step):
                cut = slice(i * step * kernels, (i + 1) * step * kernels)
                b = b_ref[0, tx, i * step : (i + 1) * step].astype(F)
                e = rights[0, cut].reshape(step, kernels, width) * b
                for r in range(1, count):
                    right = rights[r, cut].reshape(step, kernels, width)
                    e = e + right * roll_kernels(b, -r)
                    if 2 * r != kernels:
                        e = e + roll_kernels(right * b, r)
                o_ref[0, tx, i * step : (i + 1) * step] = e.astype(BF)

    return pl.pallas_call(
        body,
        grid_spec=pltpu.PrefetchScalarGridSpec(
            num_scalar_prefetch=1,
            grid=(3,),
            in_specs=[
                pl.BlockSpec((count, band * kernels, samples), lambda t, s: (0, 0, 0)),
                pl.BlockSpec((samples, width), lambda t, s: (0, 0)),
                pl.BlockSpec((1, 3, band, kernels, width), lambda t, s: (t, 0, s[1], 0, 0)),
            ],
            out_specs=pl.BlockSpec((1, 3, band, kernels, width), lambda t, s: (t, 0, 0, 0, 0)),
            scratch_shapes=[pltpu.VMEM((count, band * kernels, width), F)],
        ),
        out_shape=jax.ShapeDtypeStruct((3, 3, band, kernels, width), BF),
        compiler_params=params(),
        cost_estimate=pl.CostEstimate(
            flops=400 * band * kernels * width,
            bytes_accessed=36 * band * kernels * width,
            transcendentals=0,
        ),
        name="bank_energy",
    )(place, lefts, ge, bank)


def line_sums(g, tap, axis):
    if tap == 0:
        return g[1] + move_down(g[0], axis)
    if tap == 1:
        return g[0] + g[1]
    return g[0] + move_up(g[1], axis)


def bank_main(places, scale, at, context, taps, energy, side):
    blocks = len(taps)
    groups, rows, width = taps[0].shape
    low = side * side
    points = 4 * low
    tokens = (rows - points) // 2
    held = blocks * groups * low
    band, kernels = energy.shape[2], energy.shape[3]

    def body(place_ref, scale_ref, a_ref, c_ref, *rest):
        here = place_ref[1]
        g_refs = rest[:blocks]
        e_ref, o_ref, token_ref, lines, sums, keyval = rest[blocks:]
        ty = pl.program_id(0)

        def source(b):
            line = lax.rem(here // 2 + blocks // 2 - b // 2, blocks // 2)
            return 2 * line + lax.bitwise_xor(lax.rem(here, 2), b % 2)

        @pl.when(ty == 0)
        def _():
            for b in range(blocks):
                for s in range(groups):
                    at_row = pl.multiple_of((source(b) * groups + s) * tokens, tokens)
                    for i in range(2):
                        cut = slice(points + i * tokens, points + (i + 1) * tokens)
                        keyval[i, pl.ds(at_row, tokens)] = g_refs[b][s, cut]
            for i in range(2):
                token_ref[:, i * width : (i + 1) * width] = (
                    dot_nn(c_ref[...], keyval[i]) * scale_ref[0]
                )
        for tap in range(3):

            @pl.when(ty == tap)
            def _():
                for b in range(blocks):
                    for s in range(groups):
                        g = g_refs[b][s, :points].astype(F).reshape(2, 2, side, side, width)
                        for px in range(2):
                            v = line_sums((g[0, px], g[1, px]), tap, 0)
                            at_row = (source(b) * groups + s) * low
                            at_row = pl.multiple_of(at_row, low)
                            lines[px, pl.ds(at_row, low)] = v.reshape(low, width)

        for tx in range(3):
            for b in range(blocks * groups):
                cut = slice(b * low, (b + 1) * low)
                pair = [lines[px, cut].reshape(side, side, width) for px in range(2)]
                sums[cut] = line_sums(pair, tx, 1).reshape(low, width).astype(BF)
            p = dot_nn(a_ref[...], sums[...]).reshape(band, kernels, width)
            o_ref[0, tx] = (p + e_ref[0, tx].astype(F)) * scale_ref[0]

    return pl.pallas_call(
        body,
        grid=(3,),
        in_specs=[
            smem(),
            smem(),
            pl.BlockSpec((band * kernels, held), lambda t: (0, 0)),
            pl.BlockSpec(context.shape, lambda t: (0, 0)),
        ]
        + [pl.BlockSpec((groups, rows, width), lambda t: (0, 0, 0))] * blocks
        + [pl.BlockSpec((1, 3, band, kernels, width), lambda t: (t, 0, 0, 0, 0))],
        out_specs=[
            pl.BlockSpec((1, 3, band, kernels, width), lambda t: (t, 0, 0, 0, 0)),
            pl.BlockSpec((band, 2 * width), lambda t: (0, 0)),
        ],
        out_shape=[
            jax.ShapeDtypeStruct((3, 3, band, kernels, width), F),
            jax.ShapeDtypeStruct((band, 2 * width), F),
        ],
        scratch_shapes=[
            pltpu.VMEM((2, held, width), F),
            pltpu.VMEM((held, width), BF),
            pltpu.VMEM((2, blocks * groups * tokens, width), BF),
        ],
        compiler_params=params(),
        cost_estimate=pl.CostEstimate(
            flops=18 * band * kernels * held * width,
            bytes_accessed=18 * held * width + 54 * band * kernels * width,
            transcendentals=0,
        ),
        name="bank_main",
    )(places, scale, at, context, *taps, energy)


def tap_sums(grads, demod, raw, side, copies):
    groups = len(grads)
    _, points, width = raw.shape
    low = side * side

    held = grads[0].shape[0]

    def body(d_ref, r_ref, *rest):
        g_refs = rest[:groups]
        taps_ref, sums_ref, en_ref = rest[groups:]
        for s in range(groups):
            part = g_refs[s][:points].astype(F)
            demod = d_ref[s]
            grad_demod = jnp.sum(part * r_ref[s].astype(F), axis=0, keepdims=True)
            en = -0.5 * grad_demod * demod * demod * demod
            for i in range(copies):
                en_ref[i, s : s + 1] = en
            taps_ref[s, :points] = (part * demod).astype(BF)
            taps_ref[s, points:] = g_refs[s][points:]
            g = taps_ref[s, :points].astype(F).reshape(2, 2, side, side, width)
            for ty in range(3):
                lines = [line_sums((g[0, px], g[1, px]), ty, 0) for px in range(2)]
                for tx in range(3):
                    v = line_sums(lines, tx, 1).reshape(low, width).astype(BF)
                    sums_ref[3 * ty + tx, s * low : (s + 1) * low] = v

    return pl.pallas_call(
        body,
        out_shape=[
            jax.ShapeDtypeStruct((groups, held, width), BF),
            jax.ShapeDtypeStruct((9, groups * low, width), BF),
            jax.ShapeDtypeStruct((copies, groups, width), F),
        ],
        compiler_params=params(),
        name="tap_sums",
    )(demod, raw, *grads)


def rms(field, gain):
    inverse = lax.rsqrt(jnp.mean(field * field, axis=-1, keepdims=True) + EPS)
    return field * inverse * gain, inverse


def rms_back(field, gain, grad_out):
    inverse = lax.rsqrt(jnp.mean(field * field, axis=-1, keepdims=True) + EPS)
    scaled = grad_out * gain
    grad_gain = jnp.sum(grad_out * field * inverse, axis=0, keepdims=True)
    mean = jnp.mean(scaled * field, axis=-1, keepdims=True)
    return inverse * scaled - field * inverse**3 * mean, grad_gain


def sigmoid(v):
    return 1.0 / (1.0 + jnp.exp(-v))


def silu_slope(v):
    q = sigmoid(v)
    return q * (1.0 + v * (1.0 - q))


def self_prob(q, k):
    kf = k.astype(F)
    square = jnp.sum(kf * kf, axis=1, keepdims=True)
    scores = (2.0 * dot_nt(k, q) - square) * (1.0 / math.sqrt(HD))
    e = jnp.exp(scores - jnp.max(scores, axis=0, keepdims=True))
    return e * (1.0 / jnp.sum(e, axis=0, keepdims=True))


def cross_prob(q, k):
    scores = dot_nt(k, q) * (1.0 / math.sqrt(HD))
    e = jnp.exp(scores - jnp.max(scores, axis=0, keepdims=True))
    return e * (1.0 / jnp.sum(e, axis=0, keepdims=True))


def side_slot(own_ref, send_ref, j, start, width):
    at = start + j // 2 * width
    return (send_ref if j % 2 else own_ref), slice(at, at + width)


def fetch(refs, buffer, sems):
    copies = [pltpu.make_async_copy(r, buffer.at[i], sems.at[i]) for i, r in enumerate(refs)]

    def take(i):
        copies[i].wait()
        return buffer[i]

    return copies, take


def anywhere(count):
    return [pl.BlockSpec(memory_space=pl.ANY)] * count


def smem():
    return pl.BlockSpec(memory_space=pltpu.SMEM)


def vmem(count):
    return [pl.BlockSpec(memory_space=pltpu.VMEM)] * count


def attn_forward(place, conv_parts, noise, gains, wqkv, wo):
    n = len(wo)
    points, width = conv_parts[0].shape
    share, channels = wo[0].shape

    def body(place_ref, noise_ref, gains_ref, *rest):
        part_r, wqkv_r, wo_r = (rest[i * n : (i + 1) * n] for i in range(3))
        conv_ref, two_ref, qkv_ref, own_ref, send_ref = rest[3 * n : 3 * n + 5]
        wide, out_w, wide_sem, out_sem = rest[3 * n + 5 :]
        wide_copies, take_wide = fetch(wqkv_r, wide, wide_sem)
        out_copies, take_out = fetch(wo_r, out_w, out_sem)
        for a, b in zip(wide_copies, out_copies):
            a.start()
            b.start()
        here = place_ref[0]
        for j in range(n):
            start = pl.multiple_of(lax.bitwise_xor(here, j) * width, width)
            conv_ref[:, pl.ds(start, width)] = part_r[j][...]
        out = conv_ref[...].astype(F) + gains_ref[0:1] * noise_ref[...] + gains_ref[1:2]
        one = out * sigmoid(out)
        normed = rms(one, gains_ref[2:3])[0].astype(BF)
        own_ref[:, :channels] = normed
        send_ref[:, :channels] = normed
        two_ref[...] = one
        for j in range(n):
            qkv_ref[j] = dot_nn(normed, take_wide(j)).astype(BF)
            heads = []
            for h in range(share // HD):
                q, k, v = (
                    qkv_ref[j, :, i * share + h * HD : i * share + (h + 1) * HD] for i in range(3)
                )
                heads.append(dot_tn(v, self_prob(q, k).astype(BF)))
            side_ref, cut = side_slot(own_ref, send_ref, j, channels, share)
            side_ref[:, cut] = jnp.concatenate(heads).T.astype(BF)
            two_ref[...] += dot_nn(side_ref[:, cut], take_out(j))

    return pl.pallas_call(
        body,
        in_specs=[smem()] + vmem(2 + n) + anywhere(2 * n),
        scratch_shapes=[
            pltpu.VMEM((n, channels, 3 * share), BF),
            pltpu.VMEM((n, share, channels), BF),
            pltpu.SemaphoreType.DMA((n,)),
            pltpu.SemaphoreType.DMA((n,)),
        ],
        out_shape=[
            jax.ShapeDtypeStruct((points, channels), BF),
            jax.ShapeDtypeStruct((points, channels), F),
            jax.ShapeDtypeStruct((n, points, 3 * share), BF),
        ]
        + [jax.ShapeDtypeStruct((points, channels + n // 2 * share), BF)] * 2,
        compiler_params=params(),
        cost_estimate=pl.CostEstimate(
            flops=10 * points * channels * channels,
            bytes_accessed=16 * channels * channels,
            transcendentals=points * points * channels // HD,
        ),
        name="attn_forward",
    )(place, noise, gains, *conv_parts, *wqkv, *wo)


def cross_forward(two, gains, cq, co, ckv):
    points, channels = two.shape
    n = len(cq)
    share = cq[0].shape[1]

    def body(two_ref, gains_ref, *rest):
        cq_r, co_r, ckv_r = (rest[i * n : (i + 1) * n] for i in range(3))
        three_ref, mlp_ref, xq_ref, own_ref, send_ref = rest[3 * n :]
        normed = rms(two_ref[...], gains_ref[3:4])[0].astype(BF)
        own_ref[:, :channels] = normed
        send_ref[:, :channels] = normed
        three_ref[...] = two_ref[...]
        for j in range(n):
            xq_ref[j] = dot_nn(normed, cq_r[j][...]).astype(BF)
            heads = []
            for h in range(share // HD):
                q = xq_ref[j, :, h * HD : (h + 1) * HD]
                k = ckv_r[j][:, h * HD : (h + 1) * HD]
                v = ckv_r[j][:, share + h * HD : share + (h + 1) * HD]
                heads.append(dot_tn(v, cross_prob(q, k).astype(BF)))
            side_ref, cut = side_slot(own_ref, send_ref, j, channels, share)
            side_ref[:, cut] = jnp.concatenate(heads).T.astype(BF)
            three_ref[...] += dot_nn(side_ref[:, cut], co_r[j][...])
        mlp_ref[...] = rms(three_ref[...], gains_ref[4:5])[0].astype(BF)

    return pl.pallas_call(
        body,
        out_shape=[
            jax.ShapeDtypeStruct((points, channels), F),
            jax.ShapeDtypeStruct((points, channels), BF),
            jax.ShapeDtypeStruct((n, points, share), BF),
        ]
        + [jax.ShapeDtypeStruct((points, channels + n // 2 * share), BF)] * 2,
        compiler_params=params(),
        cost_estimate=pl.CostEstimate(
            flops=5 * points * channels * channels,
            bytes_accessed=8 * channels * channels,
            transcendentals=points * channels,
        ),
        name="cross_forward",
    )(two, gains, *cq, *co, *ckv)


def mlp_core(inputs, grad_out, up, down):
    count = len(inputs)
    points, channels = inputs[0].shape
    hidden = up.shape[1]
    tile = min(hidden, 256)
    steps = hidden // tile
    rows = count * points

    def body(*refs):
        x_r, g_r = refs[:count], refs[count : 2 * count]
        up_ref, down_ref, act_ref, gi_ref = refs[2 * count : 2 * count + 4]
        back_r = refs[2 * count + 4 : 3 * count + 4]
        x_all, g_all, acc = refs[3 * count + 4 :]
        step = pl.program_id(0)

        @pl.when(step == 0)
        def _():
            for j in range(count):
                x_all[j * points : (j + 1) * points] = x_r[j][...]
                g_all[j * points : (j + 1) * points] = g_r[j][...]
            acc[...] = jnp.zeros_like(acc)

        inner = dot_nn(x_all[...], up_ref[...])
        gate = sigmoid(inner)
        act_ref[...] = (inner * gate).astype(BF)
        grad_act = dot_nt(g_all[...], down_ref[...])
        gi_ref[...] = (grad_act * (gate * (1.0 + inner * (1.0 - gate)))).astype(BF)
        acc[...] += dot_nt(gi_ref[...], up_ref[...])

        @pl.when(step == steps - 1)
        def _():
            for j in range(count):
                back_r[j][...] = acc[j * points : (j + 1) * points].astype(BF)

    block = pl.BlockSpec((points, channels), lambda i: (0, 0))
    return pl.pallas_call(
        body,
        grid=(steps,),
        in_specs=[block] * (2 * count)
        + [
            pl.BlockSpec((channels, tile), lambda i: (0, i)),
            pl.BlockSpec((tile, channels), lambda i: (i, 0)),
        ],
        out_specs=[pl.BlockSpec((rows, tile), lambda i: (0, i))] * 2 + [block] * count,
        out_shape=[jax.ShapeDtypeStruct((rows, hidden), BF)] * 2
        + [jax.ShapeDtypeStruct((points, channels), BF)] * count,
        scratch_shapes=[
            pltpu.VMEM((rows, channels), BF),
            pltpu.VMEM((rows, channels), BF),
            pltpu.VMEM((rows, channels), F),
        ],
        compiler_params=params(),
        cost_estimate=pl.CostEstimate(
            flops=6 * rows * channels * hidden,
            bytes_accessed=4 * channels * hidden,
            transcendentals=rows * hidden,
        ),
        name="mlp_core",
    )(*inputs, *grad_out, up, down)


def mlp_rest(inputs, grad_out, grad_inner, acts, down):
    n = len(inputs)
    points, channels = inputs[0].shape
    hidden = acts[0].shape[1]
    tile = min(hidden, 256)
    groups = len(acts)
    each = n // groups

    def body(down_ref, *rest):
        x_r, go_r = rest[:n], rest[n : 2 * n]
        gi_r, act_r = rest[2 * n : 2 * n + groups], rest[2 * n + groups : 2 * n + 2 * groups]
        outs, dw_ref = rest[2 * n + 2 * groups : 3 * n + 2 * groups], rest[3 * n + 2 * groups]
        turned = rest[3 * n + 2 * groups + 1]
        for j in range(n):
            cut = slice(j % each * points, (j % each + 1) * points)
            outs[j][...] = dot_nn(act_r[j // each][cut], down_ref[...]).astype(BF)
        for side, refs, other in ((0, x_r, gi_r), (1, go_r, act_r)):
            for j in range(n):
                turned[:, j * points : (j + 1) * points] = refs[j][...].T
            for c in range(hidden // tile):
                cut = slice(c * tile, (c + 1) * tile)
                total = None
                for g in range(groups):
                    span = each * points
                    p = dot_nn(turned[:, g * span : (g + 1) * span], other[g][:, cut])
                    total = p if total is None else total + p
                at = side * hidden + c * tile
                dw_ref[:, at : at + tile] = total.astype(BF)

    return pl.pallas_call(
        body,
        out_shape=[jax.ShapeDtypeStruct((points, channels), BF)] * n
        + [jax.ShapeDtypeStruct((channels, 2 * hidden), BF)],
        scratch_shapes=[pltpu.VMEM((channels, n * points), BF)],
        compiler_params=params(),
        cost_estimate=pl.CostEstimate(
            flops=6 * n * points * channels * hidden,
            bytes_accessed=16 * channels * hidden,
            transcendentals=0,
        ),
        name="mlp_rest",
    )(down, *inputs, *grad_out, *grad_inner, *acts)


def cross_backward(grad_norm, grad_four, three, two, gains, xq, cq, co, ckv):
    points, channels = three.shape
    n, _, share = xq.shape
    tokens = ckv[0].shape[0]

    def body(gn_ref, g4_ref, three_ref, two_ref, in_ref, xq_ref, *rest):
        cq_r, co_r, ckv_r = (rest[i * n : (i + 1) * n] for i in range(3))
        two_out, gains_ref, own_ref, send_ref = rest[3 * n : 3 * n + 4]
        dkv_r = rest[3 * n + 4 : 4 * n + 4]
        back, gain = rms_back(three_ref[...], in_ref[4:5], gn_ref[...])
        gains_ref[0:1] = gain
        grad_three = g4_ref[...] + back
        gb = grad_three.astype(BF)
        own_ref[:, :channels] = gb
        send_ref[:, :channels] = gb
        grad_norm2 = jnp.zeros((points, channels), F)
        for j in range(n):
            ga = dot_nt(gb, co_r[j][...]).astype(BF)
            kv = ckv_r[j][...]
            gq, gk, gv = [], [], []
            for h in range(share // HD):
                q = xq_ref[j, :, h * HD : (h + 1) * HD]
                k = kv[:, h * HD : (h + 1) * HD]
                v = kv[:, share + h * HD : share + (h + 1) * HD]
                g = ga[:, h * HD : (h + 1) * HD]
                p = cross_prob(q, k)
                gp = dot_nt(v, g)
                gs = p * (gp - jnp.sum(p * gp, axis=0, keepdims=True))
                raw = (gs * (1.0 / math.sqrt(HD))).astype(BF)
                gq.append(dot_tn(k, raw))
                gk.append(dot_nn(raw, q).astype(BF))
                gv.append(dot_nn(p.astype(BF), g).astype(BF))
            side_ref, cut = side_slot(own_ref, send_ref, j, 2 * channels, share)
            side_ref[:, cut] = jnp.concatenate(gq).T.astype(BF)
            dkv_r[j][...] = jnp.concatenate(gk + gv, axis=1)
            grad_norm2 = grad_norm2 + dot_nt(side_ref[:, cut], cq_r[j][...])
        back, gain = rms_back(two_ref[...], in_ref[3:4], grad_norm2)
        gains_ref[1:2] = gain
        two_out[...] = grad_three + back
        gb = two_out[...].astype(BF)
        own_ref[:, channels : 2 * channels] = gb
        send_ref[:, channels : 2 * channels] = gb

    return pl.pallas_call(
        body,
        out_shape=[
            jax.ShapeDtypeStruct((points, channels), F),
            jax.ShapeDtypeStruct((2, channels), F),
        ]
        + [jax.ShapeDtypeStruct((points, 2 * channels + n // 2 * share), BF)] * 2
        + [jax.ShapeDtypeStruct((tokens, 2 * share), BF)] * n,
        compiler_params=params(),
        cost_estimate=pl.CostEstimate(
            flops=8 * points * channels * channels,
            bytes_accessed=12 * channels * channels,
            transcendentals=points * channels,
        ),
        name="cross_backward",
    )(grad_norm, grad_four, three, two, gains, xq, *cq, *co, *ckv)


def attn_backward(place, grad_two, conv, noise, gains, qkv, token_grads, wqkv, wo, width):
    points, channels = grad_two.shape
    n = len(wo)
    share = wo[0].shape[0]
    tokens = token_grads[0].shape[0]

    def body(place_ref, g2_ref, conv_ref, noise_ref, gains_ref, qkv_ref, *rest):
        wqkv_r, wo_r, token_r = (rest[i * n : (i + 1) * n] for i in range(3))
        sums_ref = rest[3 * n]
        share_r = rest[3 * n + 1 : 4 * n + 1]
        own_ref, send_ref, gc_ref, wide, out_w, saved, wide_sem, out_sem, saved_sem = rest[4 * n + 1 :]
        wide_copies, take_wide = fetch(wqkv_r, wide, wide_sem)
        out_copies, take_out = fetch(wo_r, out_w, out_sem)
        saved_copies, take_saved = fetch([qkv_ref.at[j] for j in range(n)], saved, saved_sem)
        for trio in zip(out_copies, saved_copies, wide_copies):
            for c in trio:
                c.start()
        here = place_ref[0]
        grad_two = g2_ref[...]
        gb = grad_two.astype(BF)
        out = conv_ref[...].astype(F) + gains_ref[0:1] * noise_ref[...] + gains_ref[1:2]
        one = out * sigmoid(out)
        grad_norm = jnp.zeros((points, channels), F)
        for j in range(n):
            ga = dot_nt(gb, take_out(j)).astype(BF)
            take_saved(j)
            gq, gk, gv = [], [], []
            for h in range(share // HD):
                q, k, v = (
                    saved[j, :, i * share + h * HD : i * share + (h + 1) * HD] for i in range(3)
                )
                g = ga[:, h * HD : (h + 1) * HD]
                p = self_prob(q, k)
                gp = dot_nt(v, g)
                gs = p * (gp - jnp.sum(p * gp, axis=0, keepdims=True))
                square = jnp.sum(gs, axis=1, keepdims=True) * (-1.0 / math.sqrt(HD))
                raw = (gs * (2.0 / math.sqrt(HD))).astype(BF)
                gq.append(dot_tn(k, raw))
                gk.append((dot_nn(raw, q) + 2.0 * k.astype(F) * square).astype(BF))
                gv.append(dot_nn(p.astype(BF), g).astype(BF))
            side_ref, cut = side_slot(own_ref, send_ref, j, 0, 3 * share)
            gq = jnp.concatenate(gq).T.astype(BF)
            side_ref[:, cut] = jnp.concatenate([gq] + gk + gv, axis=1)
            grad_norm = grad_norm + dot_nt(side_ref[:, cut], take_wide(j))
        back, gain = rms_back(one, gains_ref[2:3], grad_norm)
        grad_conv = (grad_two + back) * silu_slope(out)
        gc_ref[...] = grad_conv.astype(BF)
        for j in range(n):
            start = pl.multiple_of(lax.bitwise_xor(here, j) * width, width)
            share_r[j][:points] = gc_ref[:, pl.ds(start, width)]
            for i in range(2):
                rows = slice(points + i * tokens, points + (i + 1) * tokens)
                share_r[j][rows] = token_r[j][:, i * width : (i + 1) * width]
        sums_ref[0:1] = gain
        sums_ref[1:2] = jnp.sum(grad_conv, axis=0, keepdims=True)
        sums_ref[2:3] = jnp.sum(grad_conv * noise_ref[...], axis=0, keepdims=True)

    return pl.pallas_call(
        body,
        out_shape=[
            jax.ShapeDtypeStruct((3, channels), F),
        ]
        + [jax.ShapeDtypeStruct((points + 2 * tokens, width), BF)] * n
        + [jax.ShapeDtypeStruct((points, n // 2 * 3 * share), BF)] * 2,
        in_specs=[smem()] + vmem(4) + anywhere(1 + 2 * n) + vmem(n),
        scratch_shapes=[
            pltpu.VMEM((points, channels), BF),
            pltpu.VMEM((n, channels, 3 * share), BF),
            pltpu.VMEM((n, share, channels), BF),
            pltpu.VMEM((n, points, 3 * share), BF),
            pltpu.SemaphoreType.DMA((n,)),
            pltpu.SemaphoreType.DMA((n,)),
            pltpu.SemaphoreType.DMA((n,)),
        ],
        compiler_params=params(),
        cost_estimate=pl.CostEstimate(
            flops=24 * points * channels * channels,
            bytes_accessed=24 * channels * channels,
            transcendentals=points * points * channels // HD,
        ),
        name="attn_backward",
    )(place, grad_two, conv, noise, gains, qkv, *wqkv, *wo, *token_grads)


def turn(turned, blocks, start, channels):
    points = blocks[0].shape[0]
    for i, block in enumerate(blocks):
        turned[:, i * points : (i + 1) * points] = block[:, start : start + channels].T


def pair_product(turned, blocks, cut):
    points = blocks[0].shape[0]
    total = None
    for i, block in enumerate(blocks):
        p = dot_nn(turned[:, i * points : (i + 1) * points], block[:, cut])
        total = p if total is None else total + p
    return total.astype(BF)


def cross_weights(attn_pair, cross_pair, grad_pair, count, share):
    points = attn_pair[0].shape[0]
    channels = attn_pair[0].shape[1] - count * share

    def body(*refs):
        attn, cross, grad = refs[:2], refs[2:4], refs[4:6]
        out, last = refs[6 : 6 + count], refs[6 + count : 6 + 2 * count]
        turned = refs[-1]
        turn(turned, cross, 0, channels)
        for i in range(count):
            cut = slice(2 * channels + i * share, 2 * channels + (i + 1) * share)
            out[i][:, :share] = pair_product(turned, grad, cut)
        turn(turned, grad, 0, channels)
        for i in range(count):
            cut = slice(channels + i * share, channels + (i + 1) * share)
            out[i][:, share:] = pair_product(turned, cross, cut)
        turn(turned, grad, channels, channels)
        for i in range(count):
            cut = slice(channels + i * share, channels + (i + 1) * share)
            last[i][...] = pair_product(turned, attn, cut)

    return pl.pallas_call(
        body,
        out_shape=[jax.ShapeDtypeStruct((channels, 2 * share), BF)] * count
        + [jax.ShapeDtypeStruct((channels, share), BF)] * count,
        scratch_shapes=[pltpu.VMEM((channels, 2 * points), BF)],
        compiler_params=params(),
        cost_estimate=pl.CostEstimate(
            flops=12 * count * points * channels * share,
            bytes_accessed=20 * points * channels,
            transcendentals=0,
        ),
        name="cross_weights",
    )(*attn_pair, *cross_pair, *grad_pair)


def attn_weights(attn_pair, grad_pair, count, share):
    points = attn_pair[0].shape[0]
    channels = attn_pair[0].shape[1] - count * share

    def body(*refs):
        attn, grad = refs[:2], refs[2:4]
        out, last, turned = refs[4 : 4 + count], refs[4 + count : 4 + 2 * count], refs[-1]
        turn(turned, attn, 0, channels)
        for i in range(count):
            at = 3 * i * share
            out[i][...] = pair_product(turned, grad, slice(at, at + 2 * share))
            last[i][...] = pair_product(turned, grad, slice(at + 2 * share, at + 3 * share))

    return pl.pallas_call(
        body,
        out_shape=[jax.ShapeDtypeStruct((channels, 2 * share), BF)] * count
        + [jax.ShapeDtypeStruct((channels, share), BF)] * count,
        scratch_shapes=[pltpu.VMEM((channels, 2 * points), BF)],
        compiler_params=params(),
        cost_estimate=pl.CostEstimate(
            flops=12 * count * points * channels * share,
            bytes_accessed=16 * points * channels,
            transcendentals=0,
        ),
        name="attn_weights",
    )(*attn_pair, *grad_pair)


def phase_order(points, side):
    row = lax.broadcasted_iota(jnp.int32, (points, points), 0)
    lane = lax.broadcasted_iota(jnp.int32, (points, points), 1)
    line, place = phase_place(row, side)
    return lane == 2 * side * line + place


def phase_place(row, side):
    phase, spot = row // (side * side), row % (side * side)
    return 2 * (spot // side) + phase // 2, 2 * (spot % side) + phase % 2


def phase_masks(side):
    shape = (4 * side * side, 2 * side)
    row = lax.broadcasted_iota(jnp.int32, shape, 0)
    lane = lax.broadcasted_iota(jnp.int32, shape, 1)
    line, place = phase_place(row, side)
    return jnp.where(lane == line, 1.0, 0.0), jnp.where(lane == place, 1.0, 0.0)


def cotangents(place, counts, features, image, noise, vectors, colors, code, rgb, side):
    points, channels = features.shape
    count = len(vectors)
    exact = dict(precision=lax.Precision.HIGHEST, preferred_element_type=F)
    along = (((1,), (0,)), ((), ()))

    def body(place_ref, live_ref, f_ref, im_ref, n_ref, col_ref, c_ref, rgb_ref, *rest):
        vec_r = rest[:count]
        four_ref, low_ref, gi_ref, no_ref, cs_ref, gains_ref = rest[count:]
        for i in range(count):
            gains_ref[i : i + 1] = vec_r[i][...].astype(F).reshape(1, channels)
        order = jnp.where(phase_order(points, side), 1.0, 0.0).astype(BF)
        by = live_ref[place_ref[0]].astype(F)
        lines, places = phase_masks(side)

        def column(v):
            rows = lax.dot_general(lines, v, along, **exact)
            return jnp.sum(rows * places, axis=1, keepdims=True)

        no_ref[...] = column(n_ref[0].astype(F))
        scale = dot_nn(c_ref[...], rgb_ref[...])[:1] + 1.0
        cs_ref[...] = scale
        four = dot_nn(order, f_ref[...]) * by
        col = col_ref[...].astype(F)
        for c in range(3):
            gi = column(im_ref[0, c]) * by
            gi_ref[:, c : c + 1] = gi
            four = four + gi * (col[c : c + 1] * scale)
        four_ref[...] = four
        low_ref[...] = four.astype(BF)

    return pl.pallas_call(
        body,
        in_specs=[smem(), smem()] + vmem(6 + count),
        out_shape=[
            jax.ShapeDtypeStruct((points, channels), F),
            jax.ShapeDtypeStruct((points, channels), BF),
            jax.ShapeDtypeStruct((points, 3), F),
            jax.ShapeDtypeStruct((points, 1), F),
            jax.ShapeDtypeStruct((1, channels), F),
            jax.ShapeDtypeStruct((count, channels), F),
        ],
        compiler_params=params(),
        name="cotangents",
    )(place, counts, features, image, noise, colors, code, rgb, *vectors)


def class_tokens(rows, pos, ck, cv):
    n = rows.shape[0]
    tokens, channels = pos.shape
    share = ck.shape[1]

    def body(r_ref, p_ref, ck_ref, cv_ref, ctx_ref, *out_r):
        pos = p_ref[...].astype(F)
        rows = r_ref[...].astype(F)
        for j in range(n):
            ctx_ref[j * tokens : (j + 1) * tokens] = (rows[j : j + 1] + pos).astype(BF)
        for w, at in ((ck_ref, 0), (cv_ref, share)):
            product = dot_nn(ctx_ref[...], w[...])
            for j in range(n):
                out_r[j][:, at : at + share] = product[j * tokens : (j + 1) * tokens].astype(BF)

    return pl.pallas_call(
        body,
        out_shape=[jax.ShapeDtypeStruct((n * tokens, channels), BF)]
        + [jax.ShapeDtypeStruct((tokens, 2 * share), BF)] * n,
        compiler_params=params(),
        name="class_tokens",
    )(rows, pos, ck, cv)


def band_prepare(place, received, codes, select, style, rows, pos, points_low):
    n_dp, _, band = received.shape
    samples, depth = codes.shape
    kernels = select.shape[0]
    low = n_dp * points_low // samples
    columns = samples * low
    step = 8

    tokens = pos.shape[0]

    def body(place_ref, x_ref, c_ref, sel_ref, sty_ref, r_ref, p_ref, *rest):
        at_ref, mix_ref, scale_ref, left_ref, ctx_ref, turned, held = rest
        pos_rows = p_ref[...].astype(F)
        class_rows = r_ref[...].astype(F)
        for s in range(samples):
            both = class_rows[s : s + 1] + pos_rows
            held[s * tokens : (s + 1) * tokens] = both.astype(BF).astype(F)
        ctx_ref[...] = held[...].T.astype(BF)
        logits = dot_nt(c_ref[...], sel_ref[...])
        e = jnp.exp(logits - jnp.max(logits, axis=1, keepdims=True))
        mixing = e / jnp.sum(e, axis=1, keepdims=True)
        mix_ref[...] = mixing
        scale_ref[...] = dot_nn(c_ref[...], sty_ref[...]) + 1.0
        scale_turned = scale_ref[...].T
        mix_turned = mixing.T
        for r in range(kernels // 2 + 1):
            ahead = jnp.concatenate([mix_turned[r:], mix_turned[:r]]) if r else mix_turned
            both = 2.0 * mix_turned * ahead
            left = (scale_turned * scale_turned)[:, None, :] * both[None]
            left_ref[r] = left.reshape(band * kernels, samples).astype(BF)
        for b in range(n_dp):
            turned[:, b * points_low : (b + 1) * points_low] = x_ref[b, :points_low].astype(F).T
        row = lax.broadcasted_iota(jnp.int32, (samples, columns), 0)
        lane = lax.broadcasted_iota(jnp.int32, (samples, columns), 1)
        repeat = jnp.where(lane // low == row, 1.0, 0.0).astype(BF)
        high = mixing.astype(BF)
        rest = (mixing - high.astype(F)).astype(BF)
        wide = dot_tn(high, repeat) + dot_tn(rest, repeat)
        for i in range(band // step):
            x = turned[i * step : (i + 1) * step]
            a = (x[:, None, :] * wide[None]).reshape(step * kernels, columns)
            at_ref[i * step * kernels : (i + 1) * step * kernels] = a.astype(BF)

    return pl.pallas_call(
        body,
        in_specs=[smem()] + vmem(6),
        out_shape=[
            jax.ShapeDtypeStruct((band * kernels, columns), BF),
            jax.ShapeDtypeStruct((samples, kernels), F),
            jax.ShapeDtypeStruct((samples, band), F),
            jax.ShapeDtypeStruct((kernels // 2 + 1, band * kernels, samples), BF),
            jax.ShapeDtypeStruct((band, samples * tokens), BF),
        ],
        scratch_shapes=[pltpu.VMEM((band, columns), F), pltpu.VMEM((samples * tokens, band), F)],
        compiler_params=params(),
        name="band_prepare",
    )(place, received, codes, select, style, rows, pos)


def side_outputs(place, three, branch, image_grad, color_scale, colors, bias, tokens, shares, ck, cv, gains, late, count_sums, count_all, side):
    points, channels = three.shape
    n, parts = len(shares), len(branch)
    share = ck.shape[1]
    low = side * side
    exact = dict(precision=lax.Precision.HIGHEST, preferred_element_type=F)

    def body(place_ref, bias_ref, three_ref, gi_ref, cs_ref, col_ref, ck_ref, cv_ref, gains_ref, late_ref, *rest):
        branch_r, share_r = rest[:parts], rest[parts : parts + n]
        feat_ref, color_ref, pack_ref, four_ref, keys, values = rest[parts + n :]
        here = place_ref[0]
        four = three_ref[...]
        for b in branch_r:
            four = four + b[...].astype(F)
        four_ref[...] = four
        order = jnp.where(phase_order(points, side), 1.0, 0.0)
        moved = lax.dot_general(order, four, (((0,), (0,)), ((), ())), **exact)
        feat_ref[...] = moved.reshape(1, 2 * side, 2 * side, channels)
        scale, col = cs_ref[...], col_ref[...].astype(F)
        tint = col * scale
        color = lax.dot_general(four_ref[...], tint, (((1,), (1,)), ((), ())), **exact)
        lines, places = phase_masks(side)
        for c in range(3):
            spread_out = color[:, c : c + 1] * places
            color_ref[0, c] = bias_ref[c] + lax.dot_general(
                lines, spread_out, (((0,), (0,)), ((), ())), **exact
            )
        gi = gi_ref[...]
        image = lax.dot_general(gi, four_ref[...], (((0,), (0,)), ((), ())), **exact)
        for j in range(n):
            cut = slice(j * tokens, (j + 1) * tokens)
            keys[cut] = share_r[j][points : points + tokens]
            values[cut] = share_r[j][points + tokens : points + 2 * tokens]
        grad = dot_nt(keys[...], ck_ref[...]) + dot_nt(values[...], cv_ref[...])
        pack_ref[...] = jnp.zeros_like(pack_ref)
        total = None
        for j in range(n):
            part = grad[j * tokens : (j + 1) * tokens]
            total = part if total is None else total + part
            row = count_sums + 2 * n + lax.bitwise_xor(here, j)
            pack_ref[pl.ds(row, 1)] = jnp.sum(part, axis=0, keepdims=True)
        pack_ref[:tokens] = total
        pack_ref[tokens : tokens + 2] = gains_ref[...]
        pack_ref[tokens + 2 : tokens + 5] = image * scale
        lane = lax.broadcasted_iota(jnp.int32, (1, channels), 1)
        row = jnp.zeros((1, channels), F)
        for c in range(3):
            row = jnp.where(lane == c, jnp.sum(gi[:, c : c + 1]), row)
        pack_ref[tokens + 5 : tokens + 6] = row
        pack_ref[tokens + 6 : tokens + 9] = late_ref[...]
        pack_ref[pl.ds(count_sums + 3 * n + here, 1)] = jnp.sum(image * col, axis=0, keepdims=True)

    return pl.pallas_call(
        body,
        in_specs=[smem(), smem()] + vmem(8 + parts + n),
        out_shape=[
            jax.ShapeDtypeStruct((1, 2 * side, 2 * side, channels), F),
            jax.ShapeDtypeStruct((1, 3, 2 * side, 2 * side), F),
            jax.ShapeDtypeStruct((count_all, channels), F),
        ],
        scratch_shapes=[
            pltpu.VMEM((points, channels), F),
            pltpu.VMEM((n * tokens, share), BF),
            pltpu.VMEM((n * tokens, share), BF),
        ],
        compiler_params=params(),
        name="side_outputs",
    )(place, bias, three, image_grad, color_scale, colors, ck, cv, gains, late, *branch, *shares)


def late_sums_kernel(place, scale, pack, low_parts, images, own_scale, energy, mixing_sum, mixing, count_sums, at_sum):
    low, channels = images.shape
    parts = len(low_parts)
    n, kernels = mixing.shape
    rows = mixing_sum.shape[0]

    def body(place_ref, scale_ref, pack_ref, im_ref, own_ref, en_ref, ms_ref, mix_ref, *rest):
        low_r, (out_ref, grad_ref) = rest[:parts], rest[parts:]
        here = place_ref[0]
        total = low_r[0][...].astype(F)
        for v in low_r[1:]:
            total = total + v[...].astype(F)
        grad_ref[...] = total * (own_ref[0:1] * scale_ref[0])
        out_ref[...] = pack_ref[...]
        line = jnp.sum(total * im_ref[...].astype(F), axis=0, keepdims=True)
        out_ref[pl.ds(count_sums + here, 1)] = line
        out_ref[count_sums + n : count_sums + 2 * n] = en_ref[...]
        out_ref[at_sum : at_sum + rows] = ms_ref[...]
        wide = split_dot(mix_ref[...], tile_mask(channels // kernels, kernels))
        lane = lax.broadcasted_iota(jnp.int32, (n, channels), 1) // kernels
        row = lax.bitwise_xor(lax.broadcasted_iota(jnp.int32, (n, channels), 0), here)
        line = jnp.sum(jnp.where(lane == row, wide, 0.0), axis=0, keepdims=True)
        out_ref[count_sums + 4 * n : count_sums + 4 * n + 1] = line

    return pl.pallas_call(
        body,
        in_specs=[smem(), smem()] + vmem(6 + parts),
        out_shape=[
            jax.ShapeDtypeStruct(pack.shape, F),
            jax.ShapeDtypeStruct((low, channels), F),
        ],
        compiler_params=params(),
        name="late_sums",
    )(place, scale, pack, images, own_scale, energy, mixing_sum, mixing, *low_parts)


def style_final(places, scale, mixing_grad, scale_grad, rgb_grad, tokens, codes, labels, select, style, rgb, classes, group):
    samples, channels = scale_grad.shape
    kernels, depth = select.shape

    def body(place_ref, s_ref, mg_ref, sg_ref, rg_ref, t_ref, c_ref, l_ref, sel_ref, sty_ref, rgb_ref, *outs):
        dsel_ref, dsty_ref, drgb_ref, dcodes_ref, table_ref, held = outs
        by = s_ref[0]
        codes = c_ref[...]
        logits = dot_nt(codes, sel_ref[...])
        e = jnp.exp(logits - jnp.max(logits, axis=1, keepdims=True))
        mixing = e / jnp.sum(e, axis=1, keepdims=True)
        mg = mg_ref[...] * by
        logit = (mixing * (mg - jnp.sum(mixing * mg, axis=1, keepdims=True))).astype(BF)
        sg = (sg_ref[...] * by).astype(BF)
        rg = (rg_ref[...] * by).astype(BF)
        dsel_ref[...] = dot_tn(logit, codes)
        dsty_ref[...] = dot_tn(codes, sg)
        drgb_ref[...] = dot_tn(codes, rg)
        held[...] = (
            dot_nn(logit, sel_ref[...]) + dot_nt(sg, sty_ref[...]) + dot_nt(rg, rgb_ref[...])
        )
        for j in range(group):
            dcodes_ref[j : j + 1] = held[pl.ds(place_ref[1] * group + j, 1)]
        ids = lax.broadcasted_iota(jnp.int32, (samples, classes), 1)
        one_hot = jnp.where(ids == l_ref[...], 1.0, 0.0).astype(BF)
        t = t_ref[...] * by
        high = t.astype(BF)
        rest = (t - high.astype(F)).astype(BF)
        table_ref[...] = dot_tn(one_hot, high) + dot_tn(one_hot, rest)

    return pl.pallas_call(
        body,
        in_specs=[smem(), smem()] + vmem(9),
        out_shape=[
            jax.ShapeDtypeStruct((kernels, depth), F),
            jax.ShapeDtypeStruct((depth, channels), F),
            jax.ShapeDtypeStruct((depth, channels), F),
            jax.ShapeDtypeStruct((group, depth), F),
            jax.ShapeDtypeStruct((classes, channels), F),
        ],
        scratch_shapes=[pltpu.VMEM((samples, depth), F)],
        compiler_params=params(),
        name="style_final",
    )(places, scale, mixing_grad, scale_grad, rgb_grad, tokens, codes, labels, select, style, rgb)


def local(
    images,
    styles,
    labels,
    noise_map,
    counts,
    cot_features,
    cot_image,
    kernel_bank,
    select_proj,
    style_proj,
    conv_bias,
    noise_gain,
    norm_attn,
    query_proj,
    key_proj,
    value_proj,
    out_proj,
    norm_cross,
    cross_query,
    cross_key,
    cross_value,
    cross_out,
    class_table,
    class_pos,
    norm_mlp,
    up_proj,
    down_proj,
    rgb_style,
    color_projection,
    color_bias,
):
    n, n_dp = lax.axis_size("rows"), lax.axis_size("dp")
    r, d = lax.axis_index("rows"), lax.axis_index("dp")
    side, channels = images.shape[1], images.shape[3]
    low = side * side
    points = 4 * low
    kernels, width = kernel_bank.shape[3], kernel_bank.shape[4]
    tokens = class_pos.shape[0]
    share = query_proj.shape[1]
    band = channels // n_dp
    samples = n * n_dp

    def by_phase(field):
        rest = field.shape[2:]
        split = field.reshape((side, 2, side, 2) + rest)
        order = (1, 3, 0, 2) + tuple(range(4, 4 + len(rest)))
        return split.transpose(order).reshape((points,) + rest)

    group_order = jnp.arange(n, dtype=jnp.int32) ^ r
    slots = jnp.arange(n_dp, dtype=jnp.int32)

    def tie_lists(*lists):
        flat = tie(*[v for part in lists for v in part])
        out = []
        for part in lists:
            out.append(list(flat[: len(part)]))
            flat = flat[len(part) :]
        return out

    def far_swaps(m):
        return [swap(m, "rows", j) for j in range(2, n, 2)]

    def near_swaps(blocks):
        return [swap(b, "rows", 1) for b in blocks]

    def whole(m, far_m, near_m):
        out = [None] * n
        out[::2] = [m] + far_m
        out[1::2] = near_m
        return out

    half = n // 2
    own_images = images[0].reshape(low, channels)
    codes = jnp.take(styles, jnp.arange(max(n, 8), dtype=jnp.int32) % n ^ r, axis=0)
    image_blocks = spread(own_images)
    depth, points_low = styles.shape[1], n * low
    label_rows = jnp.stack([labels // 256, labels % 256, counts]).astype(BF)
    payload = jnp.concatenate([styles.reshape(-1), label_rows.reshape(-1)])
    block = min(channels, 128)
    payload = jnp.pad(payload, (0, -payload.shape[0] % (16 * block))).reshape(-1, block)
    qkv_proj = jnp.concatenate([query_proj, key_proj, value_proj], axis=1)
    image_blocks, (codes, qkv_proj) = tie_lists(image_blocks, [codes, qkv_proj])
    qkv_far = far_swaps(qkv_proj)
    near = [near_swaps([m])[0] for m in (qkv_proj, out_proj, cross_query, cross_out)]
    select_turned = select_proj.T
    *conv_part, conv_raw, demod, xs, mixing, scale_in = conv_forward(
        codes, select_turned, style_proj, payload, image_blocks, kernel_bank, side
    )

    places = jnp.stack([r, d]).astype(jnp.int32)
    conv_part[0], places = tie(conv_part[0], places)
    pairs = bank_pairs(places, kernel_bank, band)

    later = [styles, labels, counts, cot_features, cot_image, noise_map, conv_bias, noise_gain]
    later += [norm_attn, norm_cross, norm_mlp, class_table, class_pos, cross_key, cross_value]
    later += [rgb_style, color_projection, color_bias, out_proj, cross_query, cross_out, xs]
    conv_part, (pairs,), later, qkv_far, near = tie_lists(
        conv_part, [pairs], later, qkv_far, near
    )
    styles, labels, counts, cot_features, cot_image, noise_map, conv_bias, noise_gain = later[:8]
    norm_attn, norm_cross, norm_mlp, class_table, class_pos, cross_key, cross_value = later[8:15]
    rgb_style, color_projection, color_bias, out_proj, cross_query, cross_out, xs = later[15:]

    parts = [conv_part[0]] + [swap(conv_part[j], "rows", j) for j in range(1, n)]
    qkv_near = near[:1] + near_swaps(qkv_far)
    place = r.astype(jnp.int32).reshape(1)
    colors = color_projection.T
    grad_four, grad_four_low, grad_image, noise, color_scale, gains = cotangents(
        place,
        counts,
        cot_features.reshape(points, channels),
        cot_image,
        noise_map,
        (noise_gain, conv_bias, norm_attn, norm_cross, norm_mlp),
        colors,
        codes,
        rgb_style,
        side,
    )
    parts, qkv_near, rest = tie_lists(
        parts,
        qkv_near,
        [grad_four, grad_four_low, grad_image, color_scale, noise, gains]
        + [xs, labels, class_table, out_proj],
    )
    grad_four, grad_four_low, grad_image, color_scale, noise, gains = rest[:6]
    xs, labels, class_table, out_proj = rest[6:]
    wo_far = far_swaps(out_proj)

    if band == block:
        bands = xs
    else:
        split = xs[:, :points_low].reshape(xs.shape[0], points_low, block // band, band)
        split = split.transpose(0, 2, 1, 3).reshape(n_dp, points_low, band)
        rest = jnp.broadcast_to(payload.reshape(1, -1, band), (n_dp, payload.size // band, band))
        bands = jnp.concatenate([split, rest], axis=1)
    received = lax.all_to_all(bands, "dp", 0, 0, tiled=True)
    wo_near = near[1:2] + near_swaps(wo_far)
    wqkv = whole(qkv_proj, qkv_far, qkv_near)
    wo = whole(out_proj, wo_far, wo_near)
    conv, two, qkv, attn_own, attn_sent = attn_forward(place, parts, noise, gains, wqkv, wo)
    cq_far = far_swaps(cross_query)
    (two, received, labels, class_table), cq_far = tie_lists(
        [two, received, labels, class_table], cq_far
    )

    co_far = far_swaps(cross_out)
    flat_context, *ckv = class_tokens(
        jnp.take(class_table, jnp.take(labels, group_order), axis=0), class_pos, cross_key, cross_value
    )
    ckv = [ckv[0]] + [swap(ckv[j], "rows", j) for j in range(1, n)]
    cq = whole(cross_query, cq_far, near[2:3] + near_swaps(cq_far))
    codes_back = received[:, points_low:].reshape(n_dp, -1)
    styles_all = codes_back[:, : n * depth].reshape(samples, depth)
    label_back = codes_back[:, n * depth : n * depth + 3 * n]
    label_back = label_back.reshape(n_dp, 3, n).astype(jnp.int32)
    inverse = (1.0 / jnp.sum(label_back[:, 2]).astype(F)).reshape(1)
    labels_all = (label_back[:, 0] * 256 + label_back[:, 1]).reshape(samples, 1)
    codes_all = jnp.take(styles_all.reshape(n_dp, n, depth), group_order, axis=1)
    band_proj = lax.dynamic_slice_in_dim(style_proj, d * band, band, axis=1)
    labels_ring = jnp.take(labels_all.reshape(n_dp, n), group_order, axis=1).reshape(samples)
    rows_band = jnp.take(class_table, labels_ring, axis=0)
    rows_band = lax.dynamic_slice_in_dim(rows_band, d * band, band, axis=1)
    pos_band = lax.dynamic_slice_in_dim(class_pos, d * band, band, axis=1)
    bands_ready = band_prepare(
        place, received, codes_all.reshape(samples, depth), select_turned, band_proj, rows_band, pos_band, points_low
    )
    (two,), co_far, cq, ckv, bands_ready, ready = tie_lists(
        [two], co_far, cq, ckv, bands_ready, [styles_all, labels_all, inverse]
    )
    at, mixing_all, scale_band, lefts, context_band = bands_ready
    styles_all, labels_all, inverse = ready
    co = whole(cross_out, co_far, near[3:4] + near_swaps(co_far))
    three, normed_mlp, xq, cross_own, cross_sent = cross_forward(two, gains, cq, co, ckv)
    grad_far = far_swaps(grad_four_low)
    grad_near = near_swaps([grad_four_low])
    attn_near = near_swaps([attn_sent])
    (three, normed_mlp), grad_far, grad_near, attn_near = tie_lists(
        [three, normed_mlp], grad_far, grad_near, attn_near
    )

    normed_near = near_swaps([normed_mlp])
    grad_near += near_swaps(grad_far)
    (normed_mlp,), normed_near, grad_near = tie_lists([normed_mlp], normed_near, grad_near)
    grad_pairs = list(zip([grad_four_low] + grad_far, grad_near))
    normed_far = far_swaps(normed_mlp)
    mlp_in = [normed_mlp] + normed_near
    act, inner, *backward = mlp_core(mlp_in, grad_pairs[0], up_proj, down_proj)
    cross_near = near_swaps([cross_sent])
    (act, inner), backward, normed_far, cross_near = tie_lists(
        [act, inner], backward, normed_far, cross_near
    )
    acts, inners = [act], [inner]
    for i, block in enumerate(normed_far):
        pair = [block] + near_swaps([block])
        act, inner, *back = mlp_core(pair, grad_pairs[i + 1], up_proj, down_proj)
        acts.append(act)
        inners.append(inner)
        mlp_in += pair
        backward += back
    backward, acts, inners = tie_lists(near_sums(backward), acts, inners)
    grad_norm = far_sum(backward)
    grad_group = [g for p in grad_pairs for g in p]
    *forward, d_mlp = mlp_rest(mlp_in, grad_group, inners, acts, down_proj)
    (grad_norm, d_mlp), forward = tie_lists([grad_norm, d_mlp], forward)
    g_mlp = lax.psum_scatter(d_mlp, "dp", scatter_dimension=0, tiled=True)

    back = cross_backward(grad_norm, grad_four, three, two, gains, xq, cq, co, ckv)
    grad_two, d_gains, grads_own, grads_sent = back[:4]
    dkv = list(back[4:])
    forward_near = near_swaps(forward[1::2])
    (grad_two, grads_sent), forward_near = tie_lists([grad_two, grads_sent], forward_near)

    def pair_sums(blocks, near_blocks):
        return [
            (a.astype(F) + b.astype(F)).astype(BF) for a, b in zip(blocks[::2], near_blocks)
        ]

    def far_parts(sums):
        return sums[:1] + [swap(v, "rows", 2 * j) for j, v in enumerate(sums) if j]

    def add_all(blocks):
        total = blocks[0].astype(F)
        for v in blocks[1:]:
            total = total + v.astype(F)
        return total

    branch = far_parts(pair_sums(forward, forward_near))
    grads_near = near_swaps([grads_sent])
    back = attn_backward(place, grad_two, conv, noise, gains, qkv, dkv, wqkv, wo, width)
    late_sums, shares, (qkv_own, qkv_sent) = back[0], list(back[1 : 1 + n]), back[1 + n :]
    (late_sums, qkv_sent), shares, grads_near, branch = tie_lists(
        [late_sums, qkv_sent], shares, grads_near, branch
    )

    shares = [shares[0]] + [swap(shares[j], "rows", j) for j in range(1, n)]
    sent_near = near_swaps([qkv_sent])
    back = cross_weights(
        [attn_own] + attn_near, [cross_own] + cross_near, [grads_own] + grads_near, half, share
    )
    d_cross, d_out = list(back[:half]), list(back[half:])
    shares, d_cross, d_out, sent_near = tie_lists(shares, d_cross, d_out, sent_near)
    grad_taps, gs, grad_energy = tap_sums(shares, demod, conv_raw, side, n_dp)

    rest, branch, d_cross, d_out, shares = tie_lists(
        [grad_taps, gs, grad_energy, late_sums, d_gains],
        branch,
        d_cross,
        d_out,
        shares,
    )
    grad_taps, gs, grad_energy, late_sums, d_gains = rest
    lines = n_dp // 2
    ring = [grad_taps]
    flipped = []

    def ring_step(*work):
        flipped.append(lax.ppermute(ring[-1], "dp", ring_perm(n_dp, 0, 1)))
        if len(ring) < lines:
            ring.append(lax.ppermute(ring[-1], "dp", ring_perm(n_dp, 1, 0)))
        (ring[-1], flipped[-1]), *work = tie_lists([ring[-1], flipped[-1]], *work)
        return work

    ge_all = lax.all_to_all(grad_energy, "dp", 0, 0, tiled=True).reshape(samples, width)
    d_cross = far_parts(d_cross)
    back = attn_weights([attn_own] + attn_near, [qkv_own] + sent_near, half, share)
    d_attn, d_value = list(back[:half]), list(back[half:])
    low_first, mix_first = conv_back(gs, xs, mixing, kernel_bank, n, 0, 2)
    (low_first, mix_first, ge_all, gs), d_cross, d_attn, d_value, d_out = ring_step(
        [low_first, mix_first, ge_all, gs], d_cross, d_attn, d_value, d_out
    )
    d_out = far_parts(d_out)
    low_last, mix_last = conv_back(gs, xs, mixing, kernel_bank, n, 1, 2)
    (low_last, mix_last), d_out, d_cross, d_attn, shares = ring_step(
        [low_last, mix_last], d_out, d_cross, d_attn, shares
    )
    low_part = jnp.concatenate([low_first, low_last], axis=2)
    mixing_conv = mix_first + mix_last

    cross_grads = jnp.concatenate([add_all(d_cross), add_all(d_out)], axis=1).astype(BF)
    d_attn = far_parts(d_attn)
    low_near = near_sums([low_part[j] for j in range(n)])
    done = energy_sums(place, mixing_all, scale_band, ge_all, pairs, n)
    count_sums = -(-(tokens + 9 + -(-samples * kernels // channels)) // 8) * 8
    count_all = -(-(count_sums + 4 * n + 1) // 8) * 8
    features, color_image, pack = side_outputs(
        place,
        three,
        branch,
        grad_image,
        color_scale,
        colors,
        color_bias.astype(F),
        tokens,
        shares,
        cross_key,
        cross_value,
        d_gains,
        late_sums,
        count_sums,
        count_all,
        side,
    )
    done, d_attn, low_near, (g_mlp, pack, lefts, cross_grads), d_value = ring_step(
        list(done), d_attn, low_near, [g_mlp, pack, lefts, cross_grads], d_value
    )
    cross_grads = scatter(cross_grads)
    scale_energy, mixing_energy = done

    def as_rows(v):
        v = v.reshape(1, -1)
        v = jnp.pad(v, ((0, 0), (0, -v.shape[1] % channels)))
        return v.reshape(-1, channels)

    low_parts = far_parts(low_near)
    pack, grad_images = late_sums_kernel(
        place,
        inverse,
        pack,
        low_parts,
        own_images,
        scale_in,
        scale_energy.reshape(n, channels),
        as_rows(mixing_energy),
        mixing_conv,
        count_sums,
        tokens + 9,
    )
    pack = add_over(pack, "rows")
    d_value = far_parts(d_value)
    energy = bank_energy(places, lefts, ge_all, kernel_bank)
    (grad_images, pack, energy), d_value, d_attn = ring_step(
        [grad_images, pack, energy], d_value, d_attn
    )
    while len(flipped) < lines:
        ((pack,),) = ring_step([pack])

    everyone_rows = jnp.broadcast_to(pack.astype(BF)[None], (n_dp,) + pack.shape)
    everyone_rows = lax.all_to_all(everyone_rows, "dp", 0, 0, tiled=True)
    attn_side = jnp.concatenate([add_all(d_attn), add_all(d_value)], axis=1).astype(BF)
    attn_side = scatter_side(attn_side)
    blocks = [None] * n_dp
    for t in range(lines):
        for e, v in enumerate((ring[t], flipped[t])):
            blocks[2 * t + e] = v
    grad_bank, token_grads = bank_main(places, inverse, at, context_band, blocks, energy, side)
    (grad_bank, everyone_rows), attn_side = tie_lists([grad_bank, everyone_rows], attn_side)
    attn_parts = scatter_lines(*attn_side)
    sums = jnp.sum(everyone_rows[:, :count_sums].astype(F), axis=0)
    gathered = everyone_rows[:, count_sums:].astype(F)
    scale_grad, bands_grad, token_all, rgb_all = (
        gathered[:, i * n : (i + 1) * n].reshape(samples, channels) for i in range(4)
    )
    bands_grad = bands_grad.reshape(n_dp, samples, band).transpose(1, 0, 2)
    scale_grad = scale_grad + bands_grad.reshape(samples, channels)
    mixing_grad = gathered[:, 4 * n, : n * kernels].reshape(samples, kernels)
    mixing_sum = sums[tokens + 9 :].reshape(-1)[: samples * kernels]
    mixing_grad = mixing_grad + mixing_sum.reshape(samples, kernels)
    sums = sums[: tokens + 9] * inverse
    grad_images = grad_images.reshape(1, side, side, channels)

    d_select, d_style, d_rgb, styles_grad, d_table = style_final(
        places,
        inverse,
        mixing_grad,
        scale_grad,
        rgb_all,
        token_all,
        styles_all,
        labels_all,
        select_turned,
        style_proj,
        rgb_style,
        class_table.shape[0],
        n,
    )

    cross_grads, attn_grads = tie(
        *(add_all(v) * inverse for v in ([cross_grads], attn_parts))
    )
    g_mlp = g_mlp.astype(F) * inverse
    wide = up_proj.shape[1]

    def column(grads, i):
        return grads[:, i * share : (i + 1) * share]

    return (
        features,
        color_image,
        grad_images,
        styles_grad,
        grad_bank,
        d_select.T,
        d_style,
        sums[tokens + 7],
        sums[tokens + 8],
        sums[tokens + 6],
        column(attn_grads, 0),
        column(attn_grads, 1),
        column(attn_grads, 2),
        column(cross_grads, 2).T,
        sums[tokens + 1],
        column(cross_grads, 0),
        column(token_grads, 0),
        column(token_grads, 1),
        column(cross_grads, 1).T,
        d_table,
        sums[:tokens],
        sums[tokens],
        g_mlp[:, :wide],
        g_mlp[:, wide:].T,
        d_rgb,
        sums[tokens + 2 : tokens + 5].T,
        sums[tokens + 5, :3],
    )


def solution(mesh):
    whole = P()
    columns = P(None, "rows")
    lines = P("rows", None)
    both = P(("dp", "rows"), None, None, None)
    placed = (
        both,
        P("dp", None),
        P("dp"),
        P(("dp", "rows"), None, None),
        P("dp"),
        both,
        both,
        P(None, None, None, None, "rows"),
        whole,
        whole,
        whole,
        whole,
        whole,
        columns,
        columns,
        columns,
        lines,
        whole,
        columns,
        columns,
        columns,
        lines,
        whole,
        whole,
        whole,
        columns,
        lines,
        whole,
        whole,
        whole,
    )
    given = (
        both,
        both,
        both,
        P("dp", None),
        P(None, None, "dp", None, "rows"),
        whole,
        whole,
        whole,
        whole,
        whole,
        P("dp", "rows"),
        P("dp", "rows"),
        P("dp", "rows"),
        P("rows", "dp"),
        whole,
        P("dp", "rows"),
        P("dp", "rows"),
        P("dp", "rows"),
        P("rows", "dp"),
        whole,
        whole,
        whole,
        P("dp", "rows"),
        P("rows", "dp"),
        whole,
        whole,
        whole,
    )
    return jax.shard_map(local, mesh=mesh, in_specs=placed, out_specs=given, check_vma=False)
```
